32 devices in a mesh: ctx: 8 (over z, x), fsdp: 4 (over y, core).
Axes of the slice: x: 2, y: 2, z: 4, core: 2. Of those that a mesh axis runs over, the one named last changes fastest.
Arguments:
- tokens: bfloat16 [4, 4096, 1024], P('fsdp', 'ctx'), may hold values from -6 to 6
- teacher: bfloat16 [4, 4096, 1024], P('fsdp', 'ctx'), may hold values from -6 to 6
- lengths: int32 [4, 2], P('fsdp'), may hold values from 1024 to 2048, as said below
- pair_owner: int32 [8], replicated, may hold values from 0 to 7, each once
- norm_gain: bfloat16 [1024], P('fsdp'), may hold values from 0.5 to 1.5
- in_proj: bfloat16 [1024, 4096], P('fsdp'), may hold values from -0.1875 to 0.1875
- conv_weight: bfloat16 [4, 2048], P(None, 'fsdp'), may hold values from -3 to 3
- conv_bias: bfloat16 [2048], P('fsdp'), may hold values from -1.5 to 1.5
- x_proj: bfloat16 [2048, 96], P('fsdp'), may hold values from -0.125 to 0.125
- dt_proj: bfloat16 [64, 2048], P(None, 'fsdp'), may hold values from -0.75 to 0.75
- dt_bias: bfloat16 [2048], P('fsdp'), may hold values from -12 to -3.5
- a_log: bfloat16 [16, 2048], P(None, 'fsdp'), may hold values from 0 to 2.765625
- skip_scale: bfloat16 [2048], P('fsdp'), may hold values from 0.5 to 1.5
- out_proj: bfloat16 [2048, 1024], P('fsdp'), may hold values from -0.125 to 0.125
Outputs:
- output: bfloat16 [4, 4096, 1024], P('fsdp', 'ctx')
- loss: float32 [], replicated
- grad_tokens: float32 [4, 4096, 1024], P('fsdp', 'ctx')
- grad_norm_gain: float32 [1024], P('fsdp')
- grad_in_proj: float32 [1024, 4096], P('fsdp')
- grad_conv_weight: float32 [4, 2048], P(None, 'fsdp')
- grad_conv_bias: float32 [2048], P('fsdp')
- grad_x_proj: float32 [2048, 96], P('fsdp')
- grad_dt_proj: float32 [64, 2048], P(None, 'fsdp')
- grad_dt_bias: float32 [2048], P('fsdp')
- grad_a_log: float32 [16, 2048], P(None, 'fsdp')
- grad_skip_scale: float32 [2048], P('fsdp')
- grad_out_proj: float32 [2048, 1024], P('fsdp')
The draws below stay inside these ranges and needn't reach their ends.
Inputs may be any that keep to these rules, and one draw needn't show every extreme that they name: `lengths`: each sequence's valid slots are its first ones, at least half of its 2048 slots; in every group one of the two sequences fills all 2048. `pair_owner`: each index of ctx holds exactly one pair.
All inputs are finite; a program needn't handle non-finite values.
Results may differ from the reference program's by a relative error of at most 0.0095.
Values may be sent and summed in bfloat16 or wider, within the bound.
No kernel may reach another device: no remote copies, remote signals or barrier semaphores. Data moves between devices by JAX's collectives and lax.ppermute only.
A program may use at most 256 MiB of HBM per device.

```python
import jax
import jax.numpy as jnp
from jax import lax

D = 1024
DI = 2048
DSTATE = 16
DTRANK = 64
DCONV = 4
PIECE = 256
BLOCK = 32
GROUPS = 4
SEQ_CAP = 2048
SLOTS = 4096
TOTAL = 16384
N_CTX = 8


def draw_tokens(key, part):
    key_mean = jax.random.fold_in(key, 21)
    key_noise = jax.random.fold_in(key, 22)
    offset = jax.random.normal(key_mean, (D,)) * 0.8
    noise = jax.random.normal(key_noise, (GROUPS, SLOTS, D))
    return jnp.clip(offset[None, None, :] + noise, -6.0, 6.0).astype(jnp.bfloat16)


def draw_lengths(key, part):
    key_len = jax.random.fold_in(key, 11)
    key_pick = jax.random.fold_in(key, 12)
    drawn = jax.random.randint(key_len, (GROUPS, 2), SEQ_CAP // 2, SEQ_CAP + 1)
    chosen = jax.random.randint(key_pick, (GROUPS, 1), 0, 2)
    return jnp.where(jnp.arange(2)[None, :] == chosen, SEQ_CAP, drawn).astype(jnp.int32)


def level_of(key, shape, shards, low, largest):
    def one(dim, blocks):
        draws = jax.random.uniform(jax.random.fold_in(jax.random.fold_in(key, 6), dim), (blocks,), jnp.float32, low / len(shards), largest / len(shards))
        return jnp.repeat(jnp.exp(draws), shape[dim] // blocks).reshape((-1,) + (1,) * (len(shape) - dim - 1))

    level = one(*shards[0])
    for cut in shards[1:]:
        level = level * one(*cut)
    return level


def normal_values(stream_key, extent, deviation, bound, pieces=(), kind=jnp.bfloat16):
    result = deviation * jax.random.normal(stream_key, extent, jnp.float32)
    if pieces:
        result = result * level_of(stream_key, extent, pieces, -0.22, 0.18)
    return jnp.clip(result, -bound, bound).astype(kind)


def setup_inputs(seed: int = 0) -> dict:
    streams_of = jax.random.split(jax.random.key(seed), 15)
    tokens = draw_tokens(jax.random.fold_in(streams_of[14], 71), 0)
    teacher = normal_values(streams_of[1], (GROUPS, SLOTS, D), 1.0, 6.0, ((0, 4), (1, 8)))
    lengths = draw_lengths(jax.random.fold_in(streams_of[14], 71), 0)
    pair_owner = jax.random.permutation(streams_of[3], N_CTX).astype(jnp.int32)
    norm_gain = jnp.clip(1.0 + 0.1 * jax.random.normal(streams_of[4], (D,), jnp.float32), 0.5, 1.5).astype(jnp.bfloat16)
    in_proj = normal_values(streams_of[5], (D, 2 * DI), D ** -0.5, 0.1875, ((0, 4),))
    conv_weight = normal_values(streams_of[6], (DCONV, DI), DCONV ** -0.5, 3.0, ((1, 4),))
    conv_bias = normal_values(streams_of[7], (DI,), 0.3, 1.5, ((0, 4),))
    x_proj = normal_values(streams_of[8], (DI, DTRANK + 2 * DSTATE), DI ** -0.5, 0.125, ((0, 4),))
    dt_proj = normal_values(streams_of[9], (DTRANK, DI), DTRANK ** -0.5, 0.75, ((1, 4),))
    dt_bias = jnp.clip(-12.0 + 8.5 * jax.random.uniform(streams_of[10], (DI,), jnp.float32) ** level_of(streams_of[10], (DI,), ((0, 4),), -0.2, 0.2), -12.0, -3.5).astype(jnp.bfloat16)
    a_log = jnp.clip(2.765625 * jax.random.uniform(streams_of[11], (DSTATE, DI), jnp.float32) ** level_of(streams_of[11], (DSTATE, DI), ((1, 4),), -0.2, 0.2), 0.0, 2.765625).astype(jnp.bfloat16)
    skip_scale = jnp.clip(0.5 + 1.0 * jax.random.uniform(streams_of[12], (DI,), jnp.float32) ** level_of(streams_of[12], (DI,), ((0, 4),), -0.2, 0.2), 0.5, 1.5).astype(jnp.bfloat16)
    out_proj = normal_values(streams_of[13], (DI, D), DI ** -0.5, 0.125, ((0, 4),))
    return {"tokens": tokens, "teacher": teacher, "lengths": lengths, "pair_owner": pair_owner, "norm_gain": norm_gain, "in_proj": in_proj, "conv_weight": conv_weight, "conv_bias": conv_bias, "x_proj": x_proj, "dt_proj": dt_proj, "dt_bias": dt_bias, "a_log": a_log, "skip_scale": skip_scale, "out_proj": out_proj}


@jax.custom_vjp
def low(v):
    return lax.optimization_barrier(v.astype(jnp.bfloat16)).astype(jnp.float32)

@jax.custom_vjp
def low_back(v):
    return v

def low_keep(v):
    return (low(v), None)

def low_pass(kept, grad):
    return (grad,)

def back_keep(v):
    return (v, None)

def back_low(kept, grad):
    return (low(grad),)
low.defvjp(low_keep, low_pass)
low_back.defvjp(back_keep, back_low)
EPSILON = 1e-05
HIGHEST = lax.Precision.HIGHEST

def matmul(left, right):
    return jnp.dot(left, right, precision=HIGHEST, preferred_element_type=jnp.float32)

def slot_rows(pair_owner):
    ctx_count = pair_owner.shape[0]
    piece_ids = jnp.arange(2 * ctx_count, dtype=jnp.int32)
    first_half = piece_ids < ctx_count
    holder = jnp.where(first_half, pair_owner[jnp.minimum(piece_ids, ctx_count - 1)], pair_owner[jnp.clip(2 * ctx_count - 1 - piece_ids, 0, ctx_count - 1)]).astype(jnp.int32)
    row_base = holder * (2 * PIECE) + jnp.where(first_half, 0, PIECE).astype(jnp.int32)
    return (row_base[:, None] + jnp.arange(PIECE, dtype=jnp.int32)[None, :]).reshape(-1).astype(jnp.int32)

def scan_block(neg_rate, state_in, block_in):
    step_blk, xs_blk, input_blk, output_blk = block_in

    def advance(state_now, item_in):
        step_now, xs_now, input_now, output_now = item_in
        decays = jnp.exp(step_now[:, None, :] * neg_rate[None])
        state_now = decays * state_now + (step_now * xs_now)[:, None, :] * input_now[:, :, None]
        return (state_now, lax.optimization_barrier(jnp.sum(output_now[:, :, None] * state_now, axis=1)))
    return lax.scan(advance, state_in, (step_blk, xs_blk, input_blk, output_blk))

def block_step(carry_in, block_in):
    state_in, rate_in = carry_in
    state_out, read_rows = scan_block(rate_in, state_in, block_in)
    return ((state_out, rate_in), read_rows)

def arrange(values):
    return values.reshape(2, SEQ_CAP // BLOCK, BLOCK, values.shape[1]).transpose(1, 2, 0, 3)

def group_forward(rows, length_pair, weights):
    norm_gain, in_proj, conv_weight, conv_bias, x_proj, dt_proj, dt_bias, a_log, skip_scale, out_proj = weights
    inv_rms = lax.rsqrt(lax.optimization_barrier(jnp.mean(rows * rows, axis=1, keepdims=True)) + EPSILON)
    normed = low(rows * inv_rms * norm_gain)
    mixed = low_back(matmul(normed, in_proj))
    x_in = low(mixed[:, :DI]).reshape(2, SEQ_CAP, DI)
    gate_pre = mixed[:, DI:]
    padded = jnp.pad(x_in, ((0, 0), (DCONV - 1, 0), (0, 0)))
    conv_out = conv_bias + padded[:, 0:SEQ_CAP] * conv_weight[0]
    for offset in range(1, DCONV):
        conv_out = conv_out + padded[:, offset:offset + SEQ_CAP] * conv_weight[offset]
    xs_vals = low(jax.nn.silu(conv_out)).reshape(SLOTS, DI)
    proj = low_back(matmul(xs_vals, x_proj))
    delta = low(proj[:, :DTRANK])
    input_map = proj[:, DTRANK:DTRANK + DSTATE]
    output_map = proj[:, DTRANK + DSTATE:]
    pre_step = low_back(matmul(delta, dt_proj)) + dt_bias
    position = jnp.arange(SEQ_CAP, dtype=jnp.int32)
    valid = (position[None, :] < length_pair[:, None]).astype(jnp.float32).reshape(SLOTS, 1)
    step_size = jax.nn.softplus(pre_step) * valid
    neg_rate = -jnp.exp(a_log)
    start_state = jnp.zeros((2, DSTATE, DI), jnp.float32)
    _, read_blocks = lax.scan(jax.checkpoint(block_step), (start_state, neg_rate), (arrange(step_size), arrange(xs_vals), arrange(input_map), arrange(output_map)))
    ssm = read_blocks.transpose(2, 0, 1, 3).reshape(SLOTS, DI) + skip_scale * xs_vals
    branch = low(ssm * jax.nn.silu(gate_pre))
    block_out = rows + low_back(matmul(branch, out_proj))
    return (block_out, valid)

def reference(tokens, teacher, lengths, pair_owner, norm_gain, in_proj, conv_weight, conv_bias, x_proj, dt_proj, dt_bias, a_log, skip_scale, out_proj):
    order = slot_rows(pair_owner)
    inverse = jnp.zeros((SLOTS,), jnp.int32).at[order].set(jnp.arange(SLOTS, dtype=jnp.int32))
    params = (norm_gain.astype(jnp.float32), in_proj.astype(jnp.float32), conv_weight.astype(jnp.float32), conv_bias.astype(jnp.float32), x_proj.astype(jnp.float32), dt_proj.astype(jnp.float32), dt_bias.astype(jnp.float32), a_log.astype(jnp.float32), skip_scale.astype(jnp.float32), out_proj.astype(jnp.float32))
    targets = teacher.astype(jnp.float32)

    def forward(rows_all, *weights):

        def one_group(group_in):
            rows, target_rows, length_pair = group_in
            block_out, valid = group_forward(rows[order], length_pair, weights)
            error_rows = block_out - target_rows[order]
            return (block_out[inverse], jnp.sum(valid * error_rows * error_rows), jnp.sum(valid))
        outs_all, squares, counts = lax.map(jax.checkpoint(one_group), (rows_all, targets, lengths))
        loss = jnp.sum(squares) / (jnp.sum(counts) * D)
        return (loss * (TOTAL * D), (outs_all, loss))
    scaled_loss, pullback, aux = jax.vjp(forward, tokens.astype(jnp.float32), *params, has_aux=True)
    outs_all, loss = aux
    grads = pullback(jnp.ones((), jnp.float32))
    return (outs_all.astype(jnp.bfloat16), loss, grads[0], grads[1], grads[2], grads[3], grads[4], grads[5], grads[6], grads[7], grads[8], grads[9], grads[10])
```

```python
import functools

import jax
import jax.numpy as jnp
from jax import lax
from jax.experimental import pallas as pl
from jax.experimental.pallas import tpu as pltpu
from jax.sharding import PartitionSpec as P

EPSILON = 1e-05
LOG2E = 1.4426950408889634
F32 = jnp.float32
BF16 = jnp.bfloat16
LANES = 128
HALO = 16
HEAD = 16
VMEM_LIMIT = 60 * 1024 * 1024


def swap(values, axis, bit):
    size = lax.axis_size(axis)
    return lax.ppermute(values, axis, [(i, i ^ bit) for i in range(size)])


def after(values, earlier):
    return lax.optimization_barrier((values, earlier))[0]


def bits_of(size):
    return [1 << k for k in range(size.bit_length() - 1)]


def gather_fsdp(values):
    blocks = {0: values}
    for bit in reversed(bits_of(lax.axis_size("fsdp"))):
        for r in sorted(blocks):
            blocks[r | bit] = swap(blocks[r], "fsdp", bit)
    return [blocks[r] for r in range(len(blocks))]


def gather_ctx(values):
    size = lax.axis_size("ctx")
    blocks = {0: values}
    for j in range(2, size, 2):
        blocks[j] = swap(values, "ctx", j)
    for j in range(0, size, 2):
        blocks[j | 1] = swap(blocks[j], "ctx", 1)
    return [blocks[j] for j in range(size)]


def total(values, axes):
    for axis in axes:
        for bit in bits_of(lax.axis_size(axis)):
            values = values + swap(values, axis, bit)
    return values


def joined(kept, received):
    return (kept.astype(F32) + received.astype(F32)).astype(BF16)


def reduce_shard(keep, send, ctx_first):
    fsdp_steps = [("fsdp", bit) for bit in bits_of(lax.axis_size("fsdp"))[1:]]
    ctx_steps = [("ctx", bit) for bit in bits_of(lax.axis_size("ctx"))]
    steps = ctx_steps + fsdp_steps if ctx_first else fsdp_steps + ctx_steps
    values = joined(keep, swap(send, "fsdp", 1))
    me = lax.axis_index("ctx")
    for axis, bit in steps:
        if axis == "fsdp":
            values = joined(values[0::2], swap(values[1::2], axis, bit))
        else:
            half = values.shape[1] // 2
            up = (me & bit) != 0
            low, high = values[:, :half], values[:, half:]
            values = joined(
                jnp.where(up, high, low), swap(jnp.where(up, low, high), axis, bit)
            )
    for axis, bit in reversed(ctx_steps):
        other = swap(values, axis, bit)
        up = (me & bit) != 0
        values = jnp.concatenate(
            [jnp.where(up, other, values), jnp.where(up, values, other)], axis=1
        )
    return values[0]


def dot(left, right):
    return jnp.dot(left, right, preferred_element_type=F32)


def rows_dot(left, right):
    return lax.dot_general(left, right, (((0,), (0,)), ((), ())), preferred_element_type=F32)


def back_dot(left, right):
    return lax.dot_general(left, right, (((1,), (1,)), ((), ())), preferred_element_type=F32)


def sigmoid(values):
    return 1.0 / (1.0 + jnp.exp(-values))


def softplus(values):
    small = jnp.exp(-jnp.abs(values))
    grown = 1.0 + small
    part = jnp.where(grown == 1.0, small, jnp.log(grown) * (small / jnp.maximum(grown - 1.0, 1e-30)))
    return jnp.maximum(values, 0.0) + part


def tile_cols(j):
    return slice(j * LANES, (j + 1) * LANES)


def input_kernel(scal, normed_ref, *refs, count, piece):
    weights, (s_ref, x_ref, conv_ref, xs_ref, proj_ref) = refs[:count], refs[count:]
    depth = weights[0].shape[0]
    width = weights[0].shape[1]
    mixed = dot(normed_ref[:, 0:depth], weights[0][...])
    for r in range(1, count):
        mixed = mixed + dot(normed_ref[:, r * depth : (r + 1) * depth], weights[r][...])
    x_low = mixed.astype(BF16).reshape(2, HALO + piece, width)
    x_ref[...] = x_low
    x = x_low.astype(F32)
    head = s_ref[0:HEAD, :].astype(F32)
    conv = head[4:5] + x[:, HALO - 3 : HALO - 3 + piece] * head[0:1]
    for k in range(1, 4):
        conv = conv + x[:, HALO - 3 + k : HALO - 3 + k + piece] * head[k : k + 1]
    conv_ref[...] = conv
    xs = (conv * sigmoid(conv)).astype(BF16)
    xs_ref[...] = xs
    part = back_dot(xs.reshape(2 * piece, width), s_ref[96:192, :])

    @pl.when(pl.program_id(0) == 0)
    def first():
        proj_ref[...] = part

    @pl.when(pl.program_id(0) > 0)
    def later():
        proj_ref[...] += part


def gate_kernel(scal, normed_ref, *refs, count, piece):
    weights, (gate_ref,) = refs[:count], refs[count:]
    depth = weights[0].shape[0]
    width = weights[0].shape[1]
    own = jnp.concatenate(
        [normed_ref[HALO : HALO + piece], normed_ref[2 * HALO + piece : 2 * HALO + 2 * piece]], axis=0
    )
    gate = dot(own[:, 0:depth], weights[0][...])
    for r in range(1, count):
        gate = gate + dot(own[:, r * depth : (r + 1) * depth], weights[r][...])
    gate_ref[...] = gate.reshape(2, piece, width)


def end_kernel(
    scal, proj_ref, s_ref, xs_ref, b_ref, step_ref, end_ref, log_ref, drive_ref, *, tiles, groups, rank
):
    piece = groups * 8
    width = tiles * LANES
    states = b_ref.shape[2]
    head = s_ref[0:HEAD, :].astype(F32)
    delta = proj_ref[:, 0:rank].astype(BF16)
    pre = dot(delta, s_ref[HEAD : HEAD + rank, :]) + head[5:6]
    row = lax.broadcasted_iota(jnp.int32, (piece, width), 0)
    for h in range(2):
        step = softplus(pre[h * piece : (h + 1) * piece])
        step = jnp.where(row < scal[1 + h], step, 0.0)
        log_ref[h : h + 1, :] = jnp.sum(step, axis=0, keepdims=True)
        step_ref[h] = step.reshape(groups, 8, width)
        drive_ref[h] = (step * xs_ref[h].astype(F32)).reshape(groups, 8, width)
    rate2 = -jnp.exp(s_ref[80 : 80 + states, :].astype(F32)) * LOG2E
    rates = [rate2[:, tile_cols(j)] for j in range(tiles)]

    def body(t, held):
        held = list(held)
        for s in range(8):
            for h in range(2):
                b = b_ref[h, t * 8 + s]
                for j in range(tiles):
                    step = step_ref[h, t, s : s + 1, tile_cols(j)]
                    drive = drive_ref[h, t, s : s + 1, tile_cols(j)]
                    k = h * tiles + j
                    held[k] = jnp.exp2(step * rates[j]) * held[k] + drive * b
        return tuple(held)

    zero = jnp.zeros((states, LANES), F32)
    held = lax.fori_loop(0, groups, body, (zero,) * (2 * tiles))
    for h in range(2):
        for j in range(tiles):
            end_ref[h * states : (h + 1) * states, tile_cols(j)] = held[h * tiles + j].astype(BF16)


def carried(ends, log_ref, rate2, h, ctx, states, cols):
    value = jnp.zeros((states, LANES), F32)
    for j in range(1, ctx):
        decay = jnp.exp2(rate2 * log_ref[h * ctx + j : h * ctx + j + 1, cols])
        value = value + decay * ends[j - 1][h * states : (h + 1) * states, cols].astype(F32)
    return value


def forward_kernel(scal, *refs, tiles, groups, ctx, features):
    ends = refs[: ctx - 1]
    (
        log_ref, scale_ref, s_ref, step_ref, xs_ref, gate_ref, b_ref, c_ref, weight_ref, tokens_ref, teacher_ref,
        ssm_ref, branch_ref, hidden_ref, start_ref, out_ref, gout_ref, dout_ref, square_ref,
        drive_ref, read_ref, acc_ref,
    ) = refs[ctx - 1 :]
    piece = groups * 8
    width = tiles * LANES
    states = b_ref.shape[2]
    i = pl.program_id(0)
    head = s_ref[0:HEAD, :].astype(F32)
    for h in range(2):
        drive_ref[h] = step_ref[h] * xs_ref[h].astype(F32).reshape(groups, 8, width)
    rate2 = -jnp.exp(s_ref[80 : 80 + states, :].astype(F32)) * LOG2E
    rates = [rate2[:, tile_cols(j)] for j in range(tiles)]
    held = []
    for h in range(2):
        for j in range(tiles):
            held.append(carried(ends, log_ref, rates[j], h, ctx, states, tile_cols(j)))
            start_ref[h, :, tile_cols(j)] = held[-1]

    def body(t, held):
        held = list(held)
        for s in range(8):
            p = t * 8 + s
            for h in range(2):
                b = b_ref[h, p]
                c = c_ref[h, p]
                for j in range(tiles):
                    step = step_ref[h, t, s : s + 1, tile_cols(j)]
                    drive = drive_ref[h, t, s : s + 1, tile_cols(j)]
                    k = h * tiles + j
                    now = jnp.exp2(step * rates[j]) * held[k] + drive * b
                    held[k] = now
                    hidden_ref[j, h, p] = now.astype(BF16)
                    read_ref[h, t, s : s + 1, tile_cols(j)] = jnp.sum(now * c, axis=0, keepdims=True)
        return tuple(held)

    lax.fori_loop(0, groups, body, tuple(held))
    branches = []
    for h in range(2):
        ssm = read_ref[h].reshape(piece, width) + head[6:7] * xs_ref[h].astype(F32)
        ssm_ref[h] = ssm
        gate = gate_ref[h]
        branches.append((ssm * (gate * sigmoid(gate))).astype(BF16))
        branch_ref[h] = branches[-1]
    part = dot(jnp.concatenate(branches, axis=0), weight_ref[...])

    @pl.when(i == 0)
    def first():
        acc_ref[...] = part

    @pl.when(i > 0)
    def later():
        acc_ref[...] += part

    @pl.when(i == pl.num_programs(0) - 1)
    def last():
        row = lax.broadcasted_iota(jnp.int32, (piece, features), 0)
        square = jnp.zeros((8, features), F32)
        for h in range(2):
            rows = slice(h * piece, (h + 1) * piece)
            block_out = tokens_ref[rows, :].astype(F32) + acc_ref[rows, :]
            out_ref[rows, :] = block_out.astype(BF16)
            error = jnp.where(row < scal[1 + h], block_out - teacher_ref[rows, :].astype(F32), 0.0)
            square = square + jnp.sum((error * error).reshape(groups, 8, features), axis=0)
            g_out = error * (2.0 * scale_ref[0, 0])
            gout_ref[rows, :] = g_out
            dout_ref[rows, :] = g_out.astype(BF16)
        square_ref[...] = square


def first_grad_kernel(
    scal, dout_ref, weight_ref, s_ref, step_ref, xs_ref, gate_ref, ssm_ref, c_ref,
    dssm_ref, dgate_ref, skip_ref, grad_ref, *, tiles, groups
):
    piece = groups * 8
    width = tiles * LANES
    states = c_ref.shape[2]
    d_branch = back_dot(dout_ref[...], weight_ref[...])
    skip = jnp.zeros((1, width), F32)
    for h in range(2):
        grad = d_branch[h * piece : (h + 1) * piece]
        gate = gate_ref[h]
        sig = sigmoid(gate)
        d_ssm = grad * (gate * sig)
        dgate_ref[h] = (grad * ssm_ref[h] * (sig * (1.0 + gate * (1.0 - sig)))).astype(BF16)
        skip = skip + jnp.sum(d_ssm * xs_ref[h].astype(F32), axis=0, keepdims=True)
        dssm_ref[h] = d_ssm.reshape(groups, 8, width)
    skip_ref[...] = skip
    rate2 = -jnp.exp(s_ref[80 : 80 + states, :].astype(F32)) * LOG2E
    rates = [rate2[:, tile_cols(j)] for j in range(tiles)]

    def body(i, held):
        held = list(held)
        t = groups - 1 - i
        for s in range(7, -1, -1):
            for h in range(2):
                c = c_ref[h, t * 8 + s]
                for j in range(tiles):
                    step = step_ref[h, t, s : s + 1, tile_cols(j)]
                    dssm = dssm_ref[h, t, s : s + 1, tile_cols(j)]
                    k = h * tiles + j
                    held[k] = jnp.exp2(step * rates[j]) * (held[k] + dssm * c)
        return tuple(held)

    zero = jnp.zeros((states, LANES), F32)
    held = lax.fori_loop(0, groups, body, (zero,) * (2 * tiles))
    for h in range(2):
        for j in range(tiles):
            grad_ref[h * states : (h + 1) * states, tile_cols(j)] = held[h * tiles + j].astype(BF16)


def out_grad_kernel(even_ref, odd_ref, dout_ref, keep_ref, send_ref):
    keep_ref[0] = rows_dot(even_ref[...], dout_ref[...]).astype(BF16)
    send_ref[0] = rows_dot(odd_ref[...], dout_ref[...]).astype(BF16)


def gate_grad_kernel(scal, normed_ref, dgate_ref, *refs, count, piece):
    weights, (keep_ref, send_ref, dnormed_ref) = refs[:count], refs[count:]
    depth = weights[0].shape[0]
    width = weights[0].shape[1]
    own = jnp.concatenate(
        [normed_ref[HALO : HALO + piece], normed_ref[2 * HALO + piece : 2 * HALO + 2 * piece]], axis=0
    )
    d_gate = dgate_ref[...].reshape(2 * piece, width)

    @pl.when(pl.program_id(0) == 0)
    def clear():
        dnormed_ref[...] = jnp.zeros_like(dnormed_ref)

    for r in range(count):
        cols = slice(r * depth, (r + 1) * depth)
        target = send_ref if r % 2 else keep_ref
        target[r // 2] = rows_dot(own[:, cols], d_gate).astype(BF16)
        dnormed_ref[:, cols] += back_dot(d_gate, weights[r][...])


def backward_kernel(scal, *refs, tiles, groups, ctx, rank):
    grads = refs[: ctx - 1]
    (
        log_ref, proj_ref, s_ref, step_ref, xs_ref, b_ref, c_ref, start_ref, dssm_ref, hidden_ref,
        dxs_ref, small_ref, ddelta_ref, db_ref, dc_ref,
        drive_ref, adj_ref, dstep_ref,
    ) = refs[ctx - 1 :]
    piece = groups * 8
    width = tiles * LANES
    states = b_ref.shape[2]
    i = pl.program_id(0)
    head = s_ref[0:HEAD, :].astype(F32)
    for h in range(2):
        drive_ref[h] = step_ref[h] * xs_ref[h].astype(F32).reshape(groups, 8, width)

    @pl.when(i == 0)
    def clear():
        db_ref[...] = jnp.zeros_like(db_ref)
        dc_ref[...] = jnp.zeros_like(dc_ref)
        ddelta_ref[...] = jnp.zeros_like(ddelta_ref)

    rate = -jnp.exp(s_ref[80 : 80 + states, :].astype(F32))
    rates = [rate[:, tile_cols(j)] for j in range(tiles)]
    rates2 = [values * LOG2E for values in rates]

    def one(t, s, p, first, later, sums):
        for h in range(2):
            b = b_ref[h, p]
            c = c_ref[h, p]
            db = dc = None
            for j in range(tiles):
                cols = tile_cols(j)
                step = step_ref[h, t, s : s + 1, cols]
                drive = drive_ref[h, t, s : s + 1, cols]
                dssm = dssm_ref[h, t, s : s + 1, cols]
                k = h * tiles + j
                hidden = hidden_ref[j, h, p].astype(F32)
                before = start_ref[h, :, cols] if first else hidden_ref[j, h, p - 1].astype(F32)
                adjoint = dssm * c + later[k]
                later[k] = jnp.exp2(step * rates2[j]) * adjoint
                term = later[k] * before
                sums[j] = sums[j] + term * step
                dstep_ref[h, t, s : s + 1, cols] = jnp.sum(term * rates[j], axis=0, keepdims=True)
                adj_ref[h, t, s : s + 1, cols] = jnp.sum(adjoint * b, axis=0, keepdims=True)
                db = adjoint * drive if db is None else db + adjoint * drive
                dc = dssm * hidden if dc is None else dc + dssm * hidden
            db_ref[h, p] += db
            dc_ref[h, p] += dc

    def body(k, both):
        later, sums = list(both[: 2 * tiles]), list(both[2 * tiles :])
        t = groups - 1 - k
        for s in range(7, -1, -1):
            one(t, s, t * 8 + s, False, later, sums)
        return tuple(later + sums)

    later = tuple(
        carried(grads, log_ref, rates2[j], h, ctx, states, tile_cols(j))
        for h in range(2)
        for j in range(tiles)
    )
    zero = jnp.zeros((states, LANES), F32)
    both = lax.fori_loop(0, groups - 1, body, later + (zero,) * tiles)
    later, sums = list(both[: 2 * tiles]), list(both[2 * tiles :])
    for s in range(7, -1, -1):
        one(0, s, s, s == 0, later, sums)
    for j in range(tiles):
        small_ref[rank : rank + states, tile_cols(j)] = sums[j] * rates[j]
    delta = proj_ref[:, 0:rank].astype(BF16)
    pre = dot(delta, s_ref[HEAD : HEAD + rank, :]) + head[5:6]
    row = lax.broadcasted_iota(jnp.int32, (piece, width), 0)
    lows = []
    bias = jnp.zeros((1, width), F32)
    for h in range(2):
        xs = xs_ref[h].astype(F32)
        adj = adj_ref[h].reshape(piece, width)
        d_step = xs * adj + dstep_ref[h].reshape(piece, width)
        d_pre = jnp.where(row < scal[1 + h], d_step * sigmoid(pre[h * piece : (h + 1) * piece]), 0.0)
        bias = bias + jnp.sum(d_pre, axis=0, keepdims=True)
        lows.append(d_pre.astype(BF16))
        dxs_ref[h] = head[6:7] * dssm_ref[h].reshape(piece, width) + step_ref[h].reshape(piece, width) * adj
    small_ref[rank + states : rank + states + 8, :] = jnp.broadcast_to(bias, (8, width))
    low = jnp.concatenate(lows, axis=0)
    small_ref[0:rank, :] = rows_dot(delta, low)
    ddelta_ref[...] += back_dot(low, s_ref[HEAD : HEAD + rank, :])


def tail_kernel(
    scal, dproj_ref, s_ref, dxs_ref, conv_ref, x_ref, xs_ref, normed_ref, *refs, count, piece
):
    weights, (small_ref, keep_ref, send_ref, dnormed_ref, pad_ref) = refs[:count], refs[count:]
    depth = weights[0].shape[0]
    width = weights[0].shape[1]
    ext = HALO + piece

    @pl.when(pl.program_id(0) == 0)
    def clear():
        dnormed_ref[...] = jnp.zeros_like(dnormed_ref)
        for h in range(2):
            pad_ref[h, 0:HALO, :] = jnp.zeros((HALO, width), F32)
            pad_ref[h, ext : ext + 8, :] = jnp.zeros((8, width), F32)

    head = s_ref[0:HEAD, :].astype(F32)
    small_ref[8:104, :] = rows_dot(dproj_ref[...], xs_ref[...].reshape(2 * piece, width))
    d_xs = dot(dproj_ref[...], s_ref[96:192, :])
    taps = [jnp.zeros((1, width), F32) for _ in range(5)]
    lows = []
    for h in range(2):
        conv = conv_ref[h]
        sig = sigmoid(conv)
        d_conv = (dxs_ref[h] + d_xs[h * piece : (h + 1) * piece]) * (sig * (1.0 + conv * (1.0 - sig)))
        pad_ref[h, HALO:ext, :] = d_conv
        x = x_ref[h].astype(F32)
        for k in range(4):
            rows = slice(HALO - 3 + k, HALO - 3 + k + piece)
            taps[k] = taps[k] + jnp.sum(d_conv * x[rows], axis=0, keepdims=True)
        taps[4] = taps[4] + jnp.sum(d_conv, axis=0, keepdims=True)
        d_x = head[3:4] * pad_ref[h, 0:ext, :]
        for k in range(3):
            d_x = d_x + head[k : k + 1] * pad_ref[h, 3 - k : 3 - k + ext, :]
        lows.append(d_x.astype(BF16))
    small_ref[0:8, :] = jnp.concatenate(taps + [jnp.zeros((3, width), F32)], axis=0)
    low = jnp.concatenate(lows, axis=0)
    for r in range(count):
        cols = slice(r * depth, (r + 1) * depth)
        target = send_ref if r % 2 else keep_ref
        target[r // 2] = rows_dot(normed_ref[:, cols], low).astype(BF16)
        dnormed_ref[:, cols] += back_dot(low, weights[r][...])


def shape(dims, dtype=F32):
    return jax.ShapeDtypeStruct(dims, dtype)


def call(kernel, name, grid, scal, args, in_specs, out_specs, out_shape, scratch, flops, exps=0):
    size = sum(a.size * a.dtype.itemsize for a in args) + sum(
        s.size * s.dtype.itemsize for s in out_shape
    )
    return pl.pallas_call(
        kernel,
        grid_spec=pltpu.PrefetchScalarGridSpec(
            num_scalar_prefetch=1,
            grid=(grid,),
            in_specs=in_specs,
            out_specs=out_specs,
            scratch_shapes=scratch,
        ),
        out_shape=out_shape,
        name=name,
        compiler_params=pltpu.CompilerParams(vmem_limit_bytes=VMEM_LIMIT),
        cost_estimate=pl.CostEstimate(flops=flops, bytes_accessed=size, transcendentals=exps),
    )(scal, *args)


def whole_spec(dims):
    return pl.BlockSpec(dims, lambda i, scal: (0,) * len(dims))


def local(
    tokens,
    teacher,
    lengths,
    pair_owner,
    norm_gain,
    in_proj,
    conv_weight,
    conv_bias,
    x_proj,
    dt_proj,
    dt_bias,
    a_log,
    skip_scale,
    out_proj,
):
    ctx = lax.axis_size("ctx")
    fsdp = lax.axis_size("fsdp")
    me_ctx = lax.axis_index("ctx")
    me_fsdp = lax.axis_index("fsdp")
    piece = tokens.shape[1] // 2
    features = tokens.shape[2]
    width = in_proj.shape[1] // 2
    rank = dt_proj.shape[0]
    states = a_log.shape[0]
    groups = piece // 8
    ext = HALO + piece
    depth = features // fsdp
    part = width // fsdp
    rows_all = 2 * piece
    elements = rows_all * states * width

    relative = jnp.arange(ctx, dtype=jnp.int32) ^ me_ctx
    pair_of = jnp.sum(
        jnp.arange(ctx, dtype=jnp.int32)[None, :]
        * (pair_owner[None, :] == relative[:, None]).astype(jnp.int32),
        axis=1,
    )
    places = jnp.stack([pair_of, ctx - 1 - pair_of])
    pair_id = pair_of[0]
    own = places[:, 0]
    limits = jnp.clip(lengths[0] - own * piece, 0, piece)
    scal = jnp.concatenate([me_fsdp[None], limits]).astype(jnp.int32)
    between = (places[:, :, None] < places[:, None, :]) & (
        places[:, None, :] < own[:, None, None]
    )
    between_back = (places[:, :, None] > places[:, None, :]) & (
        places[:, None, :] > own[:, None, None]
    )
    before = places < own[:, None]
    behind = places > own[:, None]
    has_before = jnp.stack([pair_id > 0, pair_id < ctx - 1])
    has_after = jnp.stack([pair_id < ctx - 1, pair_id > 0])
    lower = pair_owner[jnp.maximum(pair_id - 1, 0)] ^ me_ctx
    upper = pair_owner[jnp.minimum(pair_id + 1, ctx - 1)] ^ me_ctx

    rows_head = jnp.concatenate(
        [
            conv_weight,
            conv_bias[None],
            dt_bias[None],
            skip_scale[None],
            jnp.pad(norm_gain, (0, part - depth))[None],
            jnp.zeros((HEAD - 8, part), BF16),
            dt_proj,
            a_log,
            x_proj.T,
        ],
        axis=0,
    )
    small_blocks = gather_fsdp(rows_head)
    small = jnp.concatenate(small_blocks, axis=1)
    gain = jnp.concatenate([block[7, :depth] for block in small_blocks]).astype(F32)
    x_blocks = gather_fsdp(in_proj[:, :width])
    gate_blocks = gather_fsdp(after(in_proj[:, width:], x_blocks[-2]))
    out_blocks = gather_fsdp(after(out_proj, gate_blocks[-2]))

    def to_blocks(values, size):
        axis = values.ndim - 1
        return jnp.concatenate(
            [
                lax.dynamic_slice_in_dim(values, (me_fsdp ^ r) * size, size, axis=axis)
                for r in range(fsdp)
            ],
            axis=axis,
        )

    own_rows = tokens[0]
    token_rel = to_blocks(own_rows, depth).reshape(2, piece, features)
    tails = jnp.stack(gather_ctx(to_blocks(own_rows.reshape(2, piece, features)[:, piece - 3 :], depth)))
    before_rows = jnp.stack([tails[lower, 0], tails[upper, 1]])
    before_rows = jnp.where(has_before[:, None, None], before_rows, jnp.zeros_like(before_rows))
    rows_ext = jnp.concatenate(
        [jnp.zeros((2, HALO - 3, features), BF16), before_rows, token_rel], axis=1
    ).astype(F32)
    inv_rms = lax.rsqrt(jnp.mean(rows_ext * rows_ext, axis=2, keepdims=True) + EPSILON)
    normed = (rows_ext * inv_rms * gain).astype(BF16).reshape(2 * ext, features)

    count = total(jnp.sum(jnp.minimum(lengths, 2 * ctx * piece)).astype(F32)[None], ("fsdp",))
    scale = ((fsdp * rows_all * ctx) / count).reshape(1, 1)

    def cols_at(block):
        per = part // block
        return lambda i, scal: (0, (scal[0] ^ (i // per)) * per + i % per)

    def spec_small(block, offset=0):
        return pl.BlockSpec((small.shape[0], block), lambda i, scal: (0, i + offset))

    def spec_rows(block, offset=0):
        return pl.BlockSpec((2, piece, block), lambda i, scal: (0, 0, i + offset))

    def spec_groups(block):
        return pl.BlockSpec((2, groups, 8, block), lambda i, scal: (0, 0, 0, i))

    cb = min(256, part)
    steps = width // cb
    weight_specs = [pl.BlockSpec((depth, cb), cols_at(cb)) for _ in range(fsdp)]
    x_ext, conv, xs, proj = call(
        functools.partial(input_kernel, count=fsdp, piece=piece),
        "inputs", steps, scal, (normed, *x_blocks, small),
        [whole_spec((2 * ext, features)), *weight_specs, spec_small(cb)],
        [
            pl.BlockSpec((2, ext, cb), lambda i, scal: (0, 0, i)),
            spec_rows(cb),
            spec_rows(cb),
            whole_spec((rows_all, rank + 2 * states)),
        ],
        [
            shape((2, ext, width), BF16),
            shape((2, piece, width)),
            shape((2, piece, width), BF16),
            shape((rows_all, rank + 2 * states)),
        ],
        [], 2 * rows_all * features * width,
    )
    wide_dims = (2, piece, states, LANES)
    maps = proj[:, rank:].reshape(2, piece, 2 * states, 1)
    b_wide = jnp.broadcast_to(maps[:, :, :states], wide_dims)

    tiles = 4
    block = tiles * LANES
    step, ends, logs = call(
        functools.partial(end_kernel, tiles=tiles, groups=groups, rank=rank),
        "end_states", width // block, scal, (proj, small, xs, b_wide),
        [whole_spec(proj.shape), spec_small(block), spec_rows(block), whole_spec(wide_dims)],
        [
            spec_groups(block),
            pl.BlockSpec((2 * states, block), lambda i, scal: (0, i)),
            pl.BlockSpec((2, block), lambda i, scal: (0, i)),
        ],
        [shape((2, groups, 8, width)), shape((2 * states, width), BF16), shape((2, width))],
        [pltpu.VMEM((2, groups, 8, block), F32)], 5 * elements, elements,
    )
    log_hi = logs.astype(BF16)
    log_mid = (logs - log_hi.astype(F32)).astype(BF16)
    log_lo = (logs - log_hi.astype(F32) - log_mid.astype(F32)).astype(BF16)
    sent = jnp.concatenate([ends, log_hi, log_mid, log_lo, jnp.zeros((2, width), BF16)], axis=0)
    end_blocks = gather_ctx(sent)
    log_parts = jnp.stack([b[2 * states : 2 * states + 6] for b in end_blocks]).astype(F32)
    log_all = log_parts[:, 0:2] + log_parts[:, 2:4] + log_parts[:, 4:6]

    def spans(inside, wanted):
        summed = jnp.sum(
            jnp.where(inside[..., None], log_all.transpose(1, 0, 2)[:, None], 0.0), axis=2
        )
        return jnp.where(wanted[..., None], summed, 1e30).reshape(2 * ctx, width)

    log_before = spans(between, before)
    log_behind = spans(between_back, behind)

    c_wide = jnp.broadcast_to(maps[:, :, states:], wide_dims)
    (gate,) = call(
        functools.partial(gate_kernel, count=fsdp, piece=piece),
        "gates", steps, scal, (normed, *gate_blocks),
        [whole_spec((2 * ext, features)), *weight_specs], [spec_rows(cb)],
        [shape((2, piece, width))], [], 2 * rows_all * features * width,
    )
    weight_out = jnp.concatenate(out_blocks, axis=0)

    tiles = 2
    block = tiles * LANES
    end_spec = pl.BlockSpec((2 * states, block), lambda i, scal: (0, i))
    log_spec = pl.BlockSpec((2 * ctx, block), lambda i, scal: (0, i))
    hidden_spec = pl.BlockSpec((tiles, 2, piece, states, LANES), lambda i, scal: (i, 0, 0, 0, 0))
    start_spec = pl.BlockSpec((2, states, block), lambda i, scal: (0, 0, i))
    out_spec = pl.BlockSpec((block, features), lambda i, scal: (i, 0))
    row_spec = whole_spec((rows_all, features))
    ssm, branch, hidden, starts, out_low, g_out, d_out, squares = call(
        functools.partial(forward_kernel, tiles=tiles, groups=groups, ctx=ctx, features=features),
        "forward_states", width // block, scal,
        (*end_blocks[1:], log_before, scale, small, step, xs, gate, b_wide, c_wide, weight_out,
         own_rows, teacher[0]),
        [
            *([end_spec] * (ctx - 1)), log_spec, pl.BlockSpec(memory_space=pltpu.SMEM),
            spec_small(block), spec_groups(block), spec_rows(block), spec_rows(block),
            whole_spec(wide_dims), whole_spec(wide_dims), out_spec, row_spec, row_spec,
        ],
        [
            spec_rows(block), spec_rows(block), hidden_spec, start_spec, row_spec, row_spec, row_spec,
            whole_spec((8, features)),
        ],
        [
            shape((2, piece, width)),
            shape((2, piece, width), BF16),
            shape((width // LANES, 2, piece, states, LANES), BF16),
            shape((2, states, width)),
            shape((rows_all, features), BF16),
            shape((rows_all, features)),
            shape((rows_all, features), BF16),
            shape((8, features)),
        ],
        [
            pltpu.VMEM((2, groups, 8, block), F32),
            pltpu.VMEM((2, groups, 8, block), F32),
            pltpu.VMEM((rows_all, features), F32),
        ],
        10 * elements, elements,
    )
    tiles = 4
    block = tiles * LANES
    d_ssm, d_gate, grad_skip, first_grads = call(
        functools.partial(first_grad_kernel, tiles=tiles, groups=groups),
        "first_grads", width // block, scal,
        (d_out, weight_out, small, step, xs, gate, ssm, c_wide),
        [
            row_spec, pl.BlockSpec((block, features), lambda i, scal: (i, 0)), spec_small(block),
            spec_groups(block), spec_rows(block), spec_rows(block), spec_rows(block), whole_spec(wide_dims),
        ],
        [
            spec_groups(block), spec_rows(block), pl.BlockSpec((1, block), lambda i, scal: (0, i)),
            pl.BlockSpec((2 * states, block), lambda i, scal: (0, i)),
        ],
        [
            shape((2, groups, 8, width)),
            shape((2, piece, width), BF16),
            shape((1, width)),
            shape((2 * states, width), BF16),
        ],
        [], 6 * elements, elements,
    )
    grad_blocks = gather_ctx(first_grads)

    pairs = fsdp // 2
    subs = part // cb
    branch_rows = branch.reshape(rows_all, width)
    keep_out, send_out = pl.pallas_call(
        out_grad_kernel,
        grid=(pairs, subs),
        in_specs=[
            pl.BlockSpec((rows_all, cb), lambda k, s: (0, 2 * k * subs + s)),
            pl.BlockSpec((rows_all, cb), lambda k, s: (0, (2 * k + 1) * subs + s)),
            pl.BlockSpec((rows_all, features), lambda k, s: (0, 0)),
        ],
        out_specs=[pl.BlockSpec((1, cb, features), lambda k, s: (k, s, 0))] * 2,
        out_shape=[shape((pairs, part, features), BF16)] * 2,
        name="out_grads",
        compiler_params=pltpu.CompilerParams(vmem_limit_bytes=VMEM_LIMIT),
        cost_estimate=pl.CostEstimate(
            flops=2 * rows_all * width * features, bytes_accessed=9 * 2**20, transcendentals=0
        ),
    )(branch_rows, branch_rows, d_out)
    pair_spec = pl.BlockSpec((pairs, depth, cb), lambda i, scal: (0, 0, i))
    pair_at = pl.BlockSpec(
        (pairs, depth, cb), lambda i, scal: (0, 0, cols_at(cb)(i, scal)[1])
    )
    keep_gate, send_gate, d_normed_gate = call(
        functools.partial(gate_grad_kernel, count=fsdp, piece=piece),
        "gate_grads", steps, scal, (normed, d_gate, *gate_blocks),
        [whole_spec((2 * ext, features)), spec_rows(cb), *weight_specs],
        [pair_at, pair_at, row_spec],
        [shape((pairs, depth, width), BF16)] * 2 + [shape((rows_all, features))],
        [], 4 * rows_all * features * width,
    )
    sum_out = reduce_shard(keep_out, send_out, False)
    sum_gate = reduce_shard(keep_gate, send_gate, True)

    tiles = 2
    block = tiles * LANES
    d_xs, small_back, d_delta, db_wide, dc_wide = call(
        functools.partial(backward_kernel, tiles=tiles, groups=groups, ctx=ctx, rank=rank),
        "backward_states", width // block, scal,
        (*grad_blocks[1:], log_behind, proj, small, step, xs, b_wide, c_wide, starts, d_ssm, hidden),
        [
            *([end_spec] * (ctx - 1)), log_spec, whole_spec(proj.shape), spec_small(block),
            spec_groups(block), spec_rows(block), whole_spec(wide_dims), whole_spec(wide_dims),
            start_spec, spec_groups(block), hidden_spec,
        ],
        [
            spec_rows(block), pl.BlockSpec((rank + states + 8, block), lambda i, scal: (0, i)),
            whole_spec((rows_all, rank)), whole_spec(wide_dims), whole_spec(wide_dims),
        ],
        [
            shape((2, piece, width)),
            shape((rank + states + 8, width)),
            shape((rows_all, rank)),
            shape(wide_dims),
            shape(wide_dims),
        ],
        [pltpu.VMEM((2, groups, 8, block), F32)] * 3,
        24 * elements, elements,
    )
    d_proj = jnp.concatenate(
        [
            d_delta,
            jnp.sum(db_wide, axis=3).reshape(rows_all, states),
            jnp.sum(dc_wide, axis=3).reshape(rows_all, states),
        ],
        axis=1,
    ).astype(BF16)
    half_steps = steps // 2
    halves = []
    for side in range(2):
        base = side * half_steps

        def place(i, scal, base=base):
            return cols_at(cb)(i + base, scal)[1]

        def at_rows(dims):
            return pl.BlockSpec((2, dims, cb), lambda i, scal, place=place: (0, 0, place(i, scal)))

        def at_cols(i, scal, base=base):
            return 0, i + base

        halves.append(
            call(
                functools.partial(tail_kernel, count=fsdp, piece=piece),
                "tail_grads", half_steps, scal,
                (d_proj, small, d_xs, conv, x_ext, xs, normed, *x_blocks),
                [
                    whole_spec(d_proj.shape),
                    pl.BlockSpec((small.shape[0], cb), lambda i, scal, place=place: (0, place(i, scal))),
                    at_rows(piece), at_rows(piece), at_rows(ext), at_rows(piece),
                    whole_spec((2 * ext, features)),
                    *([pl.BlockSpec((depth, cb), at_cols)] * fsdp),
                ],
                [
                    pl.BlockSpec((104, cb), lambda i, scal: (0, i)),
                    pair_spec, pair_spec, whole_spec((2 * ext, features)),
                ],
                [
                    shape((104, width // 2)),
                    shape((pairs, depth, width // 2), BF16),
                    shape((pairs, depth, width // 2), BF16),
                    shape((2 * ext, features)),
                ],
                [pltpu.VMEM((2, ext + 8, cb), F32)],
                4 * rows_all * features * width // 2,
            )
        )
    sum_x = [
        reduce_shard(side[1], side[2], ctx_first) for side, ctx_first in zip(halves, (False, True))
    ]
    tail_small = to_blocks(jnp.concatenate([halves[0][0], halves[1][0]], axis=1), part)
    d_normed = (halves[0][3] + halves[1][3]).reshape(2, ext, features)
    halo_grad = d_normed[:, HALO - 3 : HALO]
    halo_all = jnp.stack(gather_ctx(halo_grad.astype(BF16))).astype(F32)
    from_next = jnp.stack([halo_all[upper, 0], halo_all[lower, 1]])
    from_next = jnp.where(has_after[:, None, None], from_next, 0.0)
    unit = rows_ext * inv_rms
    own_normed = d_normed[:, HALO:] + d_normed_gate.reshape(2, piece, features)
    grad_gain = jnp.sum(halo_grad * unit[:, HALO - 3 : HALO], axis=(0, 1)) + jnp.sum(
        own_normed * unit[:, HALO:], axis=(0, 1)
    )
    grad_gain = jnp.pad(grad_gain.reshape(fsdp, 1, depth), ((0, 0), (0, 0), (0, part - depth)))
    small_rows = jnp.concatenate(
        [
            tail_small[0:5],
            small_back[rank + states : rank + states + 1],
            grad_skip,
            grad_gain.transpose(1, 0, 2).reshape(1, width),
            jnp.zeros((HEAD - 8, width), F32),
            small_back[0 : rank + states],
            tail_small[8:104],
        ],
        axis=0,
    ).astype(BF16)
    small_pairs = small_rows.reshape(small_rows.shape[0], pairs, 2, part).transpose(2, 1, 0, 3)
    sum_small = reduce_shard(small_pairs[0], small_pairs[1], False).astype(F32)

    own_normed = own_normed + jnp.pad(from_next, ((0, 0), (piece - 3, 0), (0, 0)))
    own_inv = inv_rms[:, HALO:]
    own_u = rows_ext[:, HALO:]
    scaled = own_normed * gain
    d_rows = own_inv * scaled - own_u * (own_inv * own_inv * own_inv) * jnp.mean(
        scaled * own_u, axis=2, keepdims=True
    )
    d_rows = d_rows.reshape(rows_all, features)

    grad_tokens = (to_blocks(d_rows, depth) + g_out)[None]
    square_total = total(jnp.sum(squares)[None], ("fsdp", "ctx"))[0]
    loss = square_total / (count[0] * features)
    grad_in = jnp.concatenate([*sum_x, sum_gate], axis=1).astype(F32)
    return (
        out_low[None],
        loss,
        grad_tokens,
        sum_small[7, :depth],
        grad_in,
        sum_small[0:4],
        sum_small[4],
        sum_small[96:192].T,
        sum_small[HEAD : HEAD + rank],
        sum_small[5],
        sum_small[80 : 80 + states],
        sum_small[6],
        sum_out.astype(F32),
    )


def solution(mesh):
    in_specs = (
        P("fsdp", "ctx", None),
        P("fsdp", "ctx", None),
        P("fsdp", None),
        P(),
        P("fsdp"),
        P("fsdp", None),
        P(None, "fsdp"),
        P("fsdp"),
        P("fsdp", None),
        P(None, "fsdp"),
        P("fsdp"),
        P(None, "fsdp"),
        P("fsdp"),
        P("fsdp", None),
    )
    out_specs = (
        P("fsdp", "ctx", None),
        P(),
        P("fsdp", "ctx", None),
        P("fsdp"),
        P("fsdp", None),
        P(None, "fsdp"),
        P("fsdp"),
        P("fsdp", None),
        P(None, "fsdp"),
        P("fsdp"),
        P(None, "fsdp"),
        P("fsdp"),
        P("fsdp", None),
    )
    return jax.shard_map(local, mesh=mesh, in_specs=in_specs, out_specs=out_specs, check_vma=False)
```

```python
import functools

import jax
import jax.numpy as jnp
from jax import lax
from jax.experimental import pallas as pl
from jax.experimental.pallas import tpu as pltpu
from jax.sharding import PartitionSpec as P

EPSILON = 1e-05
LOG2E = 1.4426950408889634
F32 = jnp.float32
BF16 = jnp.bfloat16
LANES = 128
HALO = 16
HEAD = 16
VMEM_LIMIT = 60 * 1024 * 1024


def swap(values, axis, bit):
    size = lax.axis_size(axis)
    return lax.ppermute(values, axis, [(i, i ^ bit) for i in range(size)])


def after(values, earlier):
    return lax.optimization_barrier((values, earlier))[0]


def bits_of(size):
    return [1 << k for k in range(size.bit_length() - 1)]


def gather_fsdp(values):
    blocks = {0: values}
    for bit in reversed(bits_of(lax.axis_size("fsdp"))):
        for r in sorted(blocks):
            blocks[r | bit] = swap(blocks[r], "fsdp", bit)
    return [blocks[r] for r in range(len(blocks))]


def gather_far(values):
    size = lax.axis_size("ctx")
    return [values] + [swap(values, "ctx", j) for j in range(2, size, 2)]


def gather_near(far):
    return [block for own in far for block in (own, swap(own, "ctx", 1))]


def together(*trees):
    return lax.optimization_barrier(trees)


def gather_small_ctx(values):
    stacked = values[None]
    for bit in bits_of(lax.axis_size("ctx")):
        stacked = jnp.concatenate([stacked, swap(stacked, "ctx", bit)], axis=0)
    return stacked


def three_parts(values):
    high = values.astype(BF16)
    rest = values - high.astype(F32)
    middle = rest.astype(BF16)
    return high, middle, (rest - middle.astype(F32)).astype(BF16)


def total(values, axes):
    for axis in axes:
        for bit in bits_of(lax.axis_size(axis)):
            values = values + swap(values, axis, bit)
    return values


def joined(kept, received):
    return (kept.astype(F32) + received.astype(F32)).astype(BF16)


def halves_of(values, bit):
    half = values.shape[1] // 2
    up = (lax.axis_index("ctx") & bit) != 0
    return values[:, :half], values[:, half:], up


def fsdp_step(bit):
    return lambda values: (values[0::2], swap(values[1::2], "fsdp", bit), joined)


def scatter_step(bit):
    def run(values):
        low, high, up = halves_of(values, bit)
        return jnp.where(up, high, low), swap(jnp.where(up, low, high), "ctx", bit), joined

    return run


def spread_step(bit):
    def finish(own, other):
        up = (lax.axis_index("ctx") & bit) != 0
        return jnp.concatenate([jnp.where(up, other, own), jnp.where(up, own, other)], axis=1)

    return lambda values: (values, swap(values, "ctx", bit), finish)


def reduce_steps(ctx_first, turn=0):
    fsdp_steps = [fsdp_step(bit) for bit in bits_of(lax.axis_size("fsdp"))[1:]]
    bits = bits_of(lax.axis_size("ctx"))
    bits = bits[turn:] + bits[:turn]
    scatter = [scatter_step(bit) for bit in bits]
    spread = [spread_step(bit) for bit in reversed(bits)]
    return (scatter + fsdp_steps if ctx_first else fsdp_steps + scatter) + spread


def advance(chains, beside=()):
    begun = [(steps.pop(0)(values) if steps else None, steps, values) for steps, values in chains]
    received = [step[1] for step, _, _ in begun if step]
    received, beside = together(received, beside)
    after = []
    for step, steps, values in begun:
        if step:
            values = step[2](step[0], received.pop(0))
        after.append((steps, values))
    return after, beside


def fsdp_blocks(blocks):
    for bit in bits_of(lax.axis_size("fsdp")):
        blocks = [joined(k, swap(v, "fsdp", bit)) for k, v in zip(blocks[0::2], blocks[1::2])]
        yield blocks


def fsdp_selected(blocks, bit):
    up = (lax.axis_index("fsdp") & bit) != 0
    return [
        joined(jnp.where(up, high, low), swap(jnp.where(up, low, high), "fsdp", bit))
        for low, high in zip(blocks[0::2], blocks[1::2])
    ]


def side_by_side(values, rows):
    return jnp.concatenate([values[:rows], values[rows:]], axis=1)


def one_above(values, columns):
    return jnp.concatenate([values[:, :columns], values[:, columns:]], axis=0)


def dot(left, right):
    return jnp.dot(left, right, preferred_element_type=F32)


def rows_dot(left, right):
    return lax.dot_general(left, right, (((0,), (0,)), ((), ())), preferred_element_type=F32)


def back_dot(left, right):
    return lax.dot_general(left, right, (((1,), (1,)), ((), ())), preferred_element_type=F32)


def sigmoid(values):
    return 1.0 / (1.0 + jnp.exp(-values))


def softplus(values):
    small = jnp.exp(-jnp.abs(values))
    grown = 1.0 + small
    part = jnp.where(grown == 1.0, small, jnp.log(grown) * (small / jnp.maximum(grown - 1.0, 1e-30)))
    return jnp.maximum(values, 0.0) + part


def tile_cols(j):
    return slice(j * LANES, (j + 1) * LANES)


def input_kernel(scal, normed_ref, *refs, count, piece):
    weights, (s_ref, x_ref, conv_ref, xs_ref, proj_ref) = refs[:count], refs[count:]
    depth = weights[0].shape[0]
    width = weights[0].shape[1]
    mixed = dot(normed_ref[:, 0:depth], weights[0][...])
    for r in range(1, count):
        mixed = mixed + dot(normed_ref[:, r * depth : (r + 1) * depth], weights[r][...])
    x_low = mixed.astype(BF16).reshape(2, HALO + piece, width)
    x_ref[...] = x_low
    x = x_low.astype(F32)
    head = s_ref[0:HEAD, :].astype(F32)
    conv = head[4:5] + x[:, HALO - 3 : HALO - 3 + piece] * head[0:1]
    for k in range(1, 4):
        conv = conv + x[:, HALO - 3 + k : HALO - 3 + k + piece] * head[k : k + 1]
    conv_ref[...] = conv
    xs = (conv * sigmoid(conv)).astype(BF16)
    xs_ref[...] = xs
    part = back_dot(xs.reshape(2 * piece, width), s_ref[96:192, :])

    @pl.when(pl.program_id(0) == 0)
    def first():
        proj_ref[...] = part

    @pl.when(pl.program_id(0) > 0)
    def later():
        proj_ref[...] += part


def gate_kernel(scal, normed_ref, *refs, count, piece):
    weights, (gate_ref,) = refs[:count], refs[count:]
    depth = weights[0].shape[0]
    width = weights[0].shape[1]
    own = jnp.concatenate(
        [normed_ref[HALO : HALO + piece], normed_ref[2 * HALO + piece : 2 * HALO + 2 * piece]], axis=0
    )
    gate = dot(own[:, 0:depth], weights[0][...])
    for r in range(1, count):
        gate = gate + dot(own[:, r * depth : (r + 1) * depth], weights[r][...])
    gate_ref[...] = gate.reshape(2, piece, width)


def end_kernel(
    scal, proj_ref, s_ref, xs_ref, b_ref, step_ref, end_ref, log_ref, drive_ref, *, tiles, groups, rank
):
    piece = groups * 8
    width = tiles * LANES
    states = b_ref.shape[2]
    head = s_ref[0:HEAD, :].astype(F32)
    delta = proj_ref[:, 0:rank].astype(BF16)
    pre = dot(delta, s_ref[HEAD : HEAD + rank, :]) + head[5:6]
    row = lax.broadcasted_iota(jnp.int32, (piece, width), 0)
    for h in range(2):
        step = softplus(pre[h * piece : (h + 1) * piece])
        step = jnp.where(row < scal[1 + h], step, 0.0)
        log_ref[h : h + 1, :] = jnp.sum(step, axis=0, keepdims=True)
        step_ref[h] = step.reshape(groups, 8, width)
        drive_ref[h] = (step * xs_ref[h].astype(F32)).reshape(groups, 8, width)
    rate2 = -jnp.exp(s_ref[80 : 80 + states, :].astype(F32)) * LOG2E
    rates = [rate2[:, tile_cols(j)] for j in range(tiles)]

    def body(t, held):
        held = list(held)
        for s in range(8):
            for h in range(2):
                b = b_ref[h, t * 8 + s]
                for j in range(tiles):
                    step = step_ref[h, t, s : s + 1, tile_cols(j)]
                    drive = drive_ref[h, t, s : s + 1, tile_cols(j)]
                    k = h * tiles + j
                    held[k] = jnp.exp2(step * rates[j]) * held[k] + drive * b
        return tuple(held)

    zero = jnp.zeros((states, LANES), F32)
    held = lax.fori_loop(0, groups, body, (zero,) * (2 * tiles))
    for h in range(2):
        for j in range(tiles):
            end_ref[h * states : (h + 1) * states, tile_cols(j)] = held[h * tiles + j].astype(BF16)


def carried(ends, log_ref, rate2, h, ctx, states, cols):
    value = jnp.zeros((states, LANES), F32)
    for j in range(1, ctx):
        decay = jnp.exp2(rate2 * log_ref[h * ctx + j : h * ctx + j + 1, cols])
        value = value + decay * ends[j - 1][h * states : (h + 1) * states, cols].astype(F32)
    return value


def forward_kernel(scal, *refs, tiles, groups, ctx, features):
    ends = refs[: ctx - 1]
    log_ref, s_ref, step_ref, xs_ref, gate_ref, b_ref, cdiag_ref, weight_ref = refs[ctx - 1 : ctx + 7]
    rest = refs[ctx + 7 :]
    scale_ref, tokens_ref, teacher_ref = rest[:3]
    ssm_ref, branch_ref, hidden_ref, start_ref, out_ref, gout_ref, dout_ref, square_ref = rest[3:11]
    drive_ref, read_ref, odd_ref, even_ref, acc_ref = rest[11:]
    piece = groups * 8
    width = tiles * LANES
    states = b_ref.shape[2]
    i = pl.program_id(0)
    head = s_ref[0:HEAD, :].astype(F32)
    for h in range(2):
        drive_ref[h] = step_ref[h] * xs_ref[h].astype(F32).reshape(groups, 8, width)
    rate2 = -jnp.exp(s_ref[80 : 80 + states, :].astype(F32)) * LOG2E
    rates = [rate2[:, tile_cols(j)] for j in range(tiles)]
    held = []
    for h in range(2):
        for j in range(tiles):
            held.append(carried(ends, log_ref, rates[j], h, ctx, states, tile_cols(j)))
            start_ref[h, :, tile_cols(j)] = held[-1]

    def scan(t, held, keep_ref):
        held = list(held)
        for s in range(16):
            p = t * 16 + s
            for h in range(2):
                b = b_ref[h, p]
                for j in range(tiles):
                    cols = tile_cols(j)
                    step = step_ref[h, t * 2 + s // 8, s % 8 : s % 8 + 1, cols]
                    drive = drive_ref[h, t * 2 + s // 8, s % 8 : s % 8 + 1, cols]
                    k = h * tiles + j
                    held[k] = jnp.exp2(step * rates[j]) * held[k] + drive * b
                    low = held[k].astype(BF16)
                    hidden_ref[j, h, p] = low
                    keep_ref[h, j, s * states : (s + 1) * states, :] = low
        return tuple(held)

    def read(t, keep_ref):
        for h in range(2):
            for j in range(tiles):
                out = dot(cdiag_ref[h, t], keep_ref[h, j])
                read_ref[h, t * 2, :, tile_cols(j)] = out[0:8]
                read_ref[h, t * 2 + 1, :, tile_cols(j)] = out[8:16]

    def body(k, held):
        t = 2 * k + 1
        read(t - 1, even_ref)
        held = scan(t, held, odd_ref)
        read(t, odd_ref)
        return scan(t + 1, held, even_ref)

    blocks = groups // 2
    held = scan(0, held, even_ref)
    held = lax.fori_loop(0, blocks // 2 - 1, body, held)
    read(blocks - 2, even_ref)
    scan(blocks - 1, held, odd_ref)
    read(blocks - 1, odd_ref)
    branches = []
    for h in range(2):
        ssm = read_ref[h].reshape(piece, width) + head[6:7] * xs_ref[h].astype(F32)
        ssm_ref[h] = ssm
        gate = gate_ref[h]
        branches.append((ssm * (gate * sigmoid(gate))).astype(BF16))
        branch_ref[h] = branches[-1]
    part = dot(jnp.concatenate(branches, axis=0), weight_ref[...])

    @pl.when(i == 0)
    def first():
        acc_ref[...] = part

    @pl.when(i > 0)
    def later():
        acc_ref[...] += part

    @pl.when(i == pl.num_programs(0) - 1)
    def last():
        row = lax.broadcasted_iota(jnp.int32, (piece, features), 0)
        square = jnp.zeros((8, features), F32)
        for h in range(2):
            rows = slice(h * piece, (h + 1) * piece)
            block_out = tokens_ref[rows, :].astype(F32) + acc_ref[rows, :]
            out_ref[rows, :] = block_out.astype(BF16)
            error = jnp.where(row < scal[1 + h], block_out - teacher_ref[rows, :].astype(F32), 0.0)
            square = square + jnp.sum((error * error).reshape(groups, 8, features), axis=0)
            g_out = error * (2.0 * scale_ref[0, 0])
            gout_ref[rows, :] = g_out
            dout_ref[rows, :] = g_out.astype(BF16)
        square_ref[...] = square


def first_grad_kernel(
    scal, dout_ref, weight_ref, s_ref, step_ref, xs_ref, gate_ref, ssm_ref, c_ref,
    dssm_ref, dgate_ref, skip_ref, grad_ref, *, tiles, groups
):
    piece = groups * 8
    width = tiles * LANES
    states = c_ref.shape[2]
    d_branch = back_dot(dout_ref[...], weight_ref[...])
    skip = jnp.zeros((1, width), F32)
    for h in range(2):
        grad = d_branch[h * piece : (h + 1) * piece]
        gate = gate_ref[h]
        sig = sigmoid(gate)
        d_ssm = grad * (gate * sig)
        dgate_ref[h] = (grad * ssm_ref[h] * (sig * (1.0 + gate * (1.0 - sig)))).astype(BF16)
        skip = skip + jnp.sum(d_ssm * xs_ref[h].astype(F32), axis=0, keepdims=True)
        dssm_ref[h] = d_ssm.reshape(groups, 8, width)
    skip_ref[...] = skip
    rate2 = -jnp.exp(s_ref[80 : 80 + states, :].astype(F32)) * LOG2E
    rates = [rate2[:, tile_cols(j)] for j in range(tiles)]

    def body(i, held):
        held = list(held)
        t = groups - 1 - i
        for s in range(7, -1, -1):
            for h in range(2):
                c = c_ref[h, t * 8 + s]
                for j in range(tiles):
                    step = step_ref[h, t, s : s + 1, tile_cols(j)]
                    dssm = dssm_ref[h, t, s : s + 1, tile_cols(j)]
                    k = h * tiles + j
                    held[k] = jnp.exp2(step * rates[j]) * (held[k] + dssm * c)
        return tuple(held)

    zero = jnp.zeros((states, LANES), F32)
    held = lax.fori_loop(0, groups, body, (zero,) * (2 * tiles))
    for h in range(2):
        for j in range(tiles):
            grad_ref[h * states : (h + 1) * states, tile_cols(j)] = held[h * tiles + j].astype(BF16)


def out_grad_kernel(even_ref, odd_ref, dout_ref, keep_ref, send_ref):
    keep_ref[0] = rows_dot(even_ref[...], dout_ref[...]).astype(BF16)
    send_ref[0] = rows_dot(odd_ref[...], dout_ref[...]).astype(BF16)


def gate_grad_kernel(scal, normed_ref, dgate_ref, *refs, count, piece):
    weights, (keep_ref, send_ref, dnormed_ref) = refs[:count], refs[count:]
    depth = weights[0].shape[0]
    width = weights[0].shape[1]
    own = jnp.concatenate(
        [normed_ref[HALO : HALO + piece], normed_ref[2 * HALO + piece : 2 * HALO + 2 * piece]], axis=0
    )
    d_gate = dgate_ref[...].reshape(2 * piece, width)

    @pl.when(pl.program_id(0) == 0)
    def clear():
        dnormed_ref[...] = jnp.zeros_like(dnormed_ref)

    for r in range(count):
        cols = slice(r * depth, (r + 1) * depth)
        target = send_ref if r % 2 else keep_ref
        target[r // 2] = rows_dot(own[:, cols], d_gate).astype(BF16)
        dnormed_ref[:, cols] += back_dot(d_gate, weights[r][...])


def backward_kernel(scal, *refs, tiles, groups, ctx, rank):
    grads = refs[: ctx - 1]
    (
        log_ref, proj_ref, s_ref, step_ref, xs_ref, c_ref, bdiag_ref, start_ref, dssm_ref, hidden_ref,
        dxs_ref, small_ref, ddelta_ref, db_ref, dc_ref,
        adj_ref, dstep_ref, dbs_ref, dcs_ref, adj_odd, adj_even, term_odd, term_even,
    ) = refs[ctx - 1 :]
    piece = groups * 8
    width = tiles * LANES
    states = c_ref.shape[2]
    blocks = groups // 2
    i = pl.program_id(0)
    head = s_ref[0:HEAD, :].astype(F32)

    @pl.when(i == 0)
    def clear():
        dbs_ref[...] = jnp.zeros_like(dbs_ref)
        dcs_ref[...] = jnp.zeros_like(dcs_ref)
        ddelta_ref[...] = jnp.zeros_like(ddelta_ref)

    rate = -jnp.exp(s_ref[80 : 80 + states, :].astype(F32))
    rates = [rate[:, tile_cols(j)] for j in range(tiles)]
    rates2 = [values * LOG2E for values in rates]
    row16 = lax.broadcasted_iota(jnp.int32, (16, 16 * states), 0)
    col16 = lax.broadcasted_iota(jnp.int32, (16, 16 * states), 1)
    same = (col16 // states == row16).astype(F32)
    same_low = same.astype(BF16)

    def scan(t, first, later, sums, adj_keep, term_keep):
        for h in range(2):
            for s in range(15, -1, -1):
                p = t * 16 + s
                c = c_ref[h, p]
                for j in range(tiles):
                    cols = tile_cols(j)
                    step = step_ref[h, t * 2 + s // 8, s % 8 : s % 8 + 1, cols]
                    dssm = dssm_ref[h, t * 2 + s // 8, s % 8 : s % 8 + 1, cols]
                    k = h * tiles + j
                    if first and s == 0:
                        before = start_ref[h, :, cols]
                    else:
                        before = hidden_ref[j, h, p - 1].astype(F32)
                    adjoint = dssm * c + later[k]
                    later[k] = jnp.exp2(step * rates2[j]) * adjoint
                    term = later[k] * before
                    sums[j] = sums[j] + term * step
                    place = slice(s * states, (s + 1) * states)
                    adj_keep[h, j, place, :] = adjoint.astype(BF16)
                    term_keep[h, j, place, :] = (term * rates[j]).astype(BF16)

    def products(t, adj_keep, term_keep):
        for h in range(2):
            db = dc = None
            for j in range(tiles):
                cols = tile_cols(j)
                adjoint = adj_keep[h, j]
                out = dot(bdiag_ref[h, t], adjoint)
                adj_ref[h, t * 2, :, cols] = out[0:8]
                adj_ref[h, t * 2 + 1, :, cols] = out[8:16]
                out = dot(same_low, term_keep[h, j])
                dstep_ref[h, t * 2, :, cols] = out[0:8]
                dstep_ref[h, t * 2 + 1, :, cols] = out[8:16]
                step = step_ref[h, pl.ds(t * 2, 2), :, cols].reshape(16, LANES)
                dssm = dssm_ref[h, pl.ds(t * 2, 2), :, cols].reshape(16, LANES)
                drive = (step * xs_ref[h, pl.ds(t * 16, 16), cols].astype(F32)).astype(BF16)
                hidden = hidden_ref[j, h, pl.ds(t * 16, 16)].reshape(16 * states, LANES)
                db_now = back_dot(drive, adjoint)
                dc_now = back_dot(dssm.astype(BF16), hidden)
                db = db_now if db is None else db + db_now
                dc = dc_now if dc is None else dc + dc_now
            dbs_ref[h, t] += db
            dcs_ref[h, t] += dc

    def body(k, both):
        later, sums = list(both[: 2 * tiles]), list(both[2 * tiles :])
        t = blocks - 2 - 2 * k
        products(t + 1, adj_odd, term_odd)
        scan(t, False, later, sums, adj_even, term_even)
        products(t, adj_even, term_even)
        scan(t - 1, False, later, sums, adj_odd, term_odd)
        return tuple(later + sums)

    later = [
        carried(grads, log_ref, rates2[j], h, ctx, states, tile_cols(j))
        for h in range(2)
        for j in range(tiles)
    ]
    sums = [jnp.zeros((states, LANES), F32)] * tiles
    scan(blocks - 1, False, later, sums, adj_odd, term_odd)
    both = lax.fori_loop(0, blocks // 2 - 1, body, tuple(later + sums))
    later, sums = list(both[: 2 * tiles]), list(both[2 * tiles :])
    products(1, adj_odd, term_odd)
    scan(0, True, later, sums, adj_even, term_even)
    products(0, adj_even, term_even)
    for j in range(tiles):
        small_ref[rank : rank + states, tile_cols(j)] = sums[j] * rates[j]
    delta = proj_ref[:, 0:rank].astype(BF16)
    pre = dot(delta, s_ref[HEAD : HEAD + rank, :]) + head[5:6]
    row = lax.broadcasted_iota(jnp.int32, (piece, width), 0)
    lows = []
    bias = jnp.zeros((1, width), F32)
    for h in range(2):
        xs = xs_ref[h].astype(F32)
        adj = adj_ref[h].reshape(piece, width)
        d_step = xs * adj + dstep_ref[h].reshape(piece, width)
        d_pre = jnp.where(row < scal[1 + h], d_step * sigmoid(pre[h * piece : (h + 1) * piece]), 0.0)
        bias = bias + jnp.sum(d_pre, axis=0, keepdims=True)
        lows.append(d_pre.astype(BF16))
        dxs_ref[h] = head[6:7] * dssm_ref[h].reshape(piece, width) + step_ref[h].reshape(piece, width) * adj
    small_ref[rank + states : rank + states + 8, :] = jnp.broadcast_to(bias, (8, width))
    low = jnp.concatenate(lows, axis=0)
    small_ref[0:rank, :] = rows_dot(delta, low)
    ddelta_ref[...] += back_dot(low, s_ref[HEAD : HEAD + rank, :])

    @pl.when(i == pl.num_programs(0) - 1)
    def last():
        for h in range(2):
            for t in range(blocks):
                db_ref[h, t : t + 1, :] = jnp.sum(dbs_ref[h, t] * same, axis=0, keepdims=True)
                dc_ref[h, t : t + 1, :] = jnp.sum(dcs_ref[h, t] * same, axis=0, keepdims=True)


def tail_kernel(
    scal, dproj_ref, s_ref, dlow_ref, dhigh_ref, conv_ref, x_ref, xs_ref, normed_ref, before_ref, *refs,
    count, piece, is_upper
):
    weights, (small_ref, keep_ref, send_ref, dnormed_ref, pad_ref) = refs[: 2 * count], refs[2 * count :]
    half = weights[0].shape[0]
    depth = 2 * half
    width = weights[0].shape[1]
    ext = HALO + piece

    @pl.when(pl.program_id(0) == 0)
    def clear():
        dnormed_ref[...] = before_ref[...]
        for h in range(2):
            pad_ref[h, 0:HALO, :] = jnp.zeros((HALO, width), F32)
            pad_ref[h, ext : ext + 8, :] = jnp.zeros((8, width), F32)

    upper = is_upper(pl.program_id(0), scal)
    head = s_ref[0:HEAD, :].astype(F32)
    small_ref[8:104, :] = rows_dot(dproj_ref[...], xs_ref[...].reshape(2 * piece, width))
    d_xs = dot(dproj_ref[...], s_ref[96:192, :])
    taps = [jnp.zeros((1, width), F32) for _ in range(5)]
    lows = []
    for h in range(2):
        conv = conv_ref[h]
        sig = sigmoid(conv)
        dxs = jnp.where(upper, dhigh_ref[h], dlow_ref[h])
        d_conv = (dxs + d_xs[h * piece : (h + 1) * piece]) * (sig * (1.0 + conv * (1.0 - sig)))
        pad_ref[h, HALO:ext, :] = d_conv
        x = x_ref[h].astype(F32)
        for k in range(4):
            rows = slice(HALO - 3 + k, HALO - 3 + k + piece)
            taps[k] = taps[k] + jnp.sum(d_conv * x[rows], axis=0, keepdims=True)
        taps[4] = taps[4] + jnp.sum(d_conv, axis=0, keepdims=True)
        d_x = head[3:4] * pad_ref[h, 0:ext, :]
        for k in range(3):
            d_x = d_x + head[k : k + 1] * pad_ref[h, 3 - k : 3 - k + ext, :]
        lows.append(d_x.astype(BF16))
    small_ref[0:8, :] = jnp.concatenate(taps + [jnp.zeros((3, width), F32)], axis=0)
    low = jnp.concatenate(lows, axis=0)
    for r in range(count):
        cols = slice(r * depth, (r + 1) * depth)
        target = send_ref if r % 2 else keep_ref
        target[r // 2] = rows_dot(normed_ref[:, cols], low).astype(BF16)
    for r in range(2 * count):
        dnormed_ref[:, r * half : (r + 1) * half] += back_dot(low, weights[r][...])


def shape(dims, dtype=F32):
    return jax.ShapeDtypeStruct(dims, dtype)


def call(kernel, name, grid, scal, args, in_specs, out_specs, out_shape, scratch, flops, exps=0):
    size = sum(a.size * a.dtype.itemsize for a in args) + sum(
        s.size * s.dtype.itemsize for s in out_shape
    )
    return pl.pallas_call(
        kernel,
        grid_spec=pltpu.PrefetchScalarGridSpec(
            num_scalar_prefetch=1,
            grid=(grid,),
            in_specs=in_specs,
            out_specs=out_specs,
            scratch_shapes=scratch,
        ),
        out_shape=out_shape,
        name=name,
        compiler_params=pltpu.CompilerParams(vmem_limit_bytes=VMEM_LIMIT),
        cost_estimate=pl.CostEstimate(flops=flops, bytes_accessed=size, transcendentals=exps),
    )(scal, *args)


def whole_spec(dims):
    return pl.BlockSpec(dims, lambda i, scal: (0,) * len(dims))


def local(
    tokens,
    teacher,
    lengths,
    pair_owner,
    norm_gain,
    in_proj,
    conv_weight,
    conv_bias,
    x_proj,
    dt_proj,
    dt_bias,
    a_log,
    skip_scale,
    out_proj,
):
    ctx = lax.axis_size("ctx")
    fsdp = lax.axis_size("fsdp")
    me_ctx = lax.axis_index("ctx")
    me_fsdp = lax.axis_index("fsdp")
    piece = tokens.shape[1] // 2
    features = tokens.shape[2]
    width = in_proj.shape[1] // 2
    rank = dt_proj.shape[0]
    states = a_log.shape[0]
    groups = piece // 8
    ext = HALO + piece
    depth = features // fsdp
    part = width // fsdp
    rows_all = 2 * piece
    elements = rows_all * states * width

    relative = jnp.arange(ctx, dtype=jnp.int32) ^ me_ctx
    pair_of = jnp.sum(
        jnp.arange(ctx, dtype=jnp.int32)[None, :]
        * (pair_owner[None, :] == relative[:, None]).astype(jnp.int32),
        axis=1,
    )
    places = jnp.stack([pair_of, ctx - 1 - pair_of])
    pair_id = pair_of[0]
    own = places[:, 0]
    limits = jnp.clip(lengths[0] - own * piece, 0, piece)
    scal = jnp.concatenate([me_fsdp[None], limits]).astype(jnp.int32)
    between = (places[:, :, None] < places[:, None, :]) & (
        places[:, None, :] < own[:, None, None]
    )
    between_back = (places[:, :, None] > places[:, None, :]) & (
        places[:, None, :] > own[:, None, None]
    )
    before = places < own[:, None]
    behind = places > own[:, None]
    has_before = jnp.stack([pair_id > 0, pair_id < ctx - 1])
    has_after = jnp.stack([pair_id < ctx - 1, pair_id > 0])
    lower = pair_owner[jnp.maximum(pair_id - 1, 0)] ^ me_ctx
    upper = pair_owner[jnp.minimum(pair_id + 1, ctx - 1)] ^ me_ctx

    own_rows = tokens[0]
    valid_slots = jnp.minimum(lengths[0], 2 * ctx * piece)
    coded = jnp.concatenate([valid_slots // 128, valid_slots % 128]).astype(BF16)[None]
    first, second = jnp.split(in_proj[:, :width], 2, axis=0)
    x_first = gather_fsdp(first)
    second, coded, last_rows, _ = lax.optimization_barrier(
        (second, coded, own_rows.reshape(2, piece, features)[:, piece - 3 :], x_first[fsdp // 2])
    )
    rows_head = jnp.concatenate(
        [
            conv_weight,
            conv_bias[None],
            dt_bias[None],
            skip_scale[None],
            jnp.pad(norm_gain, (0, part - depth))[None],
            jnp.pad(coded, ((0, 0), (0, part - 4))),
            jnp.zeros((HEAD - 9, part), BF16),
            dt_proj,
            a_log,
            x_proj.T,
        ],
        axis=0,
    )
    small_blocks = gather_fsdp(rows_head)
    small = jnp.concatenate(small_blocks, axis=1)
    gain = jnp.concatenate([block[7, :depth] for block in small_blocks]).astype(F32)
    x_second = gather_fsdp(second)
    x_blocks = [piece_now for pair in zip(x_first, x_second) for piece_now in pair]
    gate_blocks = gather_fsdp(after(in_proj[:, width:], x_second[fsdp // 2]))
    out_blocks = gather_fsdp(after(out_proj, gate_blocks[fsdp // 2]))

    def to_blocks(values, size):
        axis = values.ndim - 1
        return jnp.concatenate(
            [
                lax.dynamic_slice_in_dim(values, (me_fsdp ^ r) * size, size, axis=axis)
                for r in range(fsdp)
            ],
            axis=axis,
        )

    token_rel = to_blocks(own_rows, depth).reshape(2, piece, features)
    tails = gather_small_ctx(to_blocks(last_rows, depth))
    before_rows = jnp.stack([tails[lower, 0], tails[upper, 1]])
    before_rows = jnp.where(has_before[:, None, None], before_rows, jnp.zeros_like(before_rows))
    rows_ext = jnp.concatenate(
        [jnp.zeros((2, HALO - 3, features), BF16), before_rows, token_rel], axis=1
    ).astype(F32)
    inv_rms = lax.rsqrt(jnp.mean(rows_ext * rows_ext, axis=2, keepdims=True) + EPSILON)
    normed = (rows_ext * inv_rms * gain).astype(BF16).reshape(2 * ext, features)

    codes = jnp.stack([block[8, :4] for block in small_blocks]).astype(F32)
    count = jnp.sum(codes[:, 0:2] * 128.0 + codes[:, 2:4])
    scale = ((fsdp * rows_all * ctx) / count).reshape(1, 1)

    def cols_at(block):
        per = part // block
        return lambda i, scal: (0, (scal[0] ^ (i // per)) * per + i % per)

    def spec_small(block, offset=0):
        return pl.BlockSpec((small.shape[0], block), lambda i, scal: (0, i + offset))

    def spec_rows(block, offset=0):
        return pl.BlockSpec((2, piece, block), lambda i, scal: (0, 0, i + offset))

    def spec_groups(block):
        return pl.BlockSpec((2, groups, 8, block), lambda i, scal: (0, 0, 0, i))

    cb = min(256, part)
    steps = width // cb
    weight_specs = [pl.BlockSpec((depth, cb), cols_at(cb)) for _ in range(fsdp)]
    half_specs = [pl.BlockSpec((depth // 2, cb), cols_at(cb)) for _ in range(2 * fsdp)]
    x_ext, conv, xs, proj = call(
        functools.partial(input_kernel, count=2 * fsdp, piece=piece),
        "inputs", steps, scal, (normed, *x_blocks, small),
        [whole_spec((2 * ext, features)), *half_specs, spec_small(cb)],
        [
            pl.BlockSpec((2, ext, cb), lambda i, scal: (0, 0, i)),
            spec_rows(cb),
            spec_rows(cb),
            whole_spec((rows_all, rank + 2 * states)),
        ],
        [
            shape((2, ext, width), BF16),
            shape((2, piece, width)),
            shape((2, piece, width), BF16),
            shape((rows_all, rank + 2 * states)),
        ],
        [], 2 * rows_all * features * width,
    )
    wide_dims = (2, piece, states, LANES)
    maps = proj[:, rank:].reshape(2, piece, 2 * states, 1)
    b_wide = jnp.broadcast_to(maps[:, :, :states], wide_dims)

    tiles = 4
    block = tiles * LANES
    half = width // 2
    per_half = half // block
    group_spec = spec_groups(block)
    state_row = pl.BlockSpec((2 * states, block), lambda i, scal: (0, i))
    log_spec = pl.BlockSpec((2 * ctx, block), lambda i, scal: (0, i))
    row_spec = whole_spec((rows_all, features))
    wide_spec = whole_spec(wide_dims)
    diag_spec = whole_spec((2, piece // 16, 16, 16 * states))
    hidden_spec = pl.BlockSpec((tiles, 2, piece, states, LANES), lambda i, scal: (i, 0, 0, 0, 0))
    start_spec = pl.BlockSpec((2, states, block), lambda i, scal: (0, 0, i))
    keep_spaces = [pltpu.VMEM((2, tiles, 16 * states, LANES), BF16)]
    group_space = pltpu.VMEM((2, groups, 8, block), F32)

    step, ends, logs = call(
        functools.partial(end_kernel, tiles=tiles, groups=groups, rank=rank),
        "end_states", width // block, scal, (proj, small, xs, b_wide),
        [whole_spec(proj.shape), spec_small(block), spec_rows(block), wide_spec],
        [group_spec, state_row, pl.BlockSpec((2, block), lambda i, scal: (0, i))],
        [shape((2, groups, 8, width)), shape((2 * states, width), BF16), shape((2, width))],
        [group_space], 5 * elements, elements,
    )
    sent = jnp.concatenate([ends, *three_parts(logs), jnp.zeros((2, width), BF16)], axis=0)

    def diagonal(values):
        values = values.reshape(2, piece // 16, 1, 16, states).astype(BF16)
        same = jnp.eye(16, dtype=BF16)[None, None, :, :, None]
        return (values * same).reshape(2, piece // 16, 16, 16 * states)

    far = gather_far(sent)
    (gate,) = call(
        functools.partial(gate_kernel, count=fsdp, piece=piece),
        "gates", steps, scal, (normed, *gate_blocks),
        [whole_spec((2 * ext, features)), *weight_specs], [spec_rows(cb)],
        [shape((2, piece, width))], [], 2 * rows_all * features * width,
    )
    far, gate = together(far, gate)
    near = gather_near(far)
    c_wide = jnp.broadcast_to(maps[:, :, states:], wide_dims)
    b_diag = diagonal(maps[:, :, :states])
    c_diag = diagonal(maps[:, :, states:])
    weight_out = jnp.concatenate(out_blocks, axis=0)
    near, c_wide, b_diag, c_diag, weight_out = together(near, c_wide, b_diag, c_diag, weight_out)
    parts = jnp.stack([b[2 * states : 2 * states + 6] for b in near]).astype(F32)
    logs = (parts[:, 0:2] + parts[:, 2:4] + parts[:, 4:6]).transpose(1, 0, 2)

    def spans(inside, wanted):
        summed = jnp.sum(jnp.where(inside[..., None], logs[:, None], 0.0), axis=2)
        return jnp.where(wanted[..., None], summed, 1e30).reshape(2 * ctx, width)

    ssm, branch, hidden, starts, out_low, g_out, d_out, squares = call(
        functools.partial(forward_kernel, tiles=tiles, groups=groups, ctx=ctx, features=features),
        "forward_states", width // block, scal,
        (*near[1:], spans(between, before), small, step, xs, gate, b_wide, c_diag, weight_out,
         scale, own_rows, teacher[0]),
        [
            *([state_row] * (ctx - 1)), log_spec, spec_small(block), group_spec, spec_rows(block),
            spec_rows(block), wide_spec, diag_spec,
            pl.BlockSpec((block, features), lambda i, scal: (i, 0)),
            pl.BlockSpec(memory_space=pltpu.SMEM), row_spec, row_spec,
        ],
        [
            spec_rows(block), spec_rows(block), hidden_spec, start_spec, row_spec, row_spec, row_spec,
            whole_spec((8, features)),
        ],
        [
            shape((2, piece, width)),
            shape((2, piece, width), BF16),
            shape((width // LANES, 2, piece, states, LANES), BF16),
            shape((2, states, width)),
            shape((rows_all, features), BF16),
            shape((rows_all, features)),
            shape((rows_all, features), BF16),
            shape((8, features)),
        ],
        [group_space] * 2 + keep_spaces * 2 + [pltpu.VMEM((rows_all, features), F32)],
        10 * elements, elements,
    )
    d_ssm, d_gate, grad_skip, grads_first = call(
        functools.partial(first_grad_kernel, tiles=tiles, groups=groups),
        "first_grads", width // block, scal,
        (d_out, weight_out, small, step, xs, gate, ssm, c_wide),
        [
            row_spec, pl.BlockSpec((block, features), lambda i, scal: (i, 0)), spec_small(block),
            group_spec, spec_rows(block), spec_rows(block), spec_rows(block), wide_spec,
        ],
        [group_spec, spec_rows(block), pl.BlockSpec((1, block), lambda i, scal: (0, i)), state_row],
        [
            shape((2, groups, 8, width)),
            shape((2, piece, width), BF16),
            shape((1, width)),
            shape((2 * states, width), BF16),
        ],
        [], 6 * elements, elements,
    )
    back_far = gather_far(grads_first)

    pairs = fsdp // 2
    half_blocks = half // cb
    pair_spec = pl.BlockSpec((pairs, depth, cb), lambda i, scal: (0, 0, i))
    pair_at = pl.BlockSpec((pairs, depth, cb), lambda i, scal: (0, 0, cols_at(cb)(i, scal)[1]))
    keep_gate, send_gate, d_normed_gate = call(
        functools.partial(gate_grad_kernel, count=fsdp, piece=piece),
        "gate_grads", steps, scal, (normed, d_gate, *gate_blocks),
        [whole_spec((2 * ext, features)), spec_rows(cb), *weight_specs],
        [pair_at, pair_at, row_spec],
        [shape((pairs, depth, width), BF16)] * 2 + [shape((rows_all, features))],
        [], 4 * rows_all * features * width,
    )
    back_far, keep_gate, send_gate = together(back_far, keep_gate, send_gate)
    back_near = gather_near(back_far)
    got_gate = swap(send_gate, "fsdp", 1)
    subs = part // cb
    branch_rows = branch.reshape(rows_all, width)
    keep_out, send_out = pl.pallas_call(
        out_grad_kernel,
        grid=(pairs, subs),
        in_specs=[
            pl.BlockSpec((rows_all, cb), lambda k, s: (0, 2 * k * subs + s)),
            pl.BlockSpec((rows_all, cb), lambda k, s: (0, (2 * k + 1) * subs + s)),
            pl.BlockSpec((rows_all, features), lambda k, s: (0, 0)),
        ],
        out_specs=[pl.BlockSpec((1, cb, features), lambda k, s: (k, s, 0))] * 2,
        out_shape=[shape((pairs, part, features), BF16)] * 2,
        name="out_grads",
        compiler_params=pltpu.CompilerParams(vmem_limit_bytes=VMEM_LIMIT),
        cost_estimate=pl.CostEstimate(
            flops=2 * rows_all * width * features, bytes_accessed=9 * 2**20, transcendentals=0
        ),
    )(branch_rows, branch_rows, d_out)
    got_gate, keep_out, send_out = together(got_gate, keep_out, send_out)
    got_out = swap(send_out, "fsdp", 1)
    core_gate = joined(keep_gate, got_gate)
    back_near, got_out, core_gate = together(back_near, got_out, core_gate)
    chains = [(reduce_steps(False), joined(keep_out, got_out)), (reduce_steps(True, 1), core_gate)]
    log_behind = spans(between_back, behind)

    def backward(c):
        def at(i):
            return i + c * per_half

        return call(
            functools.partial(backward_kernel, tiles=tiles, groups=groups, ctx=ctx, rank=rank),
            "backward_states", per_half, scal,
            (*back_near[1:], log_behind, proj, small, step, xs, c_wide, b_diag, starts, d_ssm, hidden),
            [
                *([pl.BlockSpec((2 * states, block), lambda i, scal: (0, at(i)))] * (ctx - 1)),
                pl.BlockSpec((2 * ctx, block), lambda i, scal: (0, at(i))),
                whole_spec(proj.shape), spec_small(block, c * per_half),
                pl.BlockSpec((2, groups, 8, block), lambda i, scal: (0, 0, 0, at(i))),
                spec_rows(block, c * per_half), wide_spec, diag_spec,
                pl.BlockSpec((2, states, block), lambda i, scal: (0, 0, at(i))),
                pl.BlockSpec((2, groups, 8, block), lambda i, scal: (0, 0, 0, at(i))),
                pl.BlockSpec((tiles, 2, piece, states, LANES), lambda i, scal: (at(i), 0, 0, 0, 0)),
            ],
            [
                spec_rows(block), pl.BlockSpec((rank + states + 8, block), lambda i, scal: (0, i)),
                whole_spec((rows_all, rank)),
                whole_spec((2, piece // 16, 16 * states)), whole_spec((2, piece // 16, 16 * states)),
            ],
            [
                shape((2, piece, half)),
                shape((rank + states + 8, half)),
                shape((rows_all, rank)),
                shape((2, piece // 16, 16 * states)),
                shape((2, piece // 16, 16 * states)),
            ],
            [group_space] * 2 + [pltpu.VMEM((2, piece // 16, 16, 16 * states), F32)] * 2 + keep_spaces * 4,
            16 * elements // 2, elements // 2,
        )

    chains, back_first = advance(chains, backward(0))
    step, _ = together(step, [values for _, values in chains])
    chains, back_second = advance(chains, backward(1))

    def small_part(c, back):
        rows = jnp.concatenate(
            [back[1], grad_skip[:, c * half : (c + 1) * half], jnp.zeros((7, half), F32)], axis=0
        ).astype(BF16)
        return [rows[:, k * part : (k + 1) * part] for k in range(fsdp // 2)]

    d_proj = jnp.concatenate(
        [
            back_first[2] + back_second[2],
            (back_first[3] + back_second[3]).reshape(rows_all, states),
            (back_first[4] + back_second[4]).reshape(rows_all, states),
        ],
        axis=1,
    ).astype(BF16)
    half_steps = steps // 2

    def tail(c, d_proj, d_before):
        base = c * half_steps

        def place(i, scal):
            return cols_at(cb)(i + base, scal)[1]

        def at_rows(dims):
            return pl.BlockSpec((2, dims, cb), lambda i, scal: (0, 0, place(i, scal)))

        return call(
            functools.partial(
                tail_kernel, count=fsdp, piece=piece,
                is_upper=lambda i, scal: place(i, scal) >= half_blocks,
            ),
            "tail_grads", half_steps, scal,
            (d_proj, small, back_first[0], back_second[0], conv, x_ext, xs, normed, d_before, *x_blocks),
            [
                whole_spec(d_proj.shape),
                pl.BlockSpec((small.shape[0], cb), lambda i, scal: (0, place(i, scal))),
                pl.BlockSpec(
                    (2, piece, cb), lambda i, scal: (0, 0, jnp.minimum(place(i, scal), half_blocks - 1))
                ),
                pl.BlockSpec(
                    (2, piece, cb), lambda i, scal: (0, 0, jnp.maximum(place(i, scal) - half_blocks, 0))
                ),
                at_rows(piece), at_rows(ext), at_rows(piece),
                whole_spec((2 * ext, features)), whole_spec((2 * ext, features)),
                *([pl.BlockSpec((depth // 2, cb), lambda i, scal: (0, i + base))] * (2 * fsdp)),
            ],
            [
                pl.BlockSpec((104, cb), lambda i, scal: (0, i)),
                pair_spec, pair_spec, whole_spec((2 * ext, features)),
            ],
            [
                shape((104, half)),
                shape((pairs, depth, half), BF16),
                shape((pairs, depth, half), BF16),
                shape((2 * ext, features)),
            ],
            [pltpu.VMEM((2, ext + 8, cb), F32)],
            4 * rows_all * features * half,
        )

    d_before = jnp.pad(
        d_normed_gate.reshape(2, piece, features), ((0, 0), (HALO, 0), (0, 0))
    ).reshape(2 * ext, features)
    d_proj, d_before, _ = together(d_proj, d_before, [values for _, values in chains])
    chains, tail_first = advance(chains, tail(0, d_proj, d_before))
    got_ahead = swap(tail_first[2], "fsdp", 1)
    small_now = small_part(0, back_first) + small_part(1, back_second)
    for small_now in fsdp_blocks(small_now):
        pass
    d_proj, _ = together(d_proj, [values for _, values in chains])
    chains, (tail_second, got_ahead, small_now) = advance(
        chains, (tail(1, d_proj, tail_first[3]), got_ahead, small_now)
    )
    ahead = joined(tail_first[1], got_ahead)
    tail_rows = [
        values[:, k * part : (k + 1) * part].astype(BF16)
        for values in (tail_first[0], tail_second[0])
        for k in range(fsdp // 2)
    ]
    lines = small_now[0].shape[0] // 2
    lines_tail = tail_rows[0].shape[0] // 2
    got_last = swap(tail_second[2], "fsdp", 1)
    chains, (got_last, d_ext, squares) = advance(
        [*chains, (reduce_steps(True), ahead)], (got_last, tail_second[3], squares)
    )
    last = joined(tail_second[1], got_last)
    last_steps = reduce_steps(False)
    n_fsdp = len(bits_of(fsdp)) - 1
    for bit in bits_of(fsdp):
        tail_rows = fsdp_selected(tail_rows, bit)
    while last_steps:
        for_last = [([last_steps.pop(0)], last)]
        chains, tail_rows = advance([*for_last, *chains], tail_rows)
        last = chains.pop(0)[1]
        n_fsdp -= 1
        if n_fsdp == 0:
            extra = jnp.concatenate(
                [
                    side_by_side(small_now[0], lines),
                    side_by_side(tail_rows[0], lines_tail),
                    jnp.zeros((128 - lines - lines_tail, 2 * part), BF16),
                ],
                axis=0,
            ).reshape(1, -1, half)
            last = jnp.concatenate([last, extra], axis=1)
    while any(steps_left for steps_left, _ in chains):
        chains, _ = advance(chains)
    out_now, gate_now, ahead = [values for _, values in chains]
    sum_x = [ahead[0], last[0, :depth]]
    extra = last[0, depth:].reshape(128, 2 * part)
    sum_back = one_above(extra[:lines], part).astype(F32)
    sum_tail = one_above(extra[lines : lines + lines_tail], part).astype(F32)

    d_normed = d_ext.reshape(2, ext, features)
    halo_grad = d_normed[:, HALO - 3 : HALO]
    unit = rows_ext * inv_rms
    grad_gain = jnp.sum(d_normed[:, HALO - 3 :] * unit[:, HALO - 3 :], axis=(0, 1))
    square = jnp.pad(jnp.stack(three_parts(jnp.sum(squares))), (0, features - 3))
    halo_sent = jnp.concatenate(
        [halo_grad.reshape(6, features).astype(BF16), square[None], grad_gain.astype(BF16)[None]]
    )
    halo_got = gather_small_ctx(halo_sent).astype(F32)
    vector = jnp.concatenate(
        [
            to_blocks(jnp.sum(halo_got[:, 7], axis=0)[None], depth)[0],
            jnp.pad(jnp.sum(halo_got[:, 6, 0:3])[None], (0, LANES - 1)),
        ]
    )
    vector = total(vector, ("fsdp",))
    sum_gain = lax.dynamic_slice_in_dim(vector, me_fsdp * depth, depth)
    loss = vector[features] / (count * features)
    halo_all = halo_got[:, 0:6].reshape(ctx, 2, 3, features)
    from_next = jnp.stack([halo_all[upper, 0], halo_all[lower, 1]])
    from_next = jnp.where(has_after[:, None, None], from_next, 0.0)
    own_normed = d_normed[:, HALO:] + jnp.pad(from_next, ((0, 0), (piece - 3, 0), (0, 0)))
    own_inv = inv_rms[:, HALO:]
    own_u = rows_ext[:, HALO:]
    scaled = own_normed * gain
    d_rows = own_inv * scaled - own_u * (own_inv * own_inv * own_inv) * jnp.mean(
        scaled * own_u, axis=2, keepdims=True
    )
    grad_tokens = (to_blocks(d_rows.reshape(rows_all, features), depth) + g_out)[None]
    grad_in = jnp.concatenate([*sum_x, gate_now[0]], axis=1).astype(F32)
    return (
        out_low[None],
        loss,
        grad_tokens,
        sum_gain,
        grad_in,
        sum_tail[0:4],
        sum_tail[4],
        sum_tail[8:104].T,
        sum_back[0:rank],
        sum_back[rank + states],
        sum_back[rank : rank + states],
        sum_back[rank + states + 8],
        out_now[0].astype(F32),
    )


def solution(mesh):
    in_specs = (
        P("fsdp", "ctx", None),
        P("fsdp", "ctx", None),
        P("fsdp", None),
        P(),
        P("fsdp"),
        P("fsdp", None),
        P(None, "fsdp"),
        P("fsdp"),
        P("fsdp", None),
        P(None, "fsdp"),
        P("fsdp"),
        P(None, "fsdp"),
        P("fsdp"),
        P("fsdp", None),
    )
    out_specs = (
        P("fsdp", "ctx", None),
        P(),
        P("fsdp", "ctx", None),
        P("fsdp"),
        P("fsdp", None),
        P(None, "fsdp"),
        P("fsdp"),
        P("fsdp", None),
        P(None, "fsdp"),
        P("fsdp"),
        P(None, "fsdp"),
        P("fsdp"),
        P("fsdp", None),
    )
    return jax.shard_map(local, mesh=mesh, in_specs=in_specs, out_specs=out_specs, check_vma=False)
```

```python
import functools

import jax
import jax.numpy as jnp
from jax import lax
from jax.experimental import pallas as pl
from jax.experimental.pallas import tpu as pltpu
from jax.sharding import PartitionSpec as P

EPSILON = 1e-05
LOG2E = 1.4426950408889634
F32 = jnp.float32
BF16 = jnp.bfloat16
LANES = 128
HALO = 16
HEAD = 16
VMEM_LIMIT = 60 * 1024 * 1024
LIMITS = {
    "inputs": 20,
    "gates": 20,
    "end_states": 28,
    "forward_states": 60,
    "first_grads": 60,
    "gate_grads": 60,
    "backward_states": 60,
    "tail_grads": 60,
}


def swap(values, axis, bit):
    size = lax.axis_size(axis)
    return lax.ppermute(values, axis, [(i, i ^ bit) for i in range(size)])


def after(values, earlier):
    return lax.optimization_barrier((values, earlier))[0]


def bits_of(size):
    return [1 << k for k in range(size.bit_length() - 1)]


def gather_fsdp(values):
    blocks = {0: values}
    for bit in reversed(bits_of(lax.axis_size("fsdp"))):
        for r in sorted(blocks):
            blocks[r | bit] = swap(blocks[r], "fsdp", bit)
    return [blocks[r] for r in range(len(blocks))]


def gather_far(values):
    size = lax.axis_size("ctx")
    return [values] + [swap(values, "ctx", j) for j in range(2, size, 2)]


def gather_near(far, beside=()):
    blocks = [block for own in far[:2] for block in (own, swap(own, "ctx", 1))]
    rest, beside = together(far[2:], beside)
    return blocks + [block for own in rest for block in (own, swap(own, "ctx", 1))], beside


def together(*trees):
    return lax.optimization_barrier(trees)


def gather_small_ctx(values):
    stacked = values[None]
    for bit in bits_of(lax.axis_size("ctx")):
        stacked = jnp.concatenate([stacked, swap(stacked, "ctx", bit)], axis=0)
    return stacked


def three_parts(values):
    high = values.astype(BF16)
    rest = values - high.astype(F32)
    middle = rest.astype(BF16)
    return high, middle, (rest - middle.astype(F32)).astype(BF16)


def total(values, axes):
    for axis in axes:
        for bit in bits_of(lax.axis_size(axis)):
            values = values + swap(values, axis, bit)
    return values


def joined(kept, received):
    return (kept.astype(F32) + received.astype(F32)).astype(BF16)


def halves_of(values, bit):
    half = values.shape[1] // 2
    up = (lax.axis_index("ctx") & bit) != 0
    return values[:, :half], values[:, half:], up


def fsdp_step(bit):
    return lambda values: (values[0::2], swap(values[1::2], "fsdp", bit), joined)


def scatter_step(bit):
    def run(values):
        low, high, up = halves_of(values, bit)
        return jnp.where(up, high, low), swap(jnp.where(up, low, high), "ctx", bit), joined

    return run


def spread_step(bit):
    def finish(own, other):
        up = (lax.axis_index("ctx") & bit) != 0
        return jnp.concatenate([jnp.where(up, other, own), jnp.where(up, own, other)], axis=1)

    return lambda values: (values, swap(values, "ctx", bit), finish)


def gather_step(bit):
    return lambda values: (
        values, swap(values, "ctx", bit), lambda own, other: jnp.concatenate([own, other], axis=0)
    )


def sum_step(bit):
    return lambda values: (values, swap(values, "fsdp", bit), lambda own, other: own + other)


def reduce_steps(ctx_first, turn=0):
    fsdp_steps = [fsdp_step(bit) for bit in bits_of(lax.axis_size("fsdp"))[1:]]
    bits = bits_of(lax.axis_size("ctx"))
    bits = bits[turn:] + bits[:turn]
    scatter = [scatter_step(bit) for bit in bits]
    spread = [spread_step(bit) for bit in reversed(bits)]
    return (scatter + fsdp_steps if ctx_first else fsdp_steps + scatter) + spread


def advance(chains, beside=()):
    begun = [(steps.pop(0)(values) if steps else None, steps, values) for steps, values in chains]
    received = [step[1] for step, _, _ in begun if step]
    received, beside = together(received, beside)
    after = []
    for step, steps, values in begun:
        if step:
            values = step[2](step[0], received.pop(0))
        after.append((steps, values))
    return after, beside


def fsdp_blocks(blocks):
    for bit in bits_of(lax.axis_size("fsdp")):
        blocks = [joined(k, swap(v, "fsdp", bit)) for k, v in zip(blocks[0::2], blocks[1::2])]
        yield blocks


def fsdp_selected(blocks, bit):
    up = (lax.axis_index("fsdp") & bit) != 0
    return [
        joined(jnp.where(up, high, low), swap(jnp.where(up, low, high), "fsdp", bit))
        for low, high in zip(blocks[0::2], blocks[1::2])
    ]


def side_by_side(values, rows):
    return jnp.concatenate([values[:rows], values[rows:]], axis=1)


def one_above(values, columns):
    return jnp.concatenate([values[:, :columns], values[:, columns:]], axis=0)


def dot(left, right):
    return jnp.dot(left, right, preferred_element_type=F32)


def rows_dot(left, right):
    return lax.dot_general(left, right, (((0,), (0,)), ((), ())), preferred_element_type=F32)


def back_dot(left, right):
    return lax.dot_general(left, right, (((1,), (1,)), ((), ())), preferred_element_type=F32)


def sigmoid(values):
    return 1.0 / (1.0 + jnp.exp(-values))


def softplus(values):
    small = jnp.exp(-jnp.abs(values))
    grown = 1.0 + small
    part = jnp.where(grown == 1.0, small, jnp.log(grown) * (small / jnp.maximum(grown - 1.0, 1e-30)))
    return jnp.maximum(values, 0.0) + part


def tile_cols(j):
    return slice(j * LANES, (j + 1) * LANES)


def input_kernel(scal, normed_ref, *refs, count, piece, is_upper):
    lows, highs = refs[:count], refs[count : 2 * count]
    s_ref, x_ref, conv_ref, xs_ref, proj_ref, mixed_ref = refs[2 * count :]
    depth = lows[0].shape[0]
    width = lows[0].shape[1]
    upper = is_upper(pl.program_id(0), scal)

    def mix(weights):
        mixed = dot(normed_ref[:, 0:depth], weights[0][...])
        for r in range(1, count):
            mixed = mixed + dot(normed_ref[:, r * depth : (r + 1) * depth], weights[r][...])
        mixed_ref[...] = mixed

    @pl.when(upper)
    def from_high():
        mix(highs)

    @pl.when(jnp.logical_not(upper))
    def from_low():
        mix(lows)

    x_low = mixed_ref[...].astype(BF16).reshape(2, HALO + piece, width)
    x_ref[...] = x_low
    x = x_low.astype(F32)
    head = s_ref[0:HEAD, :].astype(F32)
    conv = head[4:5] + x[:, HALO - 3 : HALO - 3 + piece] * head[0:1]
    for k in range(1, 4):
        conv = conv + x[:, HALO - 3 + k : HALO - 3 + k + piece] * head[k : k + 1]
    conv_ref[...] = conv
    xs = (conv * sigmoid(conv)).astype(BF16)
    xs_ref[...] = xs
    part = back_dot(xs.reshape(2 * piece, width), s_ref[96:192, :])

    @pl.when(pl.program_id(0) == 0)
    def first():
        proj_ref[...] = part

    @pl.when(pl.program_id(0) > 0)
    def later():
        proj_ref[...] += part


def gate_kernel(scal, normed_ref, *refs, count, piece):
    weights, (gate_ref,) = refs[:count], refs[count:]
    depth = weights[0].shape[0]
    width = weights[0].shape[1]
    own = jnp.concatenate(
        [normed_ref[HALO : HALO + piece], normed_ref[2 * HALO + piece : 2 * HALO + 2 * piece]], axis=0
    )
    gate = dot(own[:, 0:depth], weights[0][...])
    for r in range(1, count):
        gate = gate + dot(own[:, r * depth : (r + 1) * depth], weights[r][...])
    gate_ref[...] = gate.reshape(2, piece, width)


def end_kernel(
    scal, proj_ref, s_ref, xs_ref, b_ref, step_ref, end_ref, drive_ref, *, tiles, groups, rank
):
    piece = groups * 8
    width = tiles * LANES
    states = b_ref.shape[2]
    head = s_ref[0:HEAD, :].astype(F32)
    delta = proj_ref[:, 0:rank].astype(BF16)
    pre = dot(delta, s_ref[HEAD : HEAD + rank, :]) + head[5:6]
    row = lax.broadcasted_iota(jnp.int32, (piece, width), 0)
    logs = []
    for h in range(2):
        step = softplus(pre[h * piece : (h + 1) * piece])
        step = jnp.where(row < scal[1 + h], step, 0.0)
        logs.append(jnp.sum(step, axis=0, keepdims=True))
        step_ref[h] = step.reshape(groups, 8, width)
        drive_ref[h] = (step * xs_ref[h].astype(F32)).reshape(groups, 8, width)
    logs = jnp.concatenate(logs, axis=0)
    parts = [part.astype(F32) for part in three_parts(logs)]
    end_ref[2 * states : 2 * states + 8, :] = jnp.concatenate(
        parts + [jnp.zeros_like(logs)], axis=0
    ).astype(BF16)
    rate2 = -jnp.exp(s_ref[80 : 80 + states, :].astype(F32)) * LOG2E
    rates = [rate2[:, tile_cols(j)] for j in range(tiles)]

    def body(t, held):
        held = list(held)
        for s in range(8):
            for h in range(2):
                b = b_ref[h, t * 8 + s]
                for j in range(tiles):
                    step = step_ref[h, t, s : s + 1, tile_cols(j)]
                    drive = drive_ref[h, t, s : s + 1, tile_cols(j)]
                    k = h * tiles + j
                    held[k] = jnp.exp2(step * rates[j]) * held[k] + drive * b
        return tuple(held)

    zero = jnp.zeros((states, LANES), F32)
    held = lax.fori_loop(0, groups, body, (zero,) * (2 * tiles))
    for h in range(2):
        for j in range(tiles):
            end_ref[h * states : (h + 1) * states, tile_cols(j)] = held[h * tiles + j].astype(BF16)


def span_logs(ends, plan_ref, h, ctx, states):
    rows = []
    for j in range(1, ctx):
        parts = ends[j - 1][2 * states : 2 * states + 8, :].astype(F32)
        rows.append(parts[h : h + 1] + parts[2 + h : 3 + h] + parts[4 + h : 5 + h])
    logs = jnp.concatenate([jnp.zeros_like(rows[0])] + rows, axis=0)
    inside = plan_ref[h * ctx : (h + 1) * ctx, 0:ctx]
    outside = plan_ref[(2 + h) * ctx : (3 + h) * ctx, 0:1]
    return outside + lax.dot_general(
        inside, logs, (((1,), (0,)), ((), ())), precision=lax.Precision.HIGHEST, preferred_element_type=F32
    )


def diagonal_maps(proj_ref, first, states):
    rows = proj_ref.shape[0]
    k = lax.broadcasted_iota(jnp.int32, (proj_ref.shape[1], 16 * states), 0)
    n = lax.broadcasted_iota(jnp.int32, (proj_ref.shape[1], 16 * states), 1) % states
    spread = dot(proj_ref[...].astype(BF16), (k == n + first).astype(F32).astype(BF16))
    row = lax.broadcasted_iota(jnp.int32, (rows, 16 * states), 0) % 16
    col = lax.broadcasted_iota(jnp.int32, (rows, 16 * states), 1) // states
    return jnp.where(row == col, spread, 0.0).astype(BF16)


def carried(ends, logs, rate2, h, ctx, states, cols):
    value = jnp.zeros((states, LANES), F32)
    for j in range(1, ctx):
        decay = jnp.exp2(rate2 * logs[j : j + 1, cols])
        value = value + decay * ends[j - 1][h * states : (h + 1) * states, cols].astype(F32)
    return value


def forward_kernel(scal, *refs, tiles, groups, ctx, features):
    ends = refs[: ctx - 1]
    plan_ref, s_ref, step_ref, xs_ref, gate_ref, b_ref, proj_ref, weight_ref = refs[ctx - 1 : ctx + 7]
    rest = refs[ctx + 7 :]
    scale_ref, tokens_ref, teacher_ref = rest[:3]
    ssm_ref, branch_ref, hidden_ref, start_ref, out_ref, gout_ref, dout_ref, square_ref = rest[3:11]
    drive_ref, read_ref, odd_ref, even_ref, acc_ref, cdiag_ref = rest[11:]
    piece = groups * 8
    width = tiles * LANES
    states = b_ref.shape[2]
    i = pl.program_id(0)
    head = s_ref[0:HEAD, :].astype(F32)

    @pl.when(i == 0)
    def maps():
        values = diagonal_maps(proj_ref, proj_ref.shape[1] - states, states)
        cdiag_ref[...] = values.reshape(cdiag_ref.shape)

    for h in range(2):
        drive_ref[h] = step_ref[h] * xs_ref[h].astype(F32).reshape(groups, 8, width)
    rate2 = -jnp.exp(s_ref[80 : 80 + states, :].astype(F32)) * LOG2E
    rates = [rate2[:, tile_cols(j)] for j in range(tiles)]
    held = []
    for h in range(2):
        logs = span_logs(ends, plan_ref, h, ctx, states)
        for j in range(tiles):
            held.append(carried(ends, logs, rates[j], h, ctx, states, tile_cols(j)))
            start_ref[h, :, tile_cols(j)] = held[-1]

    def scan(t, held, keep_ref):
        held = list(held)
        for s in range(16):
            p = t * 16 + s
            for h in range(2):
                b = b_ref[h, p]
                for j in range(tiles):
                    cols = tile_cols(j)
                    step = step_ref[h, t * 2 + s // 8, s % 8 : s % 8 + 1, cols]
                    drive = drive_ref[h, t * 2 + s // 8, s % 8 : s % 8 + 1, cols]
                    k = h * tiles + j
                    held[k] = jnp.exp2(step * rates[j]) * held[k] + drive * b
                    low = held[k].astype(BF16)
                    hidden_ref[j, h, p] = low
                    keep_ref[h, j, s * states : (s + 1) * states, :] = low
        return tuple(held)

    def read(t, keep_ref):
        for h in range(2):
            for j in range(tiles):
                out = dot(cdiag_ref[h, t], keep_ref[h, j])
                read_ref[h, t * 2, :, tile_cols(j)] = out[0:8]
                read_ref[h, t * 2 + 1, :, tile_cols(j)] = out[8:16]

    def body(k, held):
        t = 2 * k + 1
        read(t - 1, even_ref)
        held = scan(t, held, odd_ref)
        read(t, odd_ref)
        return scan(t + 1, held, even_ref)

    blocks = groups // 2
    held = scan(0, held, even_ref)
    held = lax.fori_loop(0, blocks // 2 - 1, body, held)
    read(blocks - 2, even_ref)
    scan(blocks - 1, held, odd_ref)
    read(blocks - 1, odd_ref)
    branches = []
    for h in range(2):
        ssm = read_ref[h].reshape(piece, width) + head[6:7] * xs_ref[h].astype(F32)
        ssm_ref[h] = ssm
        gate = gate_ref[h]
        branches.append((ssm * (gate * sigmoid(gate))).astype(BF16))
        branch_ref[h] = branches[-1]
    part = dot(jnp.concatenate(branches, axis=0), weight_ref[...])

    @pl.when(i == 0)
    def first():
        acc_ref[...] = part

    @pl.when(i > 0)
    def later():
        acc_ref[...] += part

    @pl.when(i == pl.num_programs(0) - 1)
    def last():
        row = lax.broadcasted_iota(jnp.int32, (piece, features), 0)
        square = jnp.zeros((8, features), F32)
        for h in range(2):
            rows = slice(h * piece, (h + 1) * piece)
            block_out = tokens_ref[rows, :].astype(F32) + acc_ref[rows, :]
            out_ref[rows, :] = block_out.astype(BF16)
            error = jnp.where(row < scal[1 + h], block_out - teacher_ref[rows, :].astype(F32), 0.0)
            square = square + jnp.sum((error * error).reshape(groups, 8, features), axis=0)
            g_out = error * (2.0 * scale_ref[0, 0])
            gout_ref[rows, :] = g_out
            dout_ref[rows, :] = g_out.astype(BF16)
        square_ref[...] = square


def first_grad_kernel(
    scal, dout_ref, weight_ref, s_ref, step_ref, xs_ref, gate_ref, ssm_ref, c_ref,
    dssm_ref, dgate_ref, skip_ref, grad_ref, *, tiles, groups
):
    piece = groups * 8
    width = tiles * LANES
    states = c_ref.shape[2]
    d_branch = back_dot(dout_ref[...], weight_ref[...])
    skip = jnp.zeros((1, width), F32)
    for h in range(2):
        grad = d_branch[h * piece : (h + 1) * piece]
        gate = gate_ref[h]
        sig = sigmoid(gate)
        d_ssm = grad * (gate * sig)
        dgate_ref[h] = (grad * ssm_ref[h] * (sig * (1.0 + gate * (1.0 - sig)))).astype(BF16)
        skip = skip + jnp.sum(d_ssm * xs_ref[h].astype(F32), axis=0, keepdims=True)
        dssm_ref[h] = d_ssm.reshape(groups, 8, width)
    skip_ref[...] = skip
    rate2 = -jnp.exp(s_ref[80 : 80 + states, :].astype(F32)) * LOG2E
    rates = [rate2[:, tile_cols(j)] for j in range(tiles)]

    def body(i, held):
        held = list(held)
        t = groups - 1 - i
        for s in range(7, -1, -1):
            for h in range(2):
                c = c_ref[h, t * 8 + s]
                for j in range(tiles):
                    step = step_ref[h, t, s : s + 1, tile_cols(j)]
                    dssm = dssm_ref[h, t, s : s + 1, tile_cols(j)]
                    k = h * tiles + j
                    held[k] = jnp.exp2(step * rates[j]) * (held[k] + dssm * c)
        return tuple(held)

    zero = jnp.zeros((states, LANES), F32)
    held = lax.fori_loop(0, groups, body, (zero,) * (2 * tiles))
    for h in range(2):
        for j in range(tiles):
            grad_ref[h * states : (h + 1) * states, tile_cols(j)] = held[h * tiles + j].astype(BF16)


def out_grad_kernel(even_ref, odd_ref, dout_ref, keep_ref, send_ref):
    keep_ref[0] = rows_dot(even_ref[...], dout_ref[...]).astype(BF16)
    send_ref[0] = rows_dot(odd_ref[...], dout_ref[...]).astype(BF16)


def gate_grad_kernel(scal, normed_ref, dgate_ref, *refs, count, piece):
    weights, (keep_ref, send_ref, dnormed_ref) = refs[:count], refs[count:]
    depth = weights[0].shape[0]
    width = weights[0].shape[1]
    own = jnp.concatenate(
        [normed_ref[HALO : HALO + piece], normed_ref[2 * HALO + piece : 2 * HALO + 2 * piece]], axis=0
    )
    d_gate = dgate_ref[...].reshape(2 * piece, width)

    @pl.when(pl.program_id(0) == 0)
    def clear():
        dnormed_ref[...] = jnp.zeros_like(dnormed_ref)

    for r in range(count):
        cols = slice(r * depth, (r + 1) * depth)
        target = send_ref if r % 2 else keep_ref
        target[r // 2] = rows_dot(own[:, cols], d_gate).astype(BF16)
        back = back_dot(d_gate, weights[r][...])
        for h in range(2):
            rows = slice(h * (HALO + piece) + HALO, (h + 1) * (HALO + piece))
            dnormed_ref[rows, cols] += back[h * piece : (h + 1) * piece]


def backward_kernel(scal, *refs, tiles, groups, ctx, rank):
    grads = refs[: ctx - 1]
    ends = refs[ctx - 1 : 2 * ctx - 2]
    (
        plan_ref, proj_ref, s_ref, step_ref, xs_ref, c_ref, start_ref, dssm_ref, hidden_ref,
        dxs_ref, small_ref, ddelta_ref, db_ref, dc_ref,
        adj_ref, dstep_ref, dbs_ref, dcs_ref, adj_odd, adj_even, term_odd, term_even, bdiag_ref,
    ) = refs[2 * ctx - 2 :]
    piece = groups * 8
    width = tiles * LANES
    states = c_ref.shape[2]
    blocks = groups // 2
    i = pl.program_id(0)
    head = s_ref[0:HEAD, :].astype(F32)

    @pl.when(i == 0)
    def clear():
        dbs_ref[...] = jnp.zeros_like(dbs_ref)
        dcs_ref[...] = jnp.zeros_like(dcs_ref)
        bdiag_ref[...] = diagonal_maps(proj_ref, rank, states).reshape(bdiag_ref.shape)
        ddelta_ref[...] = jnp.zeros_like(ddelta_ref)

    rate = -jnp.exp(s_ref[80 : 80 + states, :].astype(F32))
    rates = [rate[:, tile_cols(j)] for j in range(tiles)]
    rates2 = [values * LOG2E for values in rates]
    row16 = lax.broadcasted_iota(jnp.int32, (16, 16 * states), 0)
    col16 = lax.broadcasted_iota(jnp.int32, (16, 16 * states), 1)
    same = (col16 // states == row16).astype(F32)
    same_low = same.astype(BF16)

    def scan(t, first, later, sums, adj_keep, term_keep):
        for h in range(2):
            for s in range(15, -1, -1):
                p = t * 16 + s
                c = c_ref[h, p]
                for j in range(tiles):
                    cols = tile_cols(j)
                    step = step_ref[h, t * 2 + s // 8, s % 8 : s % 8 + 1, cols]
                    dssm = dssm_ref[h, t * 2 + s // 8, s % 8 : s % 8 + 1, cols]
                    k = h * tiles + j
                    if first and s == 0:
                        before = start_ref[h, :, cols]
                    else:
                        before = hidden_ref[j, h, p - 1].astype(F32)
                    adjoint = dssm * c + later[k]
                    later[k] = jnp.exp2(step * rates2[j]) * adjoint
                    term = later[k] * before
                    sums[j] = sums[j] + term * step
                    place = slice(s * states, (s + 1) * states)
                    adj_keep[h, j, place, :] = adjoint.astype(BF16)
                    term_keep[h, j, place, :] = (term * rates[j]).astype(BF16)

    def products(t, adj_keep, term_keep):
        for h in range(2):
            db = dc = None
            for j in range(tiles):
                cols = tile_cols(j)
                adjoint = adj_keep[h, j]
                out = dot(bdiag_ref[h, t], adjoint)
                adj_ref[h, t * 2, :, cols] = out[0:8]
                adj_ref[h, t * 2 + 1, :, cols] = out[8:16]
                out = dot(same_low, term_keep[h, j])
                dstep_ref[h, t * 2, :, cols] = out[0:8]
                dstep_ref[h, t * 2 + 1, :, cols] = out[8:16]
                step = step_ref[h, pl.ds(t * 2, 2), :, cols].reshape(16, LANES)
                dssm = dssm_ref[h, pl.ds(t * 2, 2), :, cols].reshape(16, LANES)
                drive = (step * xs_ref[h, pl.ds(t * 16, 16), cols].astype(F32)).astype(BF16)
                hidden = hidden_ref[j, h, pl.ds(t * 16, 16)].reshape(16 * states, LANES)
                db_now = back_dot(drive, adjoint)
                dc_now = back_dot(dssm.astype(BF16), hidden)
                db = db_now if db is None else db + db_now
                dc = dc_now if dc is None else dc + dc_now
            dbs_ref[h, t] += db
            dcs_ref[h, t] += dc

    def body(k, both):
        later, sums = list(both[: 2 * tiles]), list(both[2 * tiles :])
        t = blocks - 2 - 2 * k
        products(t + 1, adj_odd, term_odd)
        scan(t, False, later, sums, adj_even, term_even)
        products(t, adj_even, term_even)
        scan(t - 1, False, later, sums, adj_odd, term_odd)
        return tuple(later + sums)

    later = []
    for h in range(2):
        logs = span_logs(ends, plan_ref, h, ctx, states)
        for j in range(tiles):
            later.append(carried(grads, logs, rates2[j], h, ctx, states, tile_cols(j)))
    sums = [jnp.zeros((states, LANES), F32)] * tiles
    scan(blocks - 1, False, later, sums, adj_odd, term_odd)
    both = lax.fori_loop(0, blocks // 2 - 1, body, tuple(later + sums))
    later, sums = list(both[: 2 * tiles]), list(both[2 * tiles :])
    products(1, adj_odd, term_odd)
    scan(0, True, later, sums, adj_even, term_even)
    products(0, adj_even, term_even)
    for j in range(tiles):
        small_ref[rank : rank + states, tile_cols(j)] = sums[j] * rates[j]
    delta = proj_ref[:, 0:rank].astype(BF16)
    pre = dot(delta, s_ref[HEAD : HEAD + rank, :]) + head[5:6]
    row = lax.broadcasted_iota(jnp.int32, (piece, width), 0)
    lows = []
    bias = jnp.zeros((1, width), F32)
    for h in range(2):
        xs = xs_ref[h].astype(F32)
        adj = adj_ref[h].reshape(piece, width)
        d_step = xs * adj + dstep_ref[h].reshape(piece, width)
        d_pre = jnp.where(row < scal[1 + h], d_step * sigmoid(pre[h * piece : (h + 1) * piece]), 0.0)
        bias = bias + jnp.sum(d_pre, axis=0, keepdims=True)
        lows.append(d_pre.astype(BF16))
        dxs_ref[h] = head[6:7] * dssm_ref[h].reshape(piece, width) + step_ref[h].reshape(piece, width) * adj
    small_ref[rank + states : rank + states + 8, :] = jnp.broadcast_to(bias, (8, width))
    low = jnp.concatenate(lows, axis=0)
    small_ref[0:rank, :] = rows_dot(delta, low)
    ddelta_ref[...] += back_dot(low, s_ref[HEAD : HEAD + rank, :])

    @pl.when(i == pl.num_programs(0) - 1)
    def last():
        for h in range(2):
            for t in range(blocks):
                db_ref[h, t : t + 1, :] = jnp.sum(dbs_ref[h, t] * same, axis=0, keepdims=True)
                dc_ref[h, t : t + 1, :] = jnp.sum(dcs_ref[h, t] * same, axis=0, keepdims=True)


def tail_kernel(
    scal, dproj_ref, s_ref, dlow_ref, dhigh_ref, conv_ref, x_ref, xs_ref, normed_ref, before_ref, *refs,
    count, piece, is_upper
):
    weights, (small_ref, keep_ref, send_ref, dnormed_ref, pad_ref) = refs[:count], refs[count:]
    depth = weights[0].shape[0]
    width = weights[0].shape[1]
    ext = HALO + piece

    @pl.when(pl.program_id(0) == 0)
    def clear():
        dnormed_ref[...] = before_ref[...]
        for h in range(2):
            pad_ref[h, 0:HALO, :] = jnp.zeros((HALO, width), F32)
            pad_ref[h, ext : ext + 8, :] = jnp.zeros((8, width), F32)

    upper = is_upper(pl.program_id(0), scal)
    head = s_ref[0:HEAD, :].astype(F32)
    small_ref[8:104, :] = rows_dot(dproj_ref[...], xs_ref[...].reshape(2 * piece, width))
    d_xs = dot(dproj_ref[...], s_ref[96:192, :])
    taps = [jnp.zeros((1, width), F32) for _ in range(5)]
    lows = []
    for h in range(2):
        conv = conv_ref[h]
        sig = sigmoid(conv)
        dxs = jnp.where(upper, dhigh_ref[h], dlow_ref[h])
        d_conv = (dxs + d_xs[h * piece : (h + 1) * piece]) * (sig * (1.0 + conv * (1.0 - sig)))
        pad_ref[h, HALO:ext, :] = d_conv
        x = x_ref[h].astype(F32)
        for k in range(4):
            rows = slice(HALO - 3 + k, HALO - 3 + k + piece)
            taps[k] = taps[k] + jnp.sum(d_conv * x[rows], axis=0, keepdims=True)
        taps[4] = taps[4] + jnp.sum(d_conv, axis=0, keepdims=True)
        d_x = head[3:4] * pad_ref[h, 0:ext, :]
        for k in range(3):
            d_x = d_x + head[k : k + 1] * pad_ref[h, 3 - k : 3 - k + ext, :]
        lows.append(d_x.astype(BF16))
    small_ref[0:8, :] = jnp.concatenate(taps + [jnp.zeros((3, width), F32)], axis=0)
    low = jnp.concatenate(lows, axis=0)
    for r in range(count):
        cols = slice(r * depth, (r + 1) * depth)
        target = send_ref if r % 2 else keep_ref
        target[r // 2] = rows_dot(normed_ref[:, cols], low).astype(BF16)
        dnormed_ref[:, cols] += back_dot(low, weights[r][...])


def shape(dims, dtype=F32):
    return jax.ShapeDtypeStruct(dims, dtype)


def call(kernel, name, grid, scal, args, in_specs, out_specs, out_shape, scratch, flops, exps=0):
    size = sum(a.size * a.dtype.itemsize for a in args) + sum(
        s.size * s.dtype.itemsize for s in out_shape
    )
    return pl.pallas_call(
        kernel,
        grid_spec=pltpu.PrefetchScalarGridSpec(
            num_scalar_prefetch=1,
            grid=(grid,),
            in_specs=in_specs,
            out_specs=out_specs,
            scratch_shapes=scratch,
        ),
        out_shape=out_shape,
        name=name,
        compiler_params=pltpu.CompilerParams(vmem_limit_bytes=LIMITS[name] * 2**20),
        cost_estimate=pl.CostEstimate(flops=flops, bytes_accessed=size, transcendentals=exps),
    )(scal, *args)


def whole_spec(dims):
    return pl.BlockSpec(dims, lambda i, scal: (0,) * len(dims))


def local(
    tokens,
    teacher,
    lengths,
    pair_owner,
    norm_gain,
    in_proj,
    conv_weight,
    conv_bias,
    x_proj,
    dt_proj,
    dt_bias,
    a_log,
    skip_scale,
    out_proj,
):
    ctx = lax.axis_size("ctx")
    fsdp = lax.axis_size("fsdp")
    me_ctx = lax.axis_index("ctx")
    me_fsdp = lax.axis_index("fsdp")
    piece = tokens.shape[1] // 2
    features = tokens.shape[2]
    width = in_proj.shape[1] // 2
    rank = dt_proj.shape[0]
    states = a_log.shape[0]
    groups = piece // 8
    ext = HALO + piece
    depth = features // fsdp
    part = width // fsdp
    rows_all = 2 * piece
    elements = rows_all * states * width

    relative = jnp.arange(ctx, dtype=jnp.int32) ^ me_ctx
    pair_of = jnp.sum(
        jnp.arange(ctx, dtype=jnp.int32)[None, :]
        * (pair_owner[None, :] == relative[:, None]).astype(jnp.int32),
        axis=1,
    )
    places = jnp.stack([pair_of, ctx - 1 - pair_of])
    pair_id = pair_of[0]
    own = places[:, 0]
    limits = jnp.clip(lengths[0] - own * piece, 0, piece)
    scal = jnp.concatenate([me_fsdp[None], limits]).astype(jnp.int32)
    between = (places[:, :, None] < places[:, None, :]) & (
        places[:, None, :] < own[:, None, None]
    )
    between_back = (places[:, :, None] > places[:, None, :]) & (
        places[:, None, :] > own[:, None, None]
    )
    before = places < own[:, None]
    behind = places > own[:, None]
    has_before = jnp.stack([pair_id > 0, pair_id < ctx - 1])
    has_after = jnp.stack([pair_id < ctx - 1, pair_id > 0])
    lower_owner = pair_owner[jnp.maximum(pair_id - 1, 0)]
    upper_owner = pair_owner[jnp.minimum(pair_id + 1, ctx - 1)]
    lower, upper = lower_owner ^ me_ctx, upper_owner ^ me_ctx

    def plan_of(inside, wanted):
        inside = jnp.pad(inside.astype(F32), ((0, 0), (0, 0), (0, LANES - ctx)))
        outside = jnp.broadcast_to(jnp.where(wanted, 0.0, 1e30)[..., None], (2, ctx, LANES))
        return jnp.concatenate([inside, outside], axis=0).reshape(4 * ctx, LANES).astype(F32)

    plan_before = plan_of(between, before)
    plan_behind = plan_of(between_back, behind)

    def to_blocks(values, size):
        axis = values.ndim - 1
        return jnp.concatenate(
            [
                lax.dynamic_slice_in_dim(values, (me_fsdp ^ r) * size, size, axis=axis)
                for r in range(fsdp)
            ],
            axis=axis,
        )

    own_rows = tokens[0]
    valid_slots = jnp.minimum(lengths[0], 2 * ctx * piece)
    coded = jnp.concatenate([valid_slots // 128, valid_slots % 128]).astype(BF16)[None]
    rows_head = jnp.concatenate(
        [
            conv_weight,
            conv_bias[None],
            dt_bias[None],
            skip_scale[None],
            jnp.pad(norm_gain, (0, part - depth))[None],
            jnp.pad(coded, ((0, 0), (0, part - 4))),
            jnp.zeros((HEAD - 9, part), BF16),
            dt_proj,
            a_log,
            x_proj.T,
        ],
        axis=0,
    )
    half = width // 2
    to_send = in_proj[:, :half]
    x_far = [to_send] + [swap(to_send, "fsdp", bit) for bit in range(2, fsdp, 2)]
    last_rows = to_blocks(own_rows.reshape(2, piece, features)[:, piece - 3 :], depth)
    last_rows = jnp.broadcast_to(last_rows[None], (ctx, 2, 3, features))
    token_rel = to_blocks(own_rows, depth).reshape(2, piece, features)
    tails = lax.all_to_all(last_rows, "ctx", 0, 0)
    x_far, second, rows_head, tails, token_rel, scal, plan_before, plan_behind = together(
        x_far, in_proj[:, half:width], rows_head, tails, token_rel, scal, plan_before, plan_behind
    )
    x_first = [block for own in x_far for block in (own, swap(own, "fsdp", 1))]
    small_blocks = gather_fsdp(rows_head)
    small = jnp.concatenate(small_blocks, axis=1)
    gain = jnp.concatenate([block[7, :depth] for block in small_blocks]).astype(F32)
    x_second = gather_fsdp(second)

    before_rows = jnp.stack([tails[lower_owner, 0], tails[upper_owner, 1]])
    before_rows = jnp.where(has_before[:, None, None], before_rows, jnp.zeros_like(before_rows))
    rows_ext = jnp.concatenate(
        [jnp.zeros((2, HALO - 3, features), BF16), before_rows, token_rel], axis=1
    ).astype(F32)
    inv_rms = lax.rsqrt(jnp.mean(rows_ext * rows_ext, axis=2, keepdims=True) + EPSILON)
    normed = (rows_ext * inv_rms * gain).astype(BF16).reshape(2 * ext, features)

    codes = jnp.stack([block[8, :4] for block in small_blocks]).astype(F32)
    count = jnp.sum(codes[:, 0:2] * 128.0 + codes[:, 2:4])
    scale = ((fsdp * rows_all * ctx) / count).reshape(1, 1)

    def cols_at(block):
        per = part // block
        return lambda i, scal: (0, (scal[0] ^ (i // per)) * per + i % per)

    def spec_small(block, offset=0):
        return pl.BlockSpec((small.shape[0], block), lambda i, scal: (0, i + offset))

    def spec_rows(block, offset=0):
        return pl.BlockSpec((2, piece, block), lambda i, scal: (0, 0, i + offset))

    def spec_groups(block):
        return pl.BlockSpec((2, groups, 8, block), lambda i, scal: (0, 0, 0, i))

    cb = min(256, part)
    steps = width // cb
    weight_specs = [pl.BlockSpec((depth, cb), cols_at(cb)) for _ in range(fsdp)]
    half_blocks = half // cb

    def upper_place(i, scal):
        return cols_at(cb)(i, scal)[1] >= half_blocks

    low_spec = pl.BlockSpec(
        (depth, cb), lambda i, scal: (0, jnp.minimum(cols_at(cb)(i, scal)[1], half_blocks - 1))
    )
    high_spec = pl.BlockSpec(
        (depth, cb), lambda i, scal: (0, jnp.maximum(cols_at(cb)(i, scal)[1] - half_blocks, 0))
    )
    x_ext, conv, xs, proj = call(
        functools.partial(input_kernel, count=fsdp, piece=piece, is_upper=upper_place),
        "inputs", steps, scal, (normed, *x_first, *x_second, small),
        [whole_spec((2 * ext, features)), *([low_spec] * fsdp), *([high_spec] * fsdp), spec_small(cb)],
        [
            pl.BlockSpec((2, ext, cb), lambda i, scal: (0, 0, i)),
            spec_rows(cb),
            spec_rows(cb),
            whole_spec((rows_all, rank + 2 * states)),
        ],
        [
            shape((2, ext, width), BF16),
            shape((2, piece, width)),
            shape((2, piece, width), BF16),
            shape((rows_all, rank + 2 * states)),
        ],
        [pltpu.VMEM((2 * ext, cb), F32)], 2 * rows_all * features * width,
    )
    gate_first = after(in_proj[:, width:], x_second[fsdp // 2])
    gate_far = [gate_first] + [swap(gate_first, "fsdp", bit) for bit in range(2, fsdp, 2)]
    gate_far, proj = together(gate_far, proj)
    gate_blocks = [block for own in gate_far for block in (own, swap(own, "fsdp", 1))]
    out_first = after(out_proj, gate_far[-1])
    out_far = [out_first] + [swap(out_first, "fsdp", bit) for bit in range(2, fsdp, 2)]
    wide_dims = (2, piece, states, LANES)
    maps = proj[:, rank:].reshape(2, piece, 2 * states, 1)
    b_wide = jnp.broadcast_to(maps[:, :, :states], wide_dims)

    tiles = 4
    block = tiles * LANES
    per_half = half // block
    group_spec = spec_groups(block)
    state_row = pl.BlockSpec((2 * states, block), lambda i, scal: (0, i))
    sent_row = pl.BlockSpec((2 * states + 8, block), lambda i, scal: (0, i))
    plan_spec = whole_spec((4 * ctx, LANES))
    row_spec = whole_spec((rows_all, features))
    wide_spec = whole_spec(wide_dims)
    diag_space = pltpu.VMEM((2, piece // 16, 16, 16 * states), BF16)
    hidden_spec = pl.BlockSpec((tiles, 2, piece, states, LANES), lambda i, scal: (i, 0, 0, 0, 0))
    start_spec = pl.BlockSpec((2, states, block), lambda i, scal: (0, 0, i))
    keep_spaces = [pltpu.VMEM((2, tiles, 16 * states, LANES), BF16)]
    group_space = pltpu.VMEM((2, groups, 8, block), F32)

    step, sent = call(
        functools.partial(end_kernel, tiles=tiles, groups=groups, rank=rank),
        "end_states", width // block, scal, (proj, small, xs, b_wide),
        [whole_spec(proj.shape), spec_small(block), spec_rows(block), wide_spec],
        [group_spec, pl.BlockSpec((2 * states + 8, block), lambda i, scal: (0, i))],
        [shape((2, groups, 8, width)), shape((2 * states + 8, width), BF16)],
        [group_space], 5 * elements, elements,
    )

    far = gather_far(sent)
    (gate,) = call(
        functools.partial(gate_kernel, count=fsdp, piece=piece),
        "gates", steps, scal, (normed, *gate_blocks),
        [whole_spec((2 * ext, features)), *weight_specs], [spec_rows(cb)],
        [shape((2, piece, width))], [], 2 * rows_all * features * width,
    )
    c_wide = jnp.broadcast_to(maps[:, :, states:], wide_dims)
    far, gate, out_far = together(far, gate, out_far)
    near, c_wide = gather_near(far, c_wide)
    out_blocks = [block for own in out_far for block in (own, swap(own, "fsdp", 1))]
    weight_out = jnp.concatenate(out_blocks, axis=0)
    near, weight_out = together(near, weight_out)
    ssm, branch, hidden, starts, out_low, g_out, d_out, squares = call(
        functools.partial(forward_kernel, tiles=tiles, groups=groups, ctx=ctx, features=features),
        "forward_states", width // block, scal,
        (*near[1:], plan_before, small, step, xs, gate, b_wide, proj, weight_out,
         scale, own_rows, teacher[0]),
        [
            *([sent_row] * (ctx - 1)), plan_spec, spec_small(block), group_spec, spec_rows(block),
            spec_rows(block), wide_spec, whole_spec(proj.shape),
            pl.BlockSpec((block, features), lambda i, scal: (i, 0)),
            pl.BlockSpec(memory_space=pltpu.SMEM), row_spec, row_spec,
        ],
        [
            spec_rows(block), spec_rows(block), hidden_spec, start_spec, row_spec, row_spec, row_spec,
            whole_spec((8, features)),
        ],
        [
            shape((2, piece, width)),
            shape((2, piece, width), BF16),
            shape((width // LANES, 2, piece, states, LANES), BF16),
            shape((2, states, width)),
            shape((rows_all, features), BF16),
            shape((rows_all, features)),
            shape((rows_all, features), BF16),
            shape((8, features)),
        ],
        [group_space] * 2 + keep_spaces * 2 + [pltpu.VMEM((rows_all, features), F32), diag_space],
        10 * elements, elements,
    )
    d_ssm, d_gate, grad_skip, grads_first = call(
        functools.partial(first_grad_kernel, tiles=tiles, groups=groups),
        "first_grads", width // block, scal,
        (d_out, weight_out, small, step, xs, gate, ssm, c_wide),
        [
            row_spec, pl.BlockSpec((block, features), lambda i, scal: (i, 0)), spec_small(block),
            group_spec, spec_rows(block), spec_rows(block), spec_rows(block), wide_spec,
        ],
        [group_spec, spec_rows(block), pl.BlockSpec((1, block), lambda i, scal: (0, i)), state_row],
        [
            shape((2, groups, 8, width)),
            shape((2, piece, width), BF16),
            shape((1, width)),
            shape((2 * states, width), BF16),
        ],
        [], 6 * elements, elements,
    )
    back_far = gather_far(grads_first)

    pairs = fsdp // 2
    pair_spec = pl.BlockSpec((pairs, depth, cb), lambda i, scal: (0, 0, i))
    pair_at = pl.BlockSpec((pairs, depth, cb), lambda i, scal: (0, 0, cols_at(cb)(i, scal)[1]))
    keep_gate, send_gate, d_normed_gate = call(
        functools.partial(gate_grad_kernel, count=fsdp, piece=piece),
        "gate_grads", steps, scal, (normed, d_gate, *gate_blocks),
        [whole_spec((2 * ext, features)), spec_rows(cb), *weight_specs],
        [pair_at, pair_at, whole_spec((2 * ext, features))],
        [shape((pairs, depth, width), BF16)] * 2 + [shape((2 * ext, features))],
        [], 4 * rows_all * features * width,
    )
    subs = part // cb
    branch_rows = branch.reshape(rows_all, width)
    keep_out, send_out = pl.pallas_call(
        out_grad_kernel,
        grid=(pairs, subs),
        in_specs=[
            pl.BlockSpec((rows_all, cb), lambda k, s: (0, 2 * k * subs + s)),
            pl.BlockSpec((rows_all, cb), lambda k, s: (0, (2 * k + 1) * subs + s)),
            pl.BlockSpec((rows_all, features), lambda k, s: (0, 0)),
        ],
        out_specs=[pl.BlockSpec((1, cb, features), lambda k, s: (k, s, 0))] * 2,
        out_shape=[shape((pairs, part, features), BF16)] * 2,
        name="out_grads",
        compiler_params=pltpu.CompilerParams(vmem_limit_bytes=VMEM_LIMIT),
        cost_estimate=pl.CostEstimate(
            flops=2 * rows_all * width * features, bytes_accessed=9 * 2**20, transcendentals=0
        ),
    )(branch_rows, branch_rows, d_out)
    back_far, keep_gate, send_gate, keep_out, send_out = together(
        back_far, keep_gate, send_gate, keep_out, send_out
    )
    back_near, _ = gather_near(back_far)
    core_gate = joined(keep_gate, swap(send_gate, "fsdp", 1))
    core_out = joined(keep_out, swap(send_out, "fsdp", 1))
    back_near, core_out, core_gate = together(back_near, core_out, core_gate)
    chains = [(reduce_steps(False), core_out), (reduce_steps(True, 1), core_gate)]

    def backward(c):
        def at(i):
            return i + c * per_half

        return call(
            functools.partial(backward_kernel, tiles=tiles, groups=groups, ctx=ctx, rank=rank),
            "backward_states", per_half, scal,
            (*back_near[1:], *near[1:], plan_behind, proj, small, step, xs, c_wide, starts, d_ssm, hidden),
            [
                *([pl.BlockSpec((2 * states, block), lambda i, scal: (0, at(i)))] * (ctx - 1)),
                *([pl.BlockSpec((2 * states + 8, block), lambda i, scal: (0, at(i)))] * (ctx - 1)),
                plan_spec,
                whole_spec(proj.shape), spec_small(block, c * per_half),
                pl.BlockSpec((2, groups, 8, block), lambda i, scal: (0, 0, 0, at(i))),
                spec_rows(block, c * per_half), wide_spec,
                pl.BlockSpec((2, states, block), lambda i, scal: (0, 0, at(i))),
                pl.BlockSpec((2, groups, 8, block), lambda i, scal: (0, 0, 0, at(i))),
                pl.BlockSpec((tiles, 2, piece, states, LANES), lambda i, scal: (at(i), 0, 0, 0, 0)),
            ],
            [
                spec_rows(block), pl.BlockSpec((rank + states + 8, block), lambda i, scal: (0, i)),
                whole_spec((rows_all, rank)),
                whole_spec((2, piece // 16, 16 * states)), whole_spec((2, piece // 16, 16 * states)),
            ],
            [
                shape((2, piece, half)),
                shape((rank + states + 8, half)),
                shape((rows_all, rank)),
                shape((2, piece // 16, 16 * states)),
                shape((2, piece // 16, 16 * states)),
            ],
            [group_space] * 2 + [pltpu.VMEM((2, piece // 16, 16, 16 * states), F32)] * 2 + keep_spaces * 4
            + [diag_space],
            16 * elements // 2, elements // 2,
        )

    chains, back_first = advance(chains, backward(0))
    step, _ = together(step, [values for _, values in chains])
    chains, back_second = advance(chains, backward(1))

    def small_part(c, back):
        rows = jnp.concatenate(
            [back[1], grad_skip[:, c * half : (c + 1) * half], jnp.zeros((7, half), F32)], axis=0
        ).astype(BF16)
        return [rows[:, k * part : (k + 1) * part] for k in range(fsdp // 2)]

    d_proj = jnp.concatenate(
        [
            back_first[2] + back_second[2],
            (back_first[3] + back_second[3]).reshape(rows_all, states),
            (back_first[4] + back_second[4]).reshape(rows_all, states),
        ],
        axis=1,
    ).astype(BF16)
    half_steps = steps // 2

    def tail(c, d_proj, d_before):
        base = c * half_steps

        def place(i, scal):
            return cols_at(cb)(i + base, scal)[1]

        def at_rows(dims):
            return pl.BlockSpec((2, dims, cb), lambda i, scal: (0, 0, place(i, scal)))

        return call(
            functools.partial(
                tail_kernel, count=fsdp, piece=piece,
                is_upper=lambda i, scal: place(i, scal) >= half_blocks,
            ),
            "tail_grads", half_steps, scal,
            (d_proj, small, back_first[0], back_second[0], conv, x_ext, xs, normed, d_before,
             *(x_second if c else x_first)),
            [
                whole_spec(d_proj.shape),
                pl.BlockSpec((small.shape[0], cb), lambda i, scal: (0, place(i, scal))),
                pl.BlockSpec(
                    (2, piece, cb), lambda i, scal: (0, 0, jnp.minimum(place(i, scal), half_blocks - 1))
                ),
                pl.BlockSpec(
                    (2, piece, cb), lambda i, scal: (0, 0, jnp.maximum(place(i, scal) - half_blocks, 0))
                ),
                at_rows(piece), at_rows(ext), at_rows(piece),
                whole_spec((2 * ext, features)), whole_spec((2 * ext, features)),
                *([pl.BlockSpec((depth, cb), lambda i, scal: (0, i))] * fsdp),
            ],
            [
                pl.BlockSpec((104, cb), lambda i, scal: (0, i)),
                pair_spec, pair_spec, whole_spec((2 * ext, features)),
            ],
            [
                shape((104, half)),
                shape((pairs, depth, half), BF16),
                shape((pairs, depth, half), BF16),
                shape((2 * ext, features)),
            ],
            [pltpu.VMEM((2, ext + 8, cb), F32)],
            4 * rows_all * features * half,
        )

    d_before = d_normed_gate
    d_proj, d_before, _ = together(d_proj, d_before, [values for _, values in chains])
    chains, tail_first = advance(chains, tail(0, d_proj, d_before))
    got_ahead = swap(tail_first[2], "fsdp", 1)
    small_now = small_part(0, back_first) + small_part(1, back_second)
    for small_now in fsdp_blocks(small_now):
        pass
    d_proj, _ = together(d_proj, [values for _, values in chains])
    chains, (tail_second, got_ahead, small_now) = advance(
        chains, (tail(1, d_proj, tail_first[3]), got_ahead, small_now)
    )
    ahead = joined(tail_first[1], got_ahead)
    def halo_start(d_ext, squares):
        d_normed = d_ext.reshape(2, ext, features)
        unit = rows_ext * inv_rms
        grad_gain = jnp.sum(d_normed[:, HALO - 3 :] * unit[:, HALO - 3 :], axis=(0, 1))
        square = jnp.pad(jnp.stack(three_parts(jnp.sum(squares))), (0, features - 3))
        halo_rows = d_normed[:, HALO - 3 : HALO].reshape(6, features)
        return jnp.concatenate(
            [halo_rows.astype(BF16), square[None], grad_gain.astype(BF16)[None]]
        )[None]

    def halo_vector(halo_got):
        return jnp.concatenate(
            [
                to_blocks(jnp.sum(halo_got[:, 7], axis=0)[None], depth)[0],
                jnp.pad(jnp.sum(halo_got[:, 6, 0:3])[None], (0, LANES - 1)),
            ]
        )

    tail_rows = [
        values[:, k * part : (k + 1) * part].astype(BF16)
        for values in (tail_first[0], tail_second[0])
        for k in range(fsdp // 2)
    ]
    lines = small_now[0].shape[0] // 2
    lines_tail = tail_rows[0].shape[0] // 2
    got_last = swap(tail_second[2], "fsdp", 1)
    lead = [(reduce_steps(True), ahead)]
    lead, (got_last, d_ext, squares) = advance(lead, (got_last, tail_second[3], squares))
    chains = chains + lead
    last = joined(tail_second[1], got_last)
    last_steps = reduce_steps(False)
    n_fsdp = len(bits_of(fsdp)) - 1
    for bit in bits_of(fsdp):
        tail_rows = fsdp_selected(tail_rows, bit)
    for_halo = None
    halo_steps = [gather_step(bit) for bit in bits_of(ctx)]
    sum_steps = [sum_step(bit) for bit in bits_of(fsdp)]
    while last_steps:
        for_last = [([last_steps.pop(0)], last)]
        more = [(halo_steps or sum_steps, for_halo)] if for_halo is not None else []
        chains, tail_rows = advance([*for_last, *chains, *more], tail_rows)
        last = chains.pop(0)[1]
        if more:
            for_halo = chains.pop()[1]
            if not halo_steps and halo_got is None:
                halo_got = for_halo.astype(F32)
                for_halo = halo_vector(halo_got)
        n_fsdp -= 1
        if n_fsdp == 0:
            extra = jnp.concatenate(
                [
                    side_by_side(small_now[0], lines),
                    side_by_side(tail_rows[0], lines_tail),
                    jnp.zeros((128 - lines - lines_tail, 2 * part), BF16),
                ],
                axis=0,
            ).reshape(1, -1, half)
            last = jnp.concatenate([last, extra], axis=1)
        if n_fsdp == -1:
            last, d_ext, squares = together(last, d_ext, squares)
            for_halo, halo_got = halo_start(d_ext, squares), None
    while any(steps_left for steps_left, _ in chains):
        chains, _ = advance(chains)
    while halo_steps or sum_steps:
        [(_, for_halo)], _ = advance([(halo_steps or sum_steps, for_halo)])
        if not halo_steps and halo_got is None:
            halo_got = for_halo.astype(F32)
            for_halo = halo_vector(halo_got)
    vector = for_halo
    out_now, gate_now, ahead = [values for _, values in chains]
    sum_x = [ahead[0], last[0, :depth]]
    extra = last[0, depth:].reshape(128, 2 * part)
    sum_back = one_above(extra[:lines], part).astype(F32)
    sum_tail = one_above(extra[lines : lines + lines_tail], part).astype(F32)

    d_normed = d_ext.reshape(2, ext, features)
    sum_gain = lax.dynamic_slice_in_dim(vector, me_fsdp * depth, depth)
    loss = vector[features] / (count * features)
    halo_all = halo_got[:, 0:6].reshape(ctx, 2, 3, features)
    from_next = jnp.stack([halo_all[upper, 0], halo_all[lower, 1]])
    from_next = jnp.where(has_after[:, None, None], from_next, 0.0)
    own_normed = d_normed[:, HALO:] + jnp.pad(from_next, ((0, 0), (piece - 3, 0), (0, 0)))
    own_inv = inv_rms[:, HALO:]
    own_u = rows_ext[:, HALO:]
    scaled = own_normed * gain
    d_rows = own_inv * scaled - own_u * (own_inv * own_inv * own_inv) * jnp.mean(
        scaled * own_u, axis=2, keepdims=True
    )
    grad_tokens = (to_blocks(d_rows.reshape(rows_all, features), depth) + g_out)[None]
    grad_in = jnp.concatenate([*sum_x, gate_now[0]], axis=1).astype(F32)
    return (
        out_low[None],
        loss,
        grad_tokens,
        sum_gain,
        grad_in,
        sum_tail[0:4],
        sum_tail[4],
        sum_tail[8:104].T,
        sum_back[0:rank],
        sum_back[rank + states],
        sum_back[rank : rank + states],
        sum_back[rank + states + 8],
        out_now[0].astype(F32),
    )


def solution(mesh):
    in_specs = (
        P("fsdp", "ctx", None),
        P("fsdp", "ctx", None),
        P("fsdp", None),
        P(),
        P("fsdp"),
        P("fsdp", None),
        P(None, "fsdp"),
        P("fsdp"),
        P("fsdp", None),
        P(None, "fsdp"),
        P("fsdp"),
        P(None, "fsdp"),
        P("fsdp"),
        P("fsdp", None),
    )
    out_specs = (
        P("fsdp", "ctx", None),
        P(),
        P("fsdp", "ctx", None),
        P("fsdp"),
        P("fsdp", None),
        P(None, "fsdp"),
        P("fsdp"),
        P("fsdp", None),
        P(None, "fsdp"),
        P("fsdp"),
        P(None, "fsdp"),
        P("fsdp"),
        P("fsdp", None),
    )
    return jax.shard_map(local, mesh=mesh, in_specs=in_specs, out_specs=out_specs, check_vma=False)
```

```python
import functools

import jax
import jax.numpy as jnp
from jax import lax
from jax.experimental import pallas as pl
from jax.experimental.pallas import tpu as pltpu
from jax.sharding import PartitionSpec as P

EPSILON = 1e-05
LOG2E = 1.4426950408889634
F32 = jnp.float32
BF16 = jnp.bfloat16
LANES = 128
HALO = 16
HEAD = 16
VMEM_LIMIT = 60 * 1024 * 1024
LIMITS = {
    "inputs": 20,
    "gates": 20,
    "end_states": 28,
    "forward_states": 60,
    "first_grads": 60,
    "gate_grads": 60,
    "backward_states": 60,
    "tail_grads": 60,
}


def swap(values, axis, bit):
    size = lax.axis_size(axis)
    return lax.ppermute(values, axis, [(i, i ^ bit) for i in range(size)])


def after(values, earlier):
    return lax.optimization_barrier((values, earlier))[0]


def bits_of(size):
    return [1 << k for k in range(size.bit_length() - 1)]


def gather_fsdp(values):
    blocks = {0: values}
    for bit in reversed(bits_of(lax.axis_size("fsdp"))):
        for r in sorted(blocks):
            blocks[r | bit] = swap(blocks[r], "fsdp", bit)
    return [blocks[r] for r in range(len(blocks))]


def gather_far(values):
    size = lax.axis_size("ctx")
    return [values] + [swap(values, "ctx", j) for j in range(2, size, 2)]


def gather_near(far, beside=()):
    blocks = [block for own in far[:2] for block in (own, swap(own, "ctx", 1))]
    rest, beside = together(far[2:], beside)
    return blocks + [block for own in rest for block in (own, swap(own, "ctx", 1))], beside


def together(*trees):
    return lax.optimization_barrier(trees)


def gather_small_ctx(values):
    stacked = values[None]
    for bit in bits_of(lax.axis_size("ctx")):
        stacked = jnp.concatenate([stacked, swap(stacked, "ctx", bit)], axis=0)
    return stacked


def three_parts(values):
    high = values.astype(BF16)
    rest = values - high.astype(F32)
    middle = rest.astype(BF16)
    return high, middle, (rest - middle.astype(F32)).astype(BF16)


def total(values, axes):
    for axis in axes:
        for bit in bits_of(lax.axis_size(axis)):
            values = values + swap(values, axis, bit)
    return values


def joined(kept, received):
    return (kept.astype(F32) + received.astype(F32)).astype(BF16)


def halves_of(values, bit):
    half = values.shape[1] // 2
    up = (lax.axis_index("ctx") & bit) != 0
    return values[:, :half], values[:, half:], up


def fsdp_step(bit):
    return lambda values: (values[0::2], swap(values[1::2], "fsdp", bit), joined)


def scatter_step(bit):
    def run(values):
        low, high, up = halves_of(values, bit)
        return jnp.where(up, high, low), swap(jnp.where(up, low, high), "ctx", bit), joined

    return run


def spread_step(bit):
    def finish(own, other):
        up = (lax.axis_index("ctx") & bit) != 0
        return jnp.concatenate([jnp.where(up, other, own), jnp.where(up, own, other)], axis=1)

    return lambda values: (values, swap(values, "ctx", bit), finish)


def gather_step(bit):
    return lambda values: (
        values, swap(values, "ctx", bit), lambda own, other: jnp.concatenate([own, other], axis=0)
    )


def sum_step(bit):
    return lambda values: (values, swap(values, "fsdp", bit), lambda own, other: own + other)


def reduce_steps(ctx_first, turn=0):
    fsdp_steps = [fsdp_step(bit) for bit in bits_of(lax.axis_size("fsdp"))[1:]]
    bits = bits_of(lax.axis_size("ctx"))
    bits = bits[turn:] + bits[:turn]
    scatter = [scatter_step(bit) for bit in bits]
    spread = [spread_step(bit) for bit in reversed(bits)]
    return (scatter + fsdp_steps if ctx_first else fsdp_steps + scatter) + spread


def advance(chains, beside=()):
    begun = [(steps.pop(0)(values) if steps else None, steps, values) for steps, values in chains]
    received = [step[1] for step, _, _ in begun if step]
    received, beside = together(received, beside)
    after = []
    for step, steps, values in begun:
        if step:
            values = step[2](step[0], received.pop(0))
        after.append((steps, values))
    return after, beside


def fsdp_blocks(blocks):
    for bit in bits_of(lax.axis_size("fsdp")):
        blocks = [joined(k, swap(v, "fsdp", bit)) for k, v in zip(blocks[0::2], blocks[1::2])]
        yield blocks


def fsdp_selected(blocks, bit):
    up = (lax.axis_index("fsdp") & bit) != 0
    return [
        joined(jnp.where(up, high, low), swap(jnp.where(up, low, high), "fsdp", bit))
        for low, high in zip(blocks[0::2], blocks[1::2])
    ]


def side_by_side(values, rows):
    return jnp.concatenate([values[:rows], values[rows:]], axis=1)


def one_above(values, columns):
    return jnp.concatenate([values[:, :columns], values[:, columns:]], axis=0)


def dot(left, right):
    return jnp.dot(left, right, preferred_element_type=F32)


def rows_dot(left, right):
    return lax.dot_general(left, right, (((0,), (0,)), ((), ())), preferred_element_type=F32)


def back_dot(left, right):
    return lax.dot_general(left, right, (((1,), (1,)), ((), ())), preferred_element_type=F32)


def sigmoid(values):
    return 1.0 / (1.0 + jnp.exp(-values))


def softplus(values):
    small = jnp.exp(-jnp.abs(values))
    grown = 1.0 + small
    part = jnp.where(grown == 1.0, small, jnp.log(grown) * (small / jnp.maximum(grown - 1.0, 1e-30)))
    return jnp.maximum(values, 0.0) + part


def tile_cols(j):
    return slice(j * LANES, (j + 1) * LANES)


def input_kernel(scal, normed_ref, *refs, count, piece, is_upper):
    lows, highs = refs[:count], refs[count : 2 * count]
    s_ref, x_ref, conv_ref, xs_ref, proj_ref, mixed_ref = refs[2 * count :]
    depth = lows[0].shape[0]
    width = lows[0].shape[1]
    upper = is_upper(pl.program_id(0), scal)

    def mix(weights):
        mixed = dot(normed_ref[:, 0:depth], weights[0][...])
        for r in range(1, count):
            mixed = mixed + dot(normed_ref[:, r * depth : (r + 1) * depth], weights[r][...])
        mixed_ref[...] = mixed

    @pl.when(upper)
    def from_high():
        mix(highs)

    @pl.when(jnp.logical_not(upper))
    def from_low():
        mix(lows)

    x_low = mixed_ref[...].astype(BF16).reshape(2, HALO + piece, width)
    x_ref[...] = x_low
    x = x_low.astype(F32)
    head = s_ref[0:HEAD, :].astype(F32)
    conv = head[4:5] + x[:, HALO - 3 : HALO - 3 + piece] * head[0:1]
    for k in range(1, 4):
        conv = conv + x[:, HALO - 3 + k : HALO - 3 + k + piece] * head[k : k + 1]
    conv_ref[...] = conv
    xs = (conv * sigmoid(conv)).astype(BF16)
    xs_ref[...] = xs
    part = back_dot(xs.reshape(2 * piece, width), s_ref[96:192, :])

    @pl.when(pl.program_id(0) == 0)
    def first():
        proj_ref[...] = part

    @pl.when(pl.program_id(0) > 0)
    def later():
        proj_ref[...] += part


def gate_kernel(scal, normed_ref, *refs, count, piece):
    weights, (gate_ref,) = refs[:count], refs[count:]
    depth = weights[0].shape[0]
    width = weights[0].shape[1]
    own = jnp.concatenate(
        [normed_ref[HALO : HALO + piece], normed_ref[2 * HALO + piece : 2 * HALO + 2 * piece]], axis=0
    )
    gate = dot(own[:, 0:depth], weights[0][...])
    for r in range(1, count):
        gate = gate + dot(own[:, r * depth : (r + 1) * depth], weights[r][...])
    gate_ref[...] = gate.reshape(2, piece, width)


def end_kernel(
    scal, proj_ref, s_ref, xs_ref, b_ref, step_ref, end_ref, drive_ref, *, tiles, groups, rank
):
    piece = groups * 8
    width = tiles * LANES
    states = b_ref.shape[2]
    head = s_ref[0:HEAD, :].astype(F32)
    delta = proj_ref[:, 0:rank].astype(BF16)
    pre = dot(delta, s_ref[HEAD : HEAD + rank, :]) + head[5:6]
    row = lax.broadcasted_iota(jnp.int32, (piece, width), 0)
    logs = []
    for h in range(2):
        step = softplus(pre[h * piece : (h + 1) * piece])
        step = jnp.where(row < scal[1 + h], step, 0.0)
        logs.append(jnp.sum(step, axis=0, keepdims=True))
        step_ref[h] = step.reshape(groups, 8, width)
        drive_ref[h] = (step * xs_ref[h].astype(F32)).reshape(groups, 8, width)
    logs = jnp.concatenate(logs, axis=0)
    parts = [part.astype(F32) for part in three_parts(logs)]
    end_ref[2 * states : 2 * states + 8, :] = jnp.concatenate(
        parts + [jnp.zeros_like(logs)], axis=0
    ).astype(BF16)
    rate2 = -jnp.exp(s_ref[80 : 80 + states, :].astype(F32)) * LOG2E
    rates = [rate2[:, tile_cols(j)] for j in range(tiles)]

    def body(t, held):
        held = list(held)
        for s in range(8):
            for h in range(2):
                b = b_ref[h, t * 8 + s]
                for j in range(tiles):
                    step = step_ref[h, t, s : s + 1, tile_cols(j)]
                    drive = drive_ref[h, t, s : s + 1, tile_cols(j)]
                    k = h * tiles + j
                    held[k] = jnp.exp2(step * rates[j]) * held[k] + drive * b
        return tuple(held)

    zero = jnp.zeros((states, LANES), F32)
    held = lax.fori_loop(0, groups, body, (zero,) * (2 * tiles))
    for h in range(2):
        for j in range(tiles):
            end_ref[h * states : (h + 1) * states, tile_cols(j)] = held[h * tiles + j].astype(BF16)


def span_logs(ends, plan_ref, h, ctx, states):
    rows = []
    for j in range(1, ctx):
        parts = ends[j - 1][2 * states : 2 * states + 8, :].astype(F32)
        rows.append(parts[h : h + 1] + parts[2 + h : 3 + h] + parts[4 + h : 5 + h])
    logs = jnp.concatenate([jnp.zeros_like(rows[0])] + rows, axis=0)
    inside = plan_ref[h * ctx : (h + 1) * ctx, 0:ctx]
    outside = plan_ref[(2 + h) * ctx : (3 + h) * ctx, 0:1]
    return outside + lax.dot_general(
        inside, logs, (((1,), (0,)), ((), ())), precision=lax.Precision.HIGHEST, preferred_element_type=F32
    )


def diagonal_maps(proj_ref, first, states):
    rows = proj_ref.shape[0]
    k = lax.broadcasted_iota(jnp.int32, (proj_ref.shape[1], 16 * states), 0)
    n = lax.broadcasted_iota(jnp.int32, (proj_ref.shape[1], 16 * states), 1) % states
    spread = dot(proj_ref[...].astype(BF16), (k == n + first).astype(F32).astype(BF16))
    row = lax.broadcasted_iota(jnp.int32, (rows, 16 * states), 0) % 16
    col = lax.broadcasted_iota(jnp.int32, (rows, 16 * states), 1) // states
    return jnp.where(row == col, spread, 0.0).astype(BF16)


def carried(ends, logs, rate2, h, ctx, states, cols):
    value = jnp.zeros((states, LANES), F32)
    for j in range(1, ctx):
        decay = jnp.exp2(rate2 * logs[j : j + 1, cols])
        value = value + decay * ends[j - 1][h * states : (h + 1) * states, cols].astype(F32)
    return value


def forward_kernel(scal, *refs, tiles, groups, ctx, features):
    ends = refs[: ctx - 1]
    plan_ref, s_ref, step_ref, xs_ref, gate_ref, b_ref, proj_ref, weight_ref = refs[ctx - 1 : ctx + 7]
    rest = refs[ctx + 7 :]
    scale_ref, tokens_ref, teacher_ref = rest[:3]
    ssm_ref, branch_ref, hidden_ref, start_ref, out_ref, gout_ref, dout_ref, square_ref = rest[3:11]
    drive_ref, read_ref, acc_ref, cdiag_ref = rest[11:]
    piece = groups * 8
    width = tiles * LANES
    states = b_ref.shape[2]
    i = pl.program_id(0)
    head = s_ref[0:HEAD, :].astype(F32)

    @pl.when(i == 0)
    def maps():
        values = diagonal_maps(proj_ref, proj_ref.shape[1] - states, states)
        cdiag_ref[...] = values.reshape(cdiag_ref.shape)

    for h in range(2):
        drive_ref[h] = step_ref[h] * xs_ref[h].astype(F32).reshape(groups, 8, width)
    rate2 = -jnp.exp(s_ref[80 : 80 + states, :].astype(F32)) * LOG2E
    rates = [rate2[:, tile_cols(j)] for j in range(tiles)]
    held = []
    for h in range(2):
        logs = span_logs(ends, plan_ref, h, ctx, states)
        for j in range(tiles):
            held.append(carried(ends, logs, rates[j], h, ctx, states, tile_cols(j)))
            start_ref[h, :, tile_cols(j)] = held[-1]

    def scan(t, held):
        held = list(held)
        for s in range(16):
            p = t * 16 + s
            for h in range(2):
                b = b_ref[h, p]
                for j in range(tiles):
                    cols = tile_cols(j)
                    step = step_ref[h, t * 2 + s // 8, s % 8 : s % 8 + 1, cols]
                    drive = drive_ref[h, t * 2 + s // 8, s % 8 : s % 8 + 1, cols]
                    k = h * tiles + j
                    held[k] = jnp.exp2(step * rates[j]) * held[k] + drive * b
                    hidden_ref[j, h, p] = held[k].astype(BF16)
        return tuple(held)

    def read(t):
        for h in range(2):
            for j in range(tiles):
                low = hidden_ref[j, h, pl.ds(t * 16, 16)].reshape(16 * states, LANES)
                out = dot(cdiag_ref[h, t], low)
                read_ref[h, t * 2, :, tile_cols(j)] = out[0:8]
                read_ref[h, t * 2 + 1, :, tile_cols(j)] = out[8:16]

    def body(t, held):
        read(t - 1)
        return scan(t, held)

    blocks = groups // 2
    lax.fori_loop(1, blocks, body, scan(0, tuple(held)))
    read(blocks - 1)
    branches = []
    for h in range(2):
        ssm = read_ref[h].reshape(piece, width) + head[6:7] * xs_ref[h].astype(F32)
        ssm_ref[h] = ssm
        gate = gate_ref[h]
        branches.append((ssm * (gate * sigmoid(gate))).astype(BF16))
        branch_ref[h] = branches[-1]
    part = dot(jnp.concatenate(branches, axis=0), weight_ref[...])

    @pl.when(i == 0)
    def first():
        acc_ref[...] = part

    @pl.when(i > 0)
    def later():
        acc_ref[...] += part

    @pl.when(i == pl.num_programs(0) - 1)
    def last():
        row = lax.broadcasted_iota(jnp.int32, (piece, features), 0)
        square = jnp.zeros((8, features), F32)
        for h in range(2):
            rows = slice(h * piece, (h + 1) * piece)
            block_out = tokens_ref[rows, :].astype(F32) + acc_ref[rows, :]
            out_ref[rows, :] = block_out.astype(BF16)
            error = jnp.where(row < scal[1 + h], block_out - teacher_ref[rows, :].astype(F32), 0.0)
            square = square + jnp.sum((error * error).reshape(groups, 8, features), axis=0)
            g_out = error * (2.0 * scale_ref[0, 0])
            gout_ref[rows, :] = g_out
            dout_ref[rows, :] = g_out.astype(BF16)
        square_ref[...] = square


def first_grad_kernel(
    scal, dout_ref, weight_ref, s_ref, step_ref, xs_ref, gate_ref, ssm_ref, c_ref,
    dssm_ref, dgate_ref, skip_ref, grad_ref, *, tiles, groups
):
    piece = groups * 8
    width = tiles * LANES
    states = c_ref.shape[2]
    d_branch = back_dot(dout_ref[...], weight_ref[...])
    skip = jnp.zeros((1, width), F32)
    for h in range(2):
        grad = d_branch[h * piece : (h + 1) * piece]
        gate = gate_ref[h]
        sig = sigmoid(gate)
        d_ssm = grad * (gate * sig)
        dgate_ref[h] = (grad * ssm_ref[h] * (sig * (1.0 + gate * (1.0 - sig)))).astype(BF16)
        skip = skip + jnp.sum(d_ssm * xs_ref[h].astype(F32), axis=0, keepdims=True)
        dssm_ref[h] = d_ssm.reshape(groups, 8, width)
    skip_ref[...] = skip
    rate2 = -jnp.exp(s_ref[80 : 80 + states, :].astype(F32)) * LOG2E
    rates = [rate2[:, tile_cols(j)] for j in range(tiles)]

    def body(i, held):
        held = list(held)
        t = groups - 1 - i
        for s in range(7, -1, -1):
            for h in range(2):
                c = c_ref[h, t * 8 + s]
                for j in range(tiles):
                    step = step_ref[h, t, s : s + 1, tile_cols(j)]
                    dssm = dssm_ref[h, t, s : s + 1, tile_cols(j)]
                    k = h * tiles + j
                    held[k] = jnp.exp2(step * rates[j]) * (held[k] + dssm * c)
        return tuple(held)

    zero = jnp.zeros((states, LANES), F32)
    held = lax.fori_loop(0, groups, body, (zero,) * (2 * tiles))
    for h in range(2):
        for j in range(tiles):
            grad_ref[h * states : (h + 1) * states, tile_cols(j)] = held[h * tiles + j].astype(BF16)


def out_grad_kernel(even_ref, odd_ref, dout_ref, keep_ref, send_ref):
    keep_ref[0] = rows_dot(even_ref[...], dout_ref[...]).astype(BF16)
    send_ref[0] = rows_dot(odd_ref[...], dout_ref[...]).astype(BF16)


def gate_grad_kernel(scal, normed_ref, dgate_ref, *refs, count, piece):
    weights, (keep_ref, send_ref, dnormed_ref) = refs[:count], refs[count:]
    depth = weights[0].shape[0]
    width = weights[0].shape[1]
    own = jnp.concatenate(
        [normed_ref[HALO : HALO + piece], normed_ref[2 * HALO + piece : 2 * HALO + 2 * piece]], axis=0
    )
    d_gate = dgate_ref[...].reshape(2 * piece, width)

    @pl.when(pl.program_id(0) == 0)
    def clear():
        dnormed_ref[...] = jnp.zeros_like(dnormed_ref)

    for r in range(count):
        cols = slice(r * depth, (r + 1) * depth)
        target = send_ref if r % 2 else keep_ref
        target[r // 2] = rows_dot(own[:, cols], d_gate).astype(BF16)
        back = back_dot(d_gate, weights[r][...])
        for h in range(2):
            rows = slice(h * (HALO + piece) + HALO, (h + 1) * (HALO + piece))
            dnormed_ref[rows, cols] += back[h * piece : (h + 1) * piece]


def backward_kernel(scal, *refs, tiles, groups, ctx, rank):
    grads = refs[: ctx - 1]
    ends = refs[ctx - 1 : 2 * ctx - 2]
    (
        plan_ref, proj_ref, s_ref, step_ref, xs_ref, c_ref, start_ref, dssm_ref, hidden_ref,
        dxs_ref, small_ref, ddelta_ref, db_ref, dc_ref,
        adj_ref, dstep_ref, dbs_ref, dcs_ref, bdiag_ref,
    ) = refs[2 * ctx - 2 :]
    piece = groups * 8
    width = tiles * LANES
    states = c_ref.shape[2]
    blocks = groups // 2
    i = pl.program_id(0)
    head = s_ref[0:HEAD, :].astype(F32)

    @pl.when(i == 0)
    def clear():
        dbs_ref[...] = jnp.zeros_like(dbs_ref)
        dcs_ref[...] = jnp.zeros_like(dcs_ref)
        bdiag_ref[...] = diagonal_maps(proj_ref, rank, states).reshape(bdiag_ref.shape)
        ddelta_ref[...] = jnp.zeros_like(ddelta_ref)

    rate = -jnp.exp(s_ref[80 : 80 + states, :].astype(F32))
    rates = [rate[:, tile_cols(j)] for j in range(tiles)]
    rates2 = [values * LOG2E for values in rates]
    row16 = lax.broadcasted_iota(jnp.int32, (16, 16 * states), 0)
    col16 = lax.broadcasted_iota(jnp.int32, (16, 16 * states), 1)
    same = (col16 // states == row16).astype(F32)
    same_low = same.astype(BF16)

    def work(t, first, later, sums):
        for h in range(2):
            adjoints = [[None] * 16 for _ in range(tiles)]
            terms = [[None] * 16 for _ in range(tiles)]
            for s in range(15, -1, -1):
                p = t * 16 + s
                c = c_ref[h, p]
                for j in range(tiles):
                    cols = tile_cols(j)
                    step = step_ref[h, t * 2 + s // 8, s % 8 : s % 8 + 1, cols]
                    dssm = dssm_ref[h, t * 2 + s // 8, s % 8 : s % 8 + 1, cols]
                    k = h * tiles + j
                    if first and s == 0:
                        before = start_ref[h, :, cols]
                    else:
                        before = hidden_ref[j, h, p - 1].astype(F32)
                    adjoint = dssm * c + later[k]
                    later[k] = jnp.exp2(step * rates2[j]) * adjoint
                    term = later[k] * before
                    sums[j] = sums[j] + term * step
                    adjoints[j][s] = adjoint.astype(BF16)
                    terms[j][s] = (term * rates[j]).astype(BF16)
            db = dc = None
            for j in range(tiles):
                cols = tile_cols(j)
                adjoint = jnp.concatenate(adjoints[j], axis=0)
                out = dot(bdiag_ref[h, t], adjoint)
                adj_ref[h, t * 2, :, cols] = out[0:8]
                adj_ref[h, t * 2 + 1, :, cols] = out[8:16]
                out = dot(same_low, jnp.concatenate(terms[j], axis=0))
                dstep_ref[h, t * 2, :, cols] = out[0:8]
                dstep_ref[h, t * 2 + 1, :, cols] = out[8:16]
                step = step_ref[h, pl.ds(t * 2, 2), :, cols].reshape(16, LANES)
                dssm = dssm_ref[h, pl.ds(t * 2, 2), :, cols].reshape(16, LANES)
                drive = (step * xs_ref[h, pl.ds(t * 16, 16), cols].astype(F32)).astype(BF16)
                hidden = hidden_ref[j, h, pl.ds(t * 16, 16)].reshape(16 * states, LANES)
                db_now = back_dot(drive, adjoint)
                dc_now = back_dot(dssm.astype(BF16), hidden)
                db = db_now if db is None else db + db_now
                dc = dc_now if dc is None else dc + dc_now
            dbs_ref[h, t] += db
            dcs_ref[h, t] += dc

    def body(k, both):
        later, sums = list(both[: 2 * tiles]), list(both[2 * tiles :])
        work(blocks - 1 - k, False, later, sums)
        return tuple(later + sums)

    later = []
    for h in range(2):
        logs = span_logs(ends, plan_ref, h, ctx, states)
        for j in range(tiles):
            later.append(carried(grads, logs, rates2[j], h, ctx, states, tile_cols(j)))
    sums = [jnp.zeros((states, LANES), F32)] * tiles
    both = lax.fori_loop(0, blocks - 1, body, tuple(later + sums))
    later, sums = list(both[: 2 * tiles]), list(both[2 * tiles :])
    work(0, True, later, sums)
    for j in range(tiles):
        small_ref[rank : rank + states, tile_cols(j)] = sums[j] * rates[j]
    delta = proj_ref[:, 0:rank].astype(BF16)
    pre = dot(delta, s_ref[HEAD : HEAD + rank, :]) + head[5:6]
    row = lax.broadcasted_iota(jnp.int32, (piece, width), 0)
    lows = []
    bias = jnp.zeros((1, width), F32)
    for h in range(2):
        xs = xs_ref[h].astype(F32)
        adj = adj_ref[h].reshape(piece, width)
        d_step = xs * adj + dstep_ref[h].reshape(piece, width)
        d_pre = jnp.where(row < scal[1 + h], d_step * sigmoid(pre[h * piece : (h + 1) * piece]), 0.0)
        bias = bias + jnp.sum(d_pre, axis=0, keepdims=True)
        lows.append(d_pre.astype(BF16))
        dxs_ref[h] = head[6:7] * dssm_ref[h].reshape(piece, width) + step_ref[h].reshape(piece, width) * adj
    small_ref[rank + states : rank + states + 8, :] = jnp.broadcast_to(bias, (8, width))
    low = jnp.concatenate(lows, axis=0)
    small_ref[0:rank, :] = rows_dot(delta, low)
    ddelta_ref[...] += back_dot(low, s_ref[HEAD : HEAD + rank, :])

    @pl.when(i == pl.num_programs(0) - 1)
    def last():
        for h in range(2):
            for t in range(blocks):
                db_ref[h, t : t + 1, :] = jnp.sum(dbs_ref[h, t] * same, axis=0, keepdims=True)
                dc_ref[h, t : t + 1, :] = jnp.sum(dcs_ref[h, t] * same, axis=0, keepdims=True)


def tail_kernel(
    scal, dproj_ref, s_ref, dxs_ref, conv_ref, x_ref, xs_ref, normed_ref, before_ref, *refs,
    count, piece
):
    weights, (small_ref, keep_ref, send_ref, dnormed_ref, pad_ref) = refs[:count], refs[count:]
    depth = weights[0].shape[0]
    width = weights[0].shape[1]
    ext = HALO + piece

    @pl.when(pl.program_id(0) == 0)
    def clear():
        dnormed_ref[...] = before_ref[...]
        for h in range(2):
            pad_ref[h, 0:HALO, :] = jnp.zeros((HALO, width), F32)
            pad_ref[h, ext : ext + 8, :] = jnp.zeros((8, width), F32)

    head = s_ref[0:HEAD, :].astype(F32)
    small_ref[8:104, :] = rows_dot(dproj_ref[...], xs_ref[...].reshape(2 * piece, width))
    d_xs = dot(dproj_ref[...], s_ref[96:192, :])
    taps = [jnp.zeros((1, width), F32) for _ in range(5)]
    lows = []
    for h in range(2):
        conv = conv_ref[h]
        sig = sigmoid(conv)
        d_conv = (dxs_ref[h] + d_xs[h * piece : (h + 1) * piece]) * (sig * (1.0 + conv * (1.0 - sig)))
        pad_ref[h, HALO:ext, :] = d_conv
        x = x_ref[h].astype(F32)
        for k in range(4):
            rows = slice(HALO - 3 + k, HALO - 3 + k + piece)
            taps[k] = taps[k] + jnp.sum(d_conv * x[rows], axis=0, keepdims=True)
        taps[4] = taps[4] + jnp.sum(d_conv, axis=0, keepdims=True)
        d_x = head[3:4] * pad_ref[h, 0:ext, :]
        for k in range(3):
            d_x = d_x + head[k : k + 1] * pad_ref[h, 3 - k : 3 - k + ext, :]
        lows.append(d_x.astype(BF16))
    small_ref[0:8, :] = jnp.concatenate(taps + [jnp.zeros((3, width), F32)], axis=0)
    low = jnp.concatenate(lows, axis=0)
    for r in range(count):
        cols = slice(r * depth, (r + 1) * depth)
        target = send_ref if r % 2 else keep_ref
        target[r // 2] = rows_dot(normed_ref[:, cols], low).astype(BF16)
        dnormed_ref[:, cols] += back_dot(low, weights[r][...])


def shape(dims, dtype=F32):
    return jax.ShapeDtypeStruct(dims, dtype)


def call(kernel, name, grid, scal, args, in_specs, out_specs, out_shape, scratch, flops, exps=0):
    size = sum(a.size * a.dtype.itemsize for a in args) + sum(
        s.size * s.dtype.itemsize for s in out_shape
    )
    return pl.pallas_call(
        kernel,
        grid_spec=pltpu.PrefetchScalarGridSpec(
            num_scalar_prefetch=1,
            grid=(grid,),
            in_specs=in_specs,
            out_specs=out_specs,
            scratch_shapes=scratch,
        ),
        out_shape=out_shape,
        name=name,
        compiler_params=pltpu.CompilerParams(vmem_limit_bytes=LIMITS[name] * 2**20),
        cost_estimate=pl.CostEstimate(flops=flops, bytes_accessed=size, transcendentals=exps),
    )(scal, *args)


def whole_spec(dims):
    return pl.BlockSpec(dims, lambda i, scal: (0,) * len(dims))


def local(
    tokens,
    teacher,
    lengths,
    pair_owner,
    norm_gain,
    in_proj,
    conv_weight,
    conv_bias,
    x_proj,
    dt_proj,
    dt_bias,
    a_log,
    skip_scale,
    out_proj,
):
    ctx = lax.axis_size("ctx")
    fsdp = lax.axis_size("fsdp")
    me_ctx = lax.axis_index("ctx")
    me_fsdp = lax.axis_index("fsdp")
    piece = tokens.shape[1] // 2
    features = tokens.shape[2]
    width = in_proj.shape[1] // 2
    rank = dt_proj.shape[0]
    states = a_log.shape[0]
    groups = piece // 8
    ext = HALO + piece
    depth = features // fsdp
    part = width // fsdp
    rows_all = 2 * piece
    elements = rows_all * states * width

    relative = jnp.arange(ctx, dtype=jnp.int32) ^ me_ctx
    pair_of = jnp.sum(
        jnp.arange(ctx, dtype=jnp.int32)[None, :]
        * (pair_owner[None, :] == relative[:, None]).astype(jnp.int32),
        axis=1,
    )
    places = jnp.stack([pair_of, ctx - 1 - pair_of])
    pair_id = pair_of[0]
    own = places[:, 0]
    limits = jnp.clip(lengths[0] - own * piece, 0, piece)
    scal = jnp.concatenate([me_fsdp[None], limits]).astype(jnp.int32)
    between = (places[:, :, None] < places[:, None, :]) & (
        places[:, None, :] < own[:, None, None]
    )
    between_back = (places[:, :, None] > places[:, None, :]) & (
        places[:, None, :] > own[:, None, None]
    )
    before = places < own[:, None]
    behind = places > own[:, None]
    has_before = jnp.stack([pair_id > 0, pair_id < ctx - 1])
    has_after = jnp.stack([pair_id < ctx - 1, pair_id > 0])
    lower_owner = pair_owner[jnp.maximum(pair_id - 1, 0)]
    upper_owner = pair_owner[jnp.minimum(pair_id + 1, ctx - 1)]
    lower, upper = lower_owner ^ me_ctx, upper_owner ^ me_ctx

    def plan_of(inside, wanted):
        inside = jnp.pad(inside.astype(F32), ((0, 0), (0, 0), (0, LANES - ctx)))
        outside = jnp.broadcast_to(jnp.where(wanted, 0.0, 1e30)[..., None], (2, ctx, LANES))
        return jnp.concatenate([inside, outside], axis=0).reshape(4 * ctx, LANES).astype(F32)

    plan_before = plan_of(between, before)
    plan_behind = plan_of(between_back, behind)

    def to_blocks(values, size):
        axis = values.ndim - 1
        return jnp.concatenate(
            [
                lax.dynamic_slice_in_dim(values, (me_fsdp ^ r) * size, size, axis=axis)
                for r in range(fsdp)
            ],
            axis=axis,
        )

    own_rows = tokens[0]
    valid_slots = jnp.minimum(lengths[0], 2 * ctx * piece)
    coded = jnp.concatenate([valid_slots // 128, valid_slots % 128]).astype(BF16)[None]
    rows_head = jnp.concatenate(
        [
            conv_weight,
            conv_bias[None],
            dt_bias[None],
            skip_scale[None],
            jnp.pad(norm_gain, (0, part - depth))[None],
            jnp.pad(coded, ((0, 0), (0, part - 4))),
            jnp.zeros((HEAD - 9, part), BF16),
            dt_proj,
            a_log,
            x_proj.T,
        ],
        axis=0,
    )
    half = width // 2
    to_send = in_proj[:, :half]
    x_far = [to_send] + [swap(to_send, "fsdp", bit) for bit in range(2, fsdp, 2)]
    last_rows = to_blocks(own_rows.reshape(2, piece, features)[:, piece - 3 :], depth)
    last_rows = jnp.broadcast_to(last_rows[None], (ctx, 2, 3, features))
    token_rel = to_blocks(own_rows, depth).reshape(2, piece, features)
    tails = lax.all_to_all(last_rows, "ctx", 0, 0)
    x_far, second, rows_head, tails, token_rel, scal, plan_before, plan_behind = together(
        x_far, in_proj[:, half:width], rows_head, tails, token_rel, scal, plan_before, plan_behind
    )
    x_first = [block for own in x_far for block in (own, swap(own, "fsdp", 1))]
    small_blocks = gather_fsdp(rows_head)
    small = jnp.concatenate(small_blocks, axis=1)
    gain = jnp.concatenate([block[7, :depth] for block in small_blocks]).astype(F32)
    x_second = gather_fsdp(second)

    before_rows = jnp.stack([tails[lower_owner, 0], tails[upper_owner, 1]])
    before_rows = jnp.where(has_before[:, None, None], before_rows, jnp.zeros_like(before_rows))
    rows_ext = jnp.concatenate(
        [jnp.zeros((2, HALO - 3, features), BF16), before_rows, token_rel], axis=1
    ).astype(F32)
    inv_rms = lax.rsqrt(jnp.mean(rows_ext * rows_ext, axis=2, keepdims=True) + EPSILON)
    normed = (rows_ext * inv_rms * gain).astype(BF16).reshape(2 * ext, features)

    codes = jnp.stack([block[8, :4] for block in small_blocks]).astype(F32)
    count = jnp.sum(codes[:, 0:2] * 128.0 + codes[:, 2:4])
    scale = ((fsdp * rows_all * ctx) / count).reshape(1, 1)

    def cols_at(block):
        per = part // block
        return lambda i, scal: (0, (scal[0] ^ (i // per)) * per + i % per)

    def spec_small(block, offset=0):
        return pl.BlockSpec((small.shape[0], block), lambda i, scal: (0, i + offset))

    def spec_rows(block, offset=0):
        return pl.BlockSpec((2, piece, block), lambda i, scal: (0, 0, i + offset))

    def spec_groups(block):
        return pl.BlockSpec((2, groups, 8, block), lambda i, scal: (0, 0, 0, i))

    cb = min(256, part)
    steps = width // cb
    weight_specs = [pl.BlockSpec((depth, cb), cols_at(cb)) for _ in range(fsdp)]
    half_blocks = half // cb

    def upper_place(i, scal):
        return cols_at(cb)(i, scal)[1] >= half_blocks

    low_spec = pl.BlockSpec(
        (depth, cb), lambda i, scal: (0, jnp.minimum(cols_at(cb)(i, scal)[1], half_blocks - 1))
    )
    high_spec = pl.BlockSpec(
        (depth, cb), lambda i, scal: (0, jnp.maximum(cols_at(cb)(i, scal)[1] - half_blocks, 0))
    )
    x_ext, conv, xs, proj = call(
        functools.partial(input_kernel, count=fsdp, piece=piece, is_upper=upper_place),
        "inputs", steps, scal, (normed, *x_first, *x_second, small),
        [whole_spec((2 * ext, features)), *([low_spec] * fsdp), *([high_spec] * fsdp), spec_small(cb)],
        [
            pl.BlockSpec((2, ext, cb), lambda i, scal: (0, 0, i)),
            spec_rows(cb),
            spec_rows(cb),
            whole_spec((rows_all, rank + 2 * states)),
        ],
        [
            shape((2, ext, width), BF16),
            shape((2, piece, width)),
            shape((2, piece, width), BF16),
            shape((rows_all, rank + 2 * states)),
        ],
        [pltpu.VMEM((2 * ext, cb), F32)], 2 * rows_all * features * width,
    )
    gate_first = after(in_proj[:, width:], x_second[fsdp // 2])
    gate_far = [gate_first] + [swap(gate_first, "fsdp", bit) for bit in range(2, fsdp, 2)]
    gate_far, proj = together(gate_far, proj)
    gate_blocks = [block for own in gate_far for block in (own, swap(own, "fsdp", 1))]
    out_first = after(out_proj, gate_far[-1])
    out_far = [out_first] + [swap(out_first, "fsdp", bit) for bit in range(2, fsdp, 2)]
    wide_dims = (2, piece, states, LANES)
    maps = proj[:, rank:].reshape(2, piece, 2 * states, 1)
    b_wide = jnp.broadcast_to(maps[:, :, :states], wide_dims)

    tiles = 4
    block = tiles * LANES
    per_half = half // block
    group_spec = spec_groups(block)
    state_row = pl.BlockSpec((2 * states, block), lambda i, scal: (0, i))
    sent_row = pl.BlockSpec((2 * states + 8, block), lambda i, scal: (0, i))
    plan_spec = whole_spec((4 * ctx, LANES))
    row_spec = whole_spec((rows_all, features))
    wide_spec = whole_spec(wide_dims)
    diag_space = pltpu.VMEM((2, piece // 16, 16, 16 * states), BF16)
    hidden_spec = pl.BlockSpec((tiles, 2, piece, states, LANES), lambda i, scal: (i, 0, 0, 0, 0))
    start_spec = pl.BlockSpec((2, states, block), lambda i, scal: (0, 0, i))
    group_space = pltpu.VMEM((2, groups, 8, block), F32)

    step, sent = call(
        functools.partial(end_kernel, tiles=tiles, groups=groups, rank=rank),
        "end_states", width // block, scal, (proj, small, xs, b_wide),
        [whole_spec(proj.shape), spec_small(block), spec_rows(block), wide_spec],
        [group_spec, pl.BlockSpec((2 * states + 8, block), lambda i, scal: (0, i))],
        [shape((2, groups, 8, width)), shape((2 * states + 8, width), BF16)],
        [group_space], 5 * elements, elements,
    )

    far = gather_far(sent)
    (gate,) = call(
        functools.partial(gate_kernel, count=fsdp, piece=piece),
        "gates", steps, scal, (normed, *gate_blocks),
        [whole_spec((2 * ext, features)), *weight_specs], [spec_rows(cb)],
        [shape((2, piece, width))], [], 2 * rows_all * features * width,
    )
    c_wide = jnp.broadcast_to(maps[:, :, states:], wide_dims)
    far, gate, out_far = together(far, gate, out_far)
    near, c_wide = gather_near(far, c_wide)
    out_blocks = [block for own in out_far for block in (own, swap(own, "fsdp", 1))]
    weight_out = jnp.concatenate(out_blocks, axis=0)
    near, weight_out = together(near, weight_out)
    ssm, branch, hidden, starts, out_low, g_out, d_out, squares = call(
        functools.partial(forward_kernel, tiles=tiles, groups=groups, ctx=ctx, features=features),
        "forward_states", width // block, scal,
        (*near[1:], plan_before, small, step, xs, gate, b_wide, proj, weight_out,
         scale, own_rows, teacher[0]),
        [
            *([sent_row] * (ctx - 1)), plan_spec, spec_small(block), group_spec, spec_rows(block),
            spec_rows(block), wide_spec, whole_spec(proj.shape),
            pl.BlockSpec((block, features), lambda i, scal: (i, 0)),
            pl.BlockSpec(memory_space=pltpu.SMEM), row_spec, row_spec,
        ],
        [
            spec_rows(block), spec_rows(block), hidden_spec, start_spec, row_spec, row_spec, row_spec,
            whole_spec((8, features)),
        ],
        [
            shape((2, piece, width)),
            shape((2, piece, width), BF16),
            shape((width // LANES, 2, piece, states, LANES), BF16),
            shape((2, states, width)),
            shape((rows_all, features), BF16),
            shape((rows_all, features)),
            shape((rows_all, features), BF16),
            shape((8, features)),
        ],
        [group_space] * 2 + [pltpu.VMEM((rows_all, features), F32), diag_space],
        10 * elements, elements,
    )
    d_ssm, d_gate, grad_skip, grads_first = call(
        functools.partial(first_grad_kernel, tiles=tiles, groups=groups),
        "first_grads", width // block, scal,
        (d_out, weight_out, small, step, xs, gate, ssm, c_wide),
        [
            row_spec, pl.BlockSpec((block, features), lambda i, scal: (i, 0)), spec_small(block),
            group_spec, spec_rows(block), spec_rows(block), spec_rows(block), wide_spec,
        ],
        [group_spec, spec_rows(block), pl.BlockSpec((1, block), lambda i, scal: (0, i)), state_row],
        [
            shape((2, groups, 8, width)),
            shape((2, piece, width), BF16),
            shape((1, width)),
            shape((2 * states, width), BF16),
        ],
        [], 6 * elements, elements,
    )
    back_far = gather_far(grads_first)

    pairs = fsdp // 2
    pair_spec = pl.BlockSpec((pairs, depth, cb), lambda i, scal: (0, 0, i))
    pair_at = pl.BlockSpec((pairs, depth, cb), lambda i, scal: (0, 0, cols_at(cb)(i, scal)[1]))
    keep_gate, send_gate, d_normed_gate = call(
        functools.partial(gate_grad_kernel, count=fsdp, piece=piece),
        "gate_grads", steps, scal, (normed, d_gate, *gate_blocks),
        [whole_spec((2 * ext, features)), spec_rows(cb), *weight_specs],
        [pair_at, pair_at, whole_spec((2 * ext, features))],
        [shape((pairs, depth, width), BF16)] * 2 + [shape((2 * ext, features))],
        [], 4 * rows_all * features * width,
    )
    subs = part // cb
    branch_rows = branch.reshape(rows_all, width)
    keep_out, send_out = pl.pallas_call(
        out_grad_kernel,
        grid=(pairs, subs),
        in_specs=[
            pl.BlockSpec((rows_all, cb), lambda k, s: (0, 2 * k * subs + s)),
            pl.BlockSpec((rows_all, cb), lambda k, s: (0, (2 * k + 1) * subs + s)),
            pl.BlockSpec((rows_all, features), lambda k, s: (0, 0)),
        ],
        out_specs=[pl.BlockSpec((1, cb, features), lambda k, s: (k, s, 0))] * 2,
        out_shape=[shape((pairs, part, features), BF16)] * 2,
        name="out_grads",
        compiler_params=pltpu.CompilerParams(vmem_limit_bytes=VMEM_LIMIT),
        cost_estimate=pl.CostEstimate(
            flops=2 * rows_all * width * features, bytes_accessed=9 * 2**20, transcendentals=0
        ),
    )(branch_rows, branch_rows, d_out)
    back_far, keep_gate, send_gate, keep_out, send_out = together(
        back_far, keep_gate, send_gate, keep_out, send_out
    )
    back_near, _ = gather_near(back_far)
    core_gate = joined(keep_gate, swap(send_gate, "fsdp", 1))
    core_out = joined(keep_out, swap(send_out, "fsdp", 1))
    back_near, core_out, core_gate = together(back_near, core_out, core_gate)
    chains = [(reduce_steps(False), core_out), (reduce_steps(True, 1), core_gate)]

    def backward():
        def at(i):
            return i

        return call(
            functools.partial(backward_kernel, tiles=tiles, groups=groups, ctx=ctx, rank=rank),
            "backward_states", width // block, scal,
            (*back_near[1:], *near[1:], plan_behind, proj, small, step, xs, c_wide, starts, d_ssm, hidden),
            [
                *([pl.BlockSpec((2 * states, block), lambda i, scal: (0, at(i)))] * (ctx - 1)),
                *([pl.BlockSpec((2 * states + 8, block), lambda i, scal: (0, at(i)))] * (ctx - 1)),
                plan_spec,
                whole_spec(proj.shape), spec_small(block),
                pl.BlockSpec((2, groups, 8, block), lambda i, scal: (0, 0, 0, at(i))),
                spec_rows(block), wide_spec,
                pl.BlockSpec((2, states, block), lambda i, scal: (0, 0, at(i))),
                pl.BlockSpec((2, groups, 8, block), lambda i, scal: (0, 0, 0, at(i))),
                pl.BlockSpec((tiles, 2, piece, states, LANES), lambda i, scal: (at(i), 0, 0, 0, 0)),
            ],
            [
                spec_rows(block), pl.BlockSpec((rank + states + 8, block), lambda i, scal: (0, i)),
                whole_spec((rows_all, rank)),
                whole_spec((2, piece // 16, 16 * states)), whole_spec((2, piece // 16, 16 * states)),
            ],
            [
                shape((2, piece, width)),
                shape((rank + states + 8, width)),
                shape((rows_all, rank)),
                shape((2, piece // 16, 16 * states)),
                shape((2, piece // 16, 16 * states)),
            ],
            [group_space] * 2 + [pltpu.VMEM((2, piece // 16, 16, 16 * states), F32)] * 2 + [diag_space],
            16 * elements, elements,
        )

    chains, back = advance(chains, backward())

    small_rows = jnp.concatenate(
        [back[1], grad_skip, jnp.zeros((7, width), F32)], axis=0
    ).astype(BF16)
    d_proj = jnp.concatenate(
        [back[2], back[3].reshape(rows_all, states), back[4].reshape(rows_all, states)], axis=1
    ).astype(BF16)
    half_steps = steps // 2

    def tail(c, d_proj, d_before):
        base = c * half_steps

        def place(i, scal):
            return cols_at(cb)(i + base, scal)[1]

        def at_rows(dims):
            return pl.BlockSpec((2, dims, cb), lambda i, scal: (0, 0, place(i, scal)))

        return call(
            functools.partial(tail_kernel, count=fsdp, piece=piece),
            "tail_grads", half_steps, scal,
            (d_proj, small, back[0], conv, x_ext, xs, normed, d_before,
             *(x_second if c else x_first)),
            [
                whole_spec(d_proj.shape),
                pl.BlockSpec((small.shape[0], cb), lambda i, scal: (0, place(i, scal))),
                at_rows(piece), at_rows(piece), at_rows(ext), at_rows(piece),
                whole_spec((2 * ext, features)), whole_spec((2 * ext, features)),
                *([pl.BlockSpec((depth, cb), lambda i, scal: (0, i))] * fsdp),
            ],
            [
                pl.BlockSpec((104, cb), lambda i, scal: (0, i)),
                pair_spec, pair_spec, whole_spec((2 * ext, features)),
            ],
            [
                shape((104, half)),
                shape((pairs, depth, half), BF16),
                shape((pairs, depth, half), BF16),
                shape((2 * ext, features)),
            ],
            [pltpu.VMEM((2, ext + 8, cb), F32)],
            4 * rows_all * features * half,
        )

    d_before = d_normed_gate
    d_proj, d_before, _ = together(d_proj, d_before, [values for _, values in chains])
    chains, tail_first = advance(chains, tail(0, d_proj, d_before))
    got_ahead = swap(tail_first[2], "fsdp", 1)
    small_now = [small_rows[:, k * part : (k + 1) * part] for k in range(fsdp)]
    for small_now in fsdp_blocks(small_now):
        pass
    d_proj, _ = together(d_proj, [values for _, values in chains])
    chains, (tail_second, got_ahead, small_now) = advance(
        chains, (tail(1, d_proj, tail_first[3]), got_ahead, small_now)
    )
    ahead = joined(tail_first[1], got_ahead)
    def halo_start(d_ext, squares):
        d_normed = d_ext.reshape(2, ext, features)
        unit = rows_ext * inv_rms
        grad_gain = jnp.sum(d_normed[:, HALO - 3 :] * unit[:, HALO - 3 :], axis=(0, 1))
        square = jnp.pad(jnp.stack(three_parts(jnp.sum(squares))), (0, features - 3))
        halo_rows = d_normed[:, HALO - 3 : HALO].reshape(6, features)
        return jnp.concatenate(
            [halo_rows.astype(BF16), square[None], grad_gain.astype(BF16)[None]]
        )[None]

    def halo_vector(halo_got):
        return jnp.concatenate(
            [
                to_blocks(jnp.sum(halo_got[:, 7], axis=0)[None], depth)[0],
                jnp.pad(jnp.sum(halo_got[:, 6, 0:3])[None], (0, LANES - 1)),
            ]
        )

    tail_rows = [
        values[:, k * part : (k + 1) * part].astype(BF16)
        for values in (tail_first[0], tail_second[0])
        for k in range(fsdp // 2)
    ]
    lines = small_now[0].shape[0] // 2
    lines_tail = tail_rows[0].shape[0] // 2
    got_last = swap(tail_second[2], "fsdp", 1)
    lead = [(reduce_steps(True), ahead)]
    lead, (got_last, d_ext, squares) = advance(lead, (got_last, tail_second[3], squares))
    chains = chains + lead
    last = joined(tail_second[1], got_last)
    last_steps = reduce_steps(False)
    n_fsdp = len(bits_of(fsdp)) - 1
    for bit in bits_of(fsdp):
        tail_rows = fsdp_selected(tail_rows, bit)
    for_halo = None
    halo_steps = [gather_step(bit) for bit in bits_of(ctx)]
    sum_steps = [sum_step(bit) for bit in bits_of(fsdp)]
    while last_steps:
        for_last = [([last_steps.pop(0)], last)]
        more = [(halo_steps or sum_steps, for_halo)] if for_halo is not None else []
        chains, tail_rows = advance([*for_last, *chains, *more], tail_rows)
        last = chains.pop(0)[1]
        if more:
            for_halo = chains.pop()[1]
            if not halo_steps and halo_got is None:
                halo_got = for_halo.astype(F32)
                for_halo = halo_vector(halo_got)
        n_fsdp -= 1
        if n_fsdp == 0:
            extra = jnp.concatenate(
                [
                    side_by_side(small_now[0], lines),
                    side_by_side(tail_rows[0], lines_tail),
                    jnp.zeros((128 - lines - lines_tail, 2 * part), BF16),
                ],
                axis=0,
            ).reshape(1, -1, half)
            last = jnp.concatenate([last, extra], axis=1)
        if n_fsdp == -1:
            last, d_ext, squares = together(last, d_ext, squares)
            for_halo, halo_got = halo_start(d_ext, squares), None
    while any(steps_left for steps_left, _ in chains):
        chains, _ = advance(chains)
    while halo_steps or sum_steps:
        [(_, for_halo)], _ = advance([(halo_steps or sum_steps, for_halo)])
        if not halo_steps and halo_got is None:
            halo_got = for_halo.astype(F32)
            for_halo = halo_vector(halo_got)
    vector = for_halo
    out_now, gate_now, ahead = [values for _, values in chains]
    sum_x = [ahead[0], last[0, :depth]]
    extra = last[0, depth:].reshape(128, 2 * part)
    sum_back = one_above(extra[:lines], part).astype(F32)
    sum_tail = one_above(extra[lines : lines + lines_tail], part).astype(F32)

    d_normed = d_ext.reshape(2, ext, features)
    sum_gain = lax.dynamic_slice_in_dim(vector, me_fsdp * depth, depth)
    loss = vector[features] / (count * features)
    halo_all = halo_got[:, 0:6].reshape(ctx, 2, 3, features)
    from_next = jnp.stack([halo_all[upper, 0], halo_all[lower, 1]])
    from_next = jnp.where(has_after[:, None, None], from_next, 0.0)
    own_normed = d_normed[:, HALO:] + jnp.pad(from_next, ((0, 0), (piece - 3, 0), (0, 0)))
    own_inv = inv_rms[:, HALO:]
    own_u = rows_ext[:, HALO:]
    scaled = own_normed * gain
    d_rows = own_inv * scaled - own_u * (own_inv * own_inv * own_inv) * jnp.mean(
        scaled * own_u, axis=2, keepdims=True
    )
    grad_tokens = (to_blocks(d_rows.reshape(rows_all, features), depth) + g_out)[None]
    grad_in = jnp.concatenate([*sum_x, gate_now[0]], axis=1).astype(F32)
    return (
        out_low[None],
        loss,
        grad_tokens,
        sum_gain,
        grad_in,
        sum_tail[0:4],
        sum_tail[4],
        sum_tail[8:104].T,
        sum_back[0:rank],
        sum_back[rank + states],
        sum_back[rank : rank + states],
        sum_back[rank + states + 8],
        out_now[0].astype(F32),
    )


def solution(mesh):
    in_specs = (
        P("fsdp", "ctx", None),
        P("fsdp", "ctx", None),
        P("fsdp", None),
        P(),
        P("fsdp"),
        P("fsdp", None),
        P(None, "fsdp"),
        P("fsdp"),
        P("fsdp", None),
        P(None, "fsdp"),
        P("fsdp"),
        P(None, "fsdp"),
        P("fsdp"),
        P("fsdp", None),
    )
    out_specs = (
        P("fsdp", "ctx", None),
        P(),
        P("fsdp", "ctx", None),
        P("fsdp"),
        P("fsdp", None),
        P(None, "fsdp"),
        P("fsdp"),
        P("fsdp", None),
        P(None, "fsdp"),
        P("fsdp"),
        P(None, "fsdp"),
        P("fsdp"),
        P("fsdp", None),
    )
    return jax.shard_map(local, mesh=mesh, in_specs=in_specs, out_specs=out_specs, check_vma=False)
```

```python
import functools

import jax
import jax.numpy as jnp
from jax import lax
from jax.experimental import pallas as pl
from jax.experimental.pallas import tpu as pltpu
from jax.sharding import PartitionSpec as P

EPSILON = 1e-05
LOG2E = 1.4426950408889634
F32 = jnp.float32
BF16 = jnp.bfloat16
LANES = 128
HALO = 16
HEAD = 16
VMEM_LIMIT = 60 * 1024 * 1024
LIMITS = {
    "inputs": 20,
    "gates": 20,
    "end_states": 28,
    "forward_states": 60,
    "first_grads": 60,
    "gate_grads": 60,
    "backward_states": 60,
    "tail_grads": 60,
}


def swap(values, axis, bit):
    size = lax.axis_size(axis)
    return lax.ppermute(values, axis, [(i, i ^ bit) for i in range(size)])


def after(values, earlier):
    return lax.optimization_barrier((values, earlier))[0]


def bits_of(size):
    return [1 << k for k in range(size.bit_length() - 1)]


def gather_fsdp(values):
    blocks = {0: values}
    for bit in reversed(bits_of(lax.axis_size("fsdp"))):
        for r in sorted(blocks):
            blocks[r | bit] = swap(blocks[r], "fsdp", bit)
    return [blocks[r] for r in range(len(blocks))]


def gather_far(values):
    size = lax.axis_size("ctx")
    return [values] + [swap(values, "ctx", j) for j in range(2, size, 2)]


def gather_near(far, beside=()):
    blocks = [block for own in far[:2] for block in (own, swap(own, "ctx", 1))]
    rest, beside = together(far[2:], beside)
    return blocks + [block for own in rest for block in (own, swap(own, "ctx", 1))], beside


def together(*trees):
    return lax.optimization_barrier(trees)


def gather_small_ctx(values):
    stacked = values[None]
    for bit in bits_of(lax.axis_size("ctx")):
        stacked = jnp.concatenate([stacked, swap(stacked, "ctx", bit)], axis=0)
    return stacked


def three_parts(values):
    high = values.astype(BF16)
    rest = values - high.astype(F32)
    middle = rest.astype(BF16)
    return high, middle, (rest - middle.astype(F32)).astype(BF16)


def total(values, axes):
    for axis in axes:
        for bit in bits_of(lax.axis_size(axis)):
            values = values + swap(values, axis, bit)
    return values


def joined(kept, received):
    return (kept.astype(F32) + received.astype(F32)).astype(BF16)


def part_of(values, take):
    if isinstance(values, tuple):
        return joined(take(values[0]), take(values[1]))
    return take(values)


def pending(own, other):
    return own, other


def fsdp_step(bit):
    def ready(values):
        return part_of(values, lambda v: v[0::2]), part_of(values, lambda v: v[1::2])

    return ready, "fsdp", bit, pending


def scatter_step(bit):
    def ready(values):
        up = (lax.axis_index("ctx") & bit) != 0

        def low(v):
            return v[:, : v.shape[1] // 2]

        def high(v):
            return v[:, v.shape[1] // 2 :]

        keep = jnp.where(up, part_of(values, high), part_of(values, low))
        return keep, jnp.where(up, part_of(values, low), part_of(values, high))

    return ready, "ctx", bit, pending


def spread_step(bit):
    def finish(own, other):
        up = (lax.axis_index("ctx") & bit) != 0
        return jnp.concatenate([jnp.where(up, other, own), jnp.where(up, own, other)], axis=1)

    def ready(values):
        values = part_of(values, lambda v: v)
        return values, values

    return ready, "ctx", bit, finish


def same_twice(values):
    return values, values


def gather_step(bit):
    return same_twice, "ctx", bit, lambda own, other: jnp.concatenate([own, other], axis=0)


def sum_step(bit):
    return same_twice, "fsdp", bit, lambda own, other: own + other


def reduce_steps(ctx_first, turn=0):
    fsdp_steps = [fsdp_step(bit) for bit in bits_of(lax.axis_size("fsdp"))[1:]]
    bits = bits_of(lax.axis_size("ctx"))
    bits = bits[turn:] + bits[:turn]
    scatter = [scatter_step(bit) for bit in bits]
    spread = [spread_step(bit) for bit in reversed(bits)]
    return (scatter + fsdp_steps if ctx_first else fsdp_steps + scatter) + spread


def advance(chains, beside=()):
    begun = []
    for steps, values in chains:
        if steps:
            ready, axis, bit, finish = steps.pop(0)
            keep, send = ready(values)
            values = (keep, swap(send, axis, bit), finish)
            begun.append((steps, values))
        else:
            begun.append((None, values))
    received, beside = together([values[1] for steps, values in begun if steps is not None], beside)
    after = []
    for steps, values in begun:
        if steps is None:
            after.append(([], values))
        else:
            after.append((steps, values[2](values[0], received.pop(0))))
    return after, beside


def fsdp_blocks(blocks):
    for bit in bits_of(lax.axis_size("fsdp")):
        blocks = [joined(k, swap(v, "fsdp", bit)) for k, v in zip(blocks[0::2], blocks[1::2])]
        yield blocks


def fsdp_selected(blocks, bit):
    up = (lax.axis_index("fsdp") & bit) != 0
    return [
        joined(jnp.where(up, high, low), swap(jnp.where(up, low, high), "fsdp", bit))
        for low, high in zip(blocks[0::2], blocks[1::2])
    ]


def side_by_side(values, rows):
    return jnp.concatenate([values[:rows], values[rows:]], axis=1)


def one_above(values, columns):
    return jnp.concatenate([values[:, :columns], values[:, columns:]], axis=0)


def dot(left, right):
    return jnp.dot(left, right, preferred_element_type=F32)


def rows_dot(left, right):
    return lax.dot_general(left, right, (((0,), (0,)), ((), ())), preferred_element_type=F32)


def back_dot(left, right):
    return lax.dot_general(left, right, (((1,), (1,)), ((), ())), preferred_element_type=F32)


def sigmoid(values):
    return 1.0 / (1.0 + jnp.exp(-values))


def softplus(values):
    small = jnp.exp(-jnp.abs(values))
    grown = 1.0 + small
    part = jnp.where(grown == 1.0, small, jnp.log(grown) * (small / jnp.maximum(grown - 1.0, 1e-30)))
    return jnp.maximum(values, 0.0) + part


def tile_cols(j):
    return slice(j * LANES, (j + 1) * LANES)


def input_kernel(scal, normed_ref, *refs, count, piece, is_upper):
    lows, highs = refs[:count], refs[count : 2 * count]
    s_ref, x_ref, conv_ref, xs_ref, proj_ref, mixed_ref = refs[2 * count :]
    depth = lows[0].shape[0]
    width = lows[0].shape[1]
    upper = is_upper(pl.program_id(0), scal)

    def mix(weights):
        mixed = dot(normed_ref[:, 0:depth], weights[0][...])
        for r in range(1, count):
            mixed = mixed + dot(normed_ref[:, r * depth : (r + 1) * depth], weights[r][...])
        mixed_ref[...] = mixed

    @pl.when(upper)
    def from_high():
        mix(highs)

    @pl.when(jnp.logical_not(upper))
    def from_low():
        mix(lows)

    x_low = mixed_ref[...].astype(BF16).reshape(2, HALO + piece, width)
    x_ref[...] = x_low
    x = x_low.astype(F32)
    head = s_ref[0:HEAD, :].astype(F32)
    conv = head[4:5] + x[:, HALO - 3 : HALO - 3 + piece] * head[0:1]
    for k in range(1, 4):
        conv = conv + x[:, HALO - 3 + k : HALO - 3 + k + piece] * head[k : k + 1]
    conv_ref[...] = conv
    xs = (conv * sigmoid(conv)).astype(BF16)
    xs_ref[...] = xs
    part = back_dot(xs.reshape(2 * piece, width), s_ref[96:192, :])

    @pl.when(pl.program_id(0) == 0)
    def first():
        proj_ref[...] = part

    @pl.when(pl.program_id(0) > 0)
    def later():
        proj_ref[...] += part


def gate_kernel(scal, normed_ref, *refs, count, piece):
    weights, (gate_ref,) = refs[:count], refs[count:]
    depth = weights[0].shape[0]
    width = weights[0].shape[1]
    own = jnp.concatenate(
        [normed_ref[HALO : HALO + piece], normed_ref[2 * HALO + piece : 2 * HALO + 2 * piece]], axis=0
    )
    gate = dot(own[:, 0:depth], weights[0][...])
    for r in range(1, count):
        gate = gate + dot(own[:, r * depth : (r + 1) * depth], weights[r][...])
    gate_ref[...] = gate.reshape(2, piece, width)


def end_kernel(
    scal, proj_ref, s_ref, xs_ref, b_ref, step_ref, end_ref, drive_ref, *, tiles, groups, rank
):
    piece = groups * 8
    width = tiles * LANES
    states = b_ref.shape[2]
    head = s_ref[0:HEAD, :].astype(F32)
    delta = proj_ref[:, 0:rank].astype(BF16)
    pre = dot(delta, s_ref[HEAD : HEAD + rank, :]) + head[5:6]
    row = lax.broadcasted_iota(jnp.int32, (piece, width), 0)
    logs = []
    for h in range(2):
        step = softplus(pre[h * piece : (h + 1) * piece])
        step = jnp.where(row < scal[1 + h], step, 0.0)
        logs.append(jnp.sum(step, axis=0, keepdims=True))
        step_ref[h] = step.reshape(groups, 8, width)
        drive_ref[h] = (step * xs_ref[h].astype(F32)).reshape(groups, 8, width)
    logs = jnp.concatenate(logs, axis=0)
    parts = [part.astype(F32) for part in three_parts(logs)]
    end_ref[2 * states : 2 * states + 8, :] = jnp.concatenate(
        parts + [jnp.zeros_like(logs)], axis=0
    ).astype(BF16)
    rate2 = -jnp.exp(s_ref[80 : 80 + states, :].astype(F32)) * LOG2E
    rates = [rate2[:, tile_cols(j)] for j in range(tiles)]

    def body(t, held):
        held = list(held)
        for s in range(8):
            for h in range(2):
                b = b_ref[h, t * 8 + s]
                for j in range(tiles):
                    step = step_ref[h, t, s : s + 1, tile_cols(j)]
                    drive = drive_ref[h, t, s : s + 1, tile_cols(j)]
                    k = h * tiles + j
                    held[k] = jnp.exp2(step * rates[j]) * held[k] + drive * b
        return tuple(held)

    zero = jnp.zeros((states, LANES), F32)
    held = lax.fori_loop(0, groups, body, (zero,) * (2 * tiles))
    for h in range(2):
        for j in range(tiles):
            end_ref[h * states : (h + 1) * states, tile_cols(j)] = held[h * tiles + j].astype(BF16)


def span_logs(ends, plan_ref, h, ctx, states):
    rows = []
    for j in range(1, ctx):
        parts = ends[j - 1][2 * states : 2 * states + 8, :].astype(F32)
        rows.append(parts[h : h + 1] + parts[2 + h : 3 + h] + parts[4 + h : 5 + h])
    logs = jnp.concatenate([jnp.zeros_like(rows[0])] + rows, axis=0)
    inside = plan_ref[h * ctx : (h + 1) * ctx, 0:ctx]
    outside = plan_ref[(2 + h) * ctx : (3 + h) * ctx, 0:1]
    return outside + lax.dot_general(
        inside, logs, (((1,), (0,)), ((), ())), precision=lax.Precision.HIGHEST, preferred_element_type=F32
    )


def diagonal_maps(proj_ref, first, states):
    rows = proj_ref.shape[0]
    k = lax.broadcasted_iota(jnp.int32, (proj_ref.shape[1], 16 * states), 0)
    n = lax.broadcasted_iota(jnp.int32, (proj_ref.shape[1], 16 * states), 1) % states
    spread = dot(proj_ref[...].astype(BF16), (k == n + first).astype(F32).astype(BF16))
    row = lax.broadcasted_iota(jnp.int32, (rows, 16 * states), 0) % 16
    col = lax.broadcasted_iota(jnp.int32, (rows, 16 * states), 1) // states
    return jnp.where(row == col, spread, 0.0).astype(BF16)


def carried(ends, logs, rate2, h, ctx, states, cols):
    value = jnp.zeros((states, LANES), F32)
    for j in range(1, ctx):
        decay = jnp.exp2(rate2 * logs[j : j + 1, cols])
        value = value + decay * ends[j - 1][h * states : (h + 1) * states, cols].astype(F32)
    return value


def forward_kernel(scal, *refs, tiles, groups, ctx, features):
    ends = refs[: ctx - 1]
    plan_ref, s_ref, step_ref, xs_ref, gate_ref, b_ref, proj_ref, weight_ref = refs[ctx - 1 : ctx + 7]
    rest = refs[ctx + 7 :]
    scale_ref, tokens_ref, teacher_ref = rest[:3]
    ssm_ref, branch_ref, hidden_ref, start_ref, out_ref, gout_ref, dout_ref, square_ref = rest[3:11]
    drive_ref, read_ref, acc_ref, cdiag_ref = rest[11:]
    piece = groups * 8
    width = tiles * LANES
    states = b_ref.shape[2]
    i = pl.program_id(0)
    head = s_ref[0:HEAD, :].astype(F32)

    @pl.when(i == 0)
    def maps():
        values = diagonal_maps(proj_ref, proj_ref.shape[1] - states, states)
        cdiag_ref[...] = values.reshape(cdiag_ref.shape)

    for h in range(2):
        drive_ref[h] = step_ref[h] * xs_ref[h].astype(F32).reshape(groups, 8, width)
    rate2 = -jnp.exp(s_ref[80 : 80 + states, :].astype(F32)) * LOG2E
    rates = [rate2[:, tile_cols(j)] for j in range(tiles)]
    held = []
    for h in range(2):
        logs = span_logs(ends, plan_ref, h, ctx, states)
        for j in range(tiles):
            held.append(carried(ends, logs, rates[j], h, ctx, states, tile_cols(j)))
            start_ref[h, :, tile_cols(j)] = held[-1]

    def scan(t, held):
        held = list(held)
        for s in range(16):
            p = t * 16 + s
            for h in range(2):
                b = b_ref[h, p]
                for j in range(tiles):
                    cols = tile_cols(j)
                    step = step_ref[h, t * 2 + s // 8, s % 8 : s % 8 + 1, cols]
                    drive = drive_ref[h, t * 2 + s // 8, s % 8 : s % 8 + 1, cols]
                    k = h * tiles + j
                    held[k] = jnp.exp2(step * rates[j]) * held[k] + drive * b
                    hidden_ref[j, h, p] = held[k].astype(BF16)
        return tuple(held)

    def read(t):
        for h in range(2):
            for j in range(tiles):
                low = hidden_ref[j, h, pl.ds(t * 16, 16)].reshape(16 * states, LANES)
                out = dot(cdiag_ref[h, t], low)
                read_ref[h, t * 2, :, tile_cols(j)] = out[0:8]
                read_ref[h, t * 2 + 1, :, tile_cols(j)] = out[8:16]

    def body(t, held):
        read(t - 1)
        return scan(t, held)

    blocks = groups // 2
    lax.fori_loop(1, blocks, body, scan(0, tuple(held)))
    read(blocks - 1)
    branches = []
    for h in range(2):
        ssm = read_ref[h].reshape(piece, width) + head[6:7] * xs_ref[h].astype(F32)
        ssm_ref[h] = ssm
        gate = gate_ref[h]
        branches.append((ssm * (gate * sigmoid(gate))).astype(BF16))
        branch_ref[h] = branches[-1]
    part = dot(jnp.concatenate(branches, axis=0), weight_ref[...])

    @pl.when(i == 0)
    def first():
        acc_ref[...] = part

    @pl.when(i > 0)
    def later():
        acc_ref[...] += part

    @pl.when(i == pl.num_programs(0) - 1)
    def last():
        row = lax.broadcasted_iota(jnp.int32, (piece, features), 0)
        square = jnp.zeros((8, features), F32)
        for h in range(2):
            rows = slice(h * piece, (h + 1) * piece)
            block_out = tokens_ref[rows, :].astype(F32) + acc_ref[rows, :]
            out_ref[rows, :] = block_out.astype(BF16)
            error = jnp.where(row < scal[1 + h], block_out - teacher_ref[rows, :].astype(F32), 0.0)
            square = square + jnp.sum((error * error).reshape(groups, 8, features), axis=0)
            g_out = error * (2.0 * scale_ref[0, 0])
            gout_ref[rows, :] = g_out
            dout_ref[rows, :] = g_out.astype(BF16)
        square_ref[...] = square


def first_grad_kernel(
    scal, dout_ref, weight_ref, s_ref, step_ref, xs_ref, gate_ref, ssm_ref, c_ref,
    dssm_ref, dgate_ref, skip_ref, grad_ref, *, tiles, groups
):
    piece = groups * 8
    width = tiles * LANES
    states = c_ref.shape[2]
    d_branch = back_dot(dout_ref[...], weight_ref[...])
    skip = jnp.zeros((1, width), F32)
    for h in range(2):
        grad = d_branch[h * piece : (h + 1) * piece]
        gate = gate_ref[h]
        sig = sigmoid(gate)
        d_ssm = grad * (gate * sig)
        dgate_ref[h] = (grad * ssm_ref[h] * (sig * (1.0 + gate * (1.0 - sig)))).astype(BF16)
        skip = skip + jnp.sum(d_ssm * xs_ref[h].astype(F32), axis=0, keepdims=True)
        dssm_ref[h] = d_ssm.reshape(groups, 8, width)
    skip_ref[...] = skip
    rate2 = -jnp.exp(s_ref[80 : 80 + states, :].astype(F32)) * LOG2E
    rates = [rate2[:, tile_cols(j)] for j in range(tiles)]

    def body(i, held):
        held = list(held)
        t = groups - 1 - i
        for s in range(7, -1, -1):
            for h in range(2):
                c = c_ref[h, t * 8 + s]
                for j in range(tiles):
                    step = step_ref[h, t, s : s + 1, tile_cols(j)]
                    dssm = dssm_ref[h, t, s : s + 1, tile_cols(j)]
                    k = h * tiles + j
                    held[k] = jnp.exp2(step * rates[j]) * (held[k] + dssm * c)
        return tuple(held)

    zero = jnp.zeros((states, LANES), F32)
    held = lax.fori_loop(0, groups, body, (zero,) * (2 * tiles))
    for h in range(2):
        for j in range(tiles):
            grad_ref[h * states : (h + 1) * states, tile_cols(j)] = held[h * tiles + j].astype(BF16)


def out_grad_kernel(even_ref, odd_ref, dout_ref, keep_ref, send_ref):
    keep_ref[0] = rows_dot(even_ref[...], dout_ref[...]).astype(BF16)
    send_ref[0] = rows_dot(odd_ref[...], dout_ref[...]).astype(BF16)


def gate_grad_kernel(scal, normed_ref, dgate_ref, *refs, count, piece):
    weights, (keep_ref, send_ref, dnormed_ref) = refs[:count], refs[count:]
    depth = weights[0].shape[0]
    width = weights[0].shape[1]
    own = jnp.concatenate(
        [normed_ref[HALO : HALO + piece], normed_ref[2 * HALO + piece : 2 * HALO + 2 * piece]], axis=0
    )
    d_gate = dgate_ref[...].reshape(2 * piece, width)

    @pl.when(pl.program_id(0) == 0)
    def clear():
        dnormed_ref[...] = jnp.zeros_like(dnormed_ref)

    for r in range(count):
        cols = slice(r * depth, (r + 1) * depth)
        target = send_ref if r % 2 else keep_ref
        target[r // 2] = rows_dot(own[:, cols], d_gate).astype(BF16)
        back = back_dot(d_gate, weights[r][...])
        for h in range(2):
            rows = slice(h * (HALO + piece) + HALO, (h + 1) * (HALO + piece))
            dnormed_ref[rows, cols] += back[h * piece : (h + 1) * piece]


def backward_kernel(scal, *refs, tiles, groups, ctx, rank):
    grads = refs[: ctx - 1]
    ends = refs[ctx - 1 : 2 * ctx - 2]
    (
        plan_ref, proj_ref, s_ref, step_ref, xs_ref, c_ref, start_ref, dssm_ref, hidden_ref,
        dxs_ref, small_ref, ddelta_ref, db_ref, dc_ref,
        adj_ref, dstep_ref, dbs_ref, dcs_ref, bdiag_ref,
    ) = refs[2 * ctx - 2 :]
    piece = groups * 8
    width = tiles * LANES
    states = c_ref.shape[2]
    blocks = groups // 2
    i = pl.program_id(0)
    head = s_ref[0:HEAD, :].astype(F32)

    @pl.when(i == 0)
    def clear():
        dbs_ref[...] = jnp.zeros_like(dbs_ref)
        dcs_ref[...] = jnp.zeros_like(dcs_ref)
        bdiag_ref[...] = diagonal_maps(proj_ref, rank, states).reshape(bdiag_ref.shape)
        ddelta_ref[...] = jnp.zeros_like(ddelta_ref)

    rate = -jnp.exp(s_ref[80 : 80 + states, :].astype(F32))
    rates = [rate[:, tile_cols(j)] for j in range(tiles)]
    rates2 = [values * LOG2E for values in rates]
    row16 = lax.broadcasted_iota(jnp.int32, (16, 16 * states), 0)
    col16 = lax.broadcasted_iota(jnp.int32, (16, 16 * states), 1)
    same = (col16 // states == row16).astype(F32)
    same_low = same.astype(BF16)

    def work(t, first, later, sums):
        for h in range(2):
            adjoints = [[None] * 16 for _ in range(tiles)]
            terms = [[None] * 16 for _ in range(tiles)]
            for s in range(15, -1, -1):
                p = t * 16 + s
                c = c_ref[h, p]
                for j in range(tiles):
                    cols = tile_cols(j)
                    step = step_ref[h, t * 2 + s // 8, s % 8 : s % 8 + 1, cols]
                    dssm = dssm_ref[h, t * 2 + s // 8, s % 8 : s % 8 + 1, cols]
                    k = h * tiles + j
                    if first and s == 0:
                        before = start_ref[h, :, cols]
                    else:
                        before = hidden_ref[j, h, p - 1].astype(F32)
                    adjoint = dssm * c + later[k]
                    later[k] = jnp.exp2(step * rates2[j]) * adjoint
                    term = later[k] * before
                    sums[j] = sums[j] + term * step
                    adjoints[j][s] = adjoint.astype(BF16)
                    terms[j][s] = (term * rates[j]).astype(BF16)
            db = dc = None
            for j in range(tiles):
                cols = tile_cols(j)
                adjoint = jnp.concatenate(adjoints[j], axis=0)
                out = dot(bdiag_ref[h, t], adjoint)
                adj_ref[h, t * 2, :, cols] = out[0:8]
                adj_ref[h, t * 2 + 1, :, cols] = out[8:16]
                out = dot(same_low, jnp.concatenate(terms[j], axis=0))
                dstep_ref[h, t * 2, :, cols] = out[0:8]
                dstep_ref[h, t * 2 + 1, :, cols] = out[8:16]
                step = step_ref[h, pl.ds(t * 2, 2), :, cols].reshape(16, LANES)
                dssm = dssm_ref[h, pl.ds(t * 2, 2), :, cols].reshape(16, LANES)
                drive = (step * xs_ref[h, pl.ds(t * 16, 16), cols].astype(F32)).astype(BF16)
                hidden = hidden_ref[j, h, pl.ds(t * 16, 16)].reshape(16 * states, LANES)
                db_now = back_dot(drive, adjoint)
                dc_now = back_dot(dssm.astype(BF16), hidden)
                db = db_now if db is None else db + db_now
                dc = dc_now if dc is None else dc + dc_now
            dbs_ref[h, t] += db
            dcs_ref[h, t] += dc

    def body(k, both):
        later, sums = list(both[: 2 * tiles]), list(both[2 * tiles :])
        work(blocks - 1 - k, False, later, sums)
        return tuple(later + sums)

    later = []
    for h in range(2):
        logs = span_logs(ends, plan_ref, h, ctx, states)
        for j in range(tiles):
            later.append(carried(grads, logs, rates2[j], h, ctx, states, tile_cols(j)))
    sums = [jnp.zeros((states, LANES), F32)] * tiles
    both = lax.fori_loop(0, blocks - 1, body, tuple(later + sums))
    later, sums = list(both[: 2 * tiles]), list(both[2 * tiles :])
    work(0, True, later, sums)
    for j in range(tiles):
        small_ref[rank : rank + states, tile_cols(j)] = sums[j] * rates[j]
    delta = proj_ref[:, 0:rank].astype(BF16)
    pre = dot(delta, s_ref[HEAD : HEAD + rank, :]) + head[5:6]
    row = lax.broadcasted_iota(jnp.int32, (piece, width), 0)
    lows = []
    bias = jnp.zeros((1, width), F32)
    for h in range(2):
        xs = xs_ref[h].astype(F32)
        adj = adj_ref[h].reshape(piece, width)
        d_step = xs * adj + dstep_ref[h].reshape(piece, width)
        d_pre = jnp.where(row < scal[1 + h], d_step * sigmoid(pre[h * piece : (h + 1) * piece]), 0.0)
        bias = bias + jnp.sum(d_pre, axis=0, keepdims=True)
        lows.append(d_pre.astype(BF16))
        dxs_ref[h] = head[6:7] * dssm_ref[h].reshape(piece, width) + step_ref[h].reshape(piece, width) * adj
    small_ref[rank + states : rank + states + 8, :] = jnp.broadcast_to(bias, (8, width))
    low = jnp.concatenate(lows, axis=0)
    small_ref[0:rank, :] = rows_dot(delta, low)
    ddelta_ref[...] += back_dot(low, s_ref[HEAD : HEAD + rank, :])

    @pl.when(i == pl.num_programs(0) - 1)
    def last():
        for h in range(2):
            for t in range(blocks):
                db_ref[h, t : t + 1, :] = jnp.sum(dbs_ref[h, t] * same, axis=0, keepdims=True)
                dc_ref[h, t : t + 1, :] = jnp.sum(dcs_ref[h, t] * same, axis=0, keepdims=True)


def tail_kernel(
    scal, dproj_ref, s_ref, dxs_ref, conv_ref, x_ref, xs_ref, normed_ref, before_ref, *refs,
    count, piece
):
    weights, (small_ref, keep_ref, send_ref, dnormed_ref, pad_ref) = refs[:count], refs[count:]
    depth = weights[0].shape[0]
    width = weights[0].shape[1]
    ext = HALO + piece

    @pl.when(pl.program_id(0) == 0)
    def clear():
        dnormed_ref[...] = before_ref[...]
        for h in range(2):
            pad_ref[h, 0:HALO, :] = jnp.zeros((HALO, width), F32)
            pad_ref[h, ext : ext + 8, :] = jnp.zeros((8, width), F32)

    head = s_ref[0:HEAD, :].astype(F32)
    small_ref[8:104, :] = rows_dot(dproj_ref[...], xs_ref[...].reshape(2 * piece, width))
    d_xs = dot(dproj_ref[...], s_ref[96:192, :])
    taps = [jnp.zeros((1, width), F32) for _ in range(5)]
    lows = []
    for h in range(2):
        conv = conv_ref[h]
        sig = sigmoid(conv)
        d_conv = (dxs_ref[h] + d_xs[h * piece : (h + 1) * piece]) * (sig * (1.0 + conv * (1.0 - sig)))
        pad_ref[h, HALO:ext, :] = d_conv
        x = x_ref[h].astype(F32)
        for k in range(4):
            rows = slice(HALO - 3 + k, HALO - 3 + k + piece)
            taps[k] = taps[k] + jnp.sum(d_conv * x[rows], axis=0, keepdims=True)
        taps[4] = taps[4] + jnp.sum(d_conv, axis=0, keepdims=True)
        d_x = head[3:4] * pad_ref[h, 0:ext, :]
        for k in range(3):
            d_x = d_x + head[k : k + 1] * pad_ref[h, 3 - k : 3 - k + ext, :]
        lows.append(d_x.astype(BF16))
    small_ref[0:8, :] = jnp.concatenate(taps + [jnp.zeros((3, width), F32)], axis=0)
    low = jnp.concatenate(lows, axis=0)
    for r in range(count):
        cols = slice(r * depth, (r + 1) * depth)
        target = send_ref if r % 2 else keep_ref
        target[r // 2] = rows_dot(normed_ref[:, cols], low).astype(BF16)
        dnormed_ref[:, cols] += back_dot(low, weights[r][...])


def shape(dims, dtype=F32):
    return jax.ShapeDtypeStruct(dims, dtype)


def call(kernel, name, grid, scal, args, in_specs, out_specs, out_shape, scratch, flops, exps=0):
    size = sum(a.size * a.dtype.itemsize for a in args) + sum(
        s.size * s.dtype.itemsize for s in out_shape
    )
    return pl.pallas_call(
        kernel,
        grid_spec=pltpu.PrefetchScalarGridSpec(
            num_scalar_prefetch=1,
            grid=(grid,),
            in_specs=in_specs,
            out_specs=out_specs,
            scratch_shapes=scratch,
        ),
        out_shape=out_shape,
        name=name,
        compiler_params=pltpu.CompilerParams(vmem_limit_bytes=LIMITS[name] * 2**20),
        cost_estimate=pl.CostEstimate(flops=flops, bytes_accessed=size, transcendentals=exps),
    )(scal, *args)


def whole_spec(dims):
    return pl.BlockSpec(dims, lambda i, scal: (0,) * len(dims))


def local(
    tokens,
    teacher,
    lengths,
    pair_owner,
    norm_gain,
    in_proj,
    conv_weight,
    conv_bias,
    x_proj,
    dt_proj,
    dt_bias,
    a_log,
    skip_scale,
    out_proj,
):
    ctx = lax.axis_size("ctx")
    fsdp = lax.axis_size("fsdp")
    me_ctx = lax.axis_index("ctx")
    me_fsdp = lax.axis_index("fsdp")
    piece = tokens.shape[1] // 2
    features = tokens.shape[2]
    width = in_proj.shape[1] // 2
    rank = dt_proj.shape[0]
    states = a_log.shape[0]
    groups = piece // 8
    ext = HALO + piece
    depth = features // fsdp
    part = width // fsdp
    rows_all = 2 * piece
    elements = rows_all * states * width

    relative = jnp.arange(ctx, dtype=jnp.int32) ^ me_ctx
    pair_of = jnp.sum(
        jnp.arange(ctx, dtype=jnp.int32)[None, :]
        * (pair_owner[None, :] == relative[:, None]).astype(jnp.int32),
        axis=1,
    )
    places = jnp.stack([pair_of, ctx - 1 - pair_of])
    pair_id = pair_of[0]
    own = places[:, 0]
    limits = jnp.clip(lengths[0] - own * piece, 0, piece)
    scal = jnp.concatenate([me_fsdp[None], limits]).astype(jnp.int32)
    between = (places[:, :, None] < places[:, None, :]) & (
        places[:, None, :] < own[:, None, None]
    )
    between_back = (places[:, :, None] > places[:, None, :]) & (
        places[:, None, :] > own[:, None, None]
    )
    before = places < own[:, None]
    behind = places > own[:, None]
    has_before = jnp.stack([pair_id > 0, pair_id < ctx - 1])
    has_after = jnp.stack([pair_id < ctx - 1, pair_id > 0])
    lower_owner = pair_owner[jnp.maximum(pair_id - 1, 0)]
    upper_owner = pair_owner[jnp.minimum(pair_id + 1, ctx - 1)]
    lower, upper = lower_owner ^ me_ctx, upper_owner ^ me_ctx

    def plan_of(inside, wanted):
        inside = jnp.pad(inside.astype(F32), ((0, 0), (0, 0), (0, LANES - ctx)))
        outside = jnp.broadcast_to(jnp.where(wanted, 0.0, 1e30)[..., None], (2, ctx, LANES))
        return jnp.concatenate([inside, outside], axis=0).reshape(4 * ctx, LANES).astype(F32)

    plan_before = plan_of(between, before)
    plan_behind = plan_of(between_back, behind)

    def to_blocks(values, size):
        axis = values.ndim - 1
        return jnp.concatenate(
            [
                lax.dynamic_slice_in_dim(values, (me_fsdp ^ r) * size, size, axis=axis)
                for r in range(fsdp)
            ],
            axis=axis,
        )

    own_rows = tokens[0]
    valid_slots = jnp.minimum(lengths[0], 2 * ctx * piece)
    coded = jnp.concatenate([valid_slots // 128, valid_slots % 128]).astype(BF16)[None]
    rows_head = jnp.concatenate(
        [
            conv_weight,
            conv_bias[None],
            dt_bias[None],
            skip_scale[None],
            jnp.pad(norm_gain, (0, part - depth))[None],
            jnp.pad(coded, ((0, 0), (0, part - 4))),
            jnp.zeros((HEAD - 9, part), BF16),
            dt_proj,
            a_log,
            x_proj.T,
        ],
        axis=0,
    )
    half = width // 2
    to_send = in_proj[:, :half]
    x_far = [to_send] + [swap(to_send, "fsdp", bit) for bit in range(2, fsdp, 2)]
    last_rows = to_blocks(own_rows.reshape(2, piece, features)[:, piece - 3 :], depth)
    last_rows = jnp.broadcast_to(last_rows[None], (ctx, 2, 3, features))
    token_rel = to_blocks(own_rows, depth).reshape(2, piece, features)
    tails = lax.all_to_all(last_rows, "ctx", 0, 0)
    x_far, second, rows_head, tails, token_rel, scal, plan_before, plan_behind = together(
        x_far, in_proj[:, half:width], rows_head, tails, token_rel, scal, plan_before, plan_behind
    )
    x_first = [block for own in x_far for block in (own, swap(own, "fsdp", 1))]
    small_blocks = gather_fsdp(rows_head)
    small = jnp.concatenate(small_blocks, axis=1)
    gain = jnp.concatenate([block[7, :depth] for block in small_blocks]).astype(F32)
    x_second = gather_fsdp(second)

    before_rows = jnp.stack([tails[lower_owner, 0], tails[upper_owner, 1]])
    before_rows = jnp.where(has_before[:, None, None], before_rows, jnp.zeros_like(before_rows))
    rows_ext = jnp.concatenate(
        [jnp.zeros((2, HALO - 3, features), BF16), before_rows, token_rel], axis=1
    ).astype(F32)
    inv_rms = lax.rsqrt(jnp.mean(rows_ext * rows_ext, axis=2, keepdims=True) + EPSILON)
    normed = (rows_ext * inv_rms * gain).astype(BF16).reshape(2 * ext, features)

    codes = jnp.stack([block[8, :4] for block in small_blocks]).astype(F32)
    count = jnp.sum(codes[:, 0:2] * 128.0 + codes[:, 2:4])
    scale = ((fsdp * rows_all * ctx) / count).reshape(1, 1)

    def cols_at(block):
        per = part // block
        return lambda i, scal: (0, (scal[0] ^ (i // per)) * per + i % per)

    def spec_small(block, offset=0):
        return pl.BlockSpec((small.shape[0], block), lambda i, scal: (0, i + offset))

    def spec_rows(block, offset=0):
        return pl.BlockSpec((2, piece, block), lambda i, scal: (0, 0, i + offset))

    def spec_groups(block):
        return pl.BlockSpec((2, groups, 8, block), lambda i, scal: (0, 0, 0, i))

    cb = min(256, part)
    steps = width // cb
    weight_specs = [pl.BlockSpec((depth, cb), cols_at(cb)) for _ in range(fsdp)]
    half_blocks = half // cb

    def upper_place(i, scal):
        return cols_at(cb)(i, scal)[1] >= half_blocks

    low_spec = pl.BlockSpec(
        (depth, cb), lambda i, scal: (0, jnp.minimum(cols_at(cb)(i, scal)[1], half_blocks - 1))
    )
    high_spec = pl.BlockSpec(
        (depth, cb), lambda i, scal: (0, jnp.maximum(cols_at(cb)(i, scal)[1] - half_blocks, 0))
    )
    x_ext, conv, xs, proj = call(
        functools.partial(input_kernel, count=fsdp, piece=piece, is_upper=upper_place),
        "inputs", steps, scal, (normed, *x_first, *x_second, small),
        [whole_spec((2 * ext, features)), *([low_spec] * fsdp), *([high_spec] * fsdp), spec_small(cb)],
        [
            pl.BlockSpec((2, ext, cb), lambda i, scal: (0, 0, i)),
            spec_rows(cb),
            spec_rows(cb),
            whole_spec((rows_all, rank + 2 * states)),
        ],
        [
            shape((2, ext, width), BF16),
            shape((2, piece, width)),
            shape((2, piece, width), BF16),
            shape((rows_all, rank + 2 * states)),
        ],
        [pltpu.VMEM((2 * ext, cb), F32)], 2 * rows_all * features * width,
    )
    gate_first = after(in_proj[:, width:], x_second[fsdp // 2])
    gate_far = [gate_first] + [swap(gate_first, "fsdp", bit) for bit in range(2, fsdp, 2)]
    gate_far, proj = together(gate_far, proj)
    gate_blocks = [block for own in gate_far for block in (own, swap(own, "fsdp", 1))]
    out_first = after(out_proj, gate_far[-1])
    out_far = [out_first] + [swap(out_first, "fsdp", bit) for bit in range(2, fsdp, 2)]
    wide_dims = (2, piece, states, LANES)
    maps = proj[:, rank:].reshape(2, piece, 2 * states, 1)
    b_wide = jnp.broadcast_to(maps[:, :, :states], wide_dims)

    tiles = 4
    block = tiles * LANES
    per_half = half // block
    group_spec = spec_groups(block)
    state_row = pl.BlockSpec((2 * states, block), lambda i, scal: (0, i))
    sent_row = pl.BlockSpec((2 * states + 8, block), lambda i, scal: (0, i))
    plan_spec = whole_spec((4 * ctx, LANES))
    row_spec = whole_spec((rows_all, features))
    wide_spec = whole_spec(wide_dims)
    diag_space = pltpu.VMEM((2, piece // 16, 16, 16 * states), BF16)
    hidden_spec = pl.BlockSpec((tiles, 2, piece, states, LANES), lambda i, scal: (i, 0, 0, 0, 0))
    start_spec = pl.BlockSpec((2, states, block), lambda i, scal: (0, 0, i))
    group_space = pltpu.VMEM((2, groups, 8, block), F32)

    step, sent = call(
        functools.partial(end_kernel, tiles=tiles, groups=groups, rank=rank),
        "end_states", width // block, scal, (proj, small, xs, b_wide),
        [whole_spec(proj.shape), spec_small(block), spec_rows(block), wide_spec],
        [group_spec, pl.BlockSpec((2 * states + 8, block), lambda i, scal: (0, i))],
        [shape((2, groups, 8, width)), shape((2 * states + 8, width), BF16)],
        [group_space], 5 * elements, elements,
    )

    far = gather_far(sent)
    (gate,) = call(
        functools.partial(gate_kernel, count=fsdp, piece=piece),
        "gates", steps, scal, (normed, *gate_blocks),
        [whole_spec((2 * ext, features)), *weight_specs], [spec_rows(cb)],
        [shape((2, piece, width))], [], 2 * rows_all * features * width,
    )
    c_wide = jnp.broadcast_to(maps[:, :, states:], wide_dims)
    far, gate, out_far = together(far, gate, out_far)
    near, c_wide = gather_near(far, c_wide)
    out_blocks = [block for own in out_far for block in (own, swap(own, "fsdp", 1))]
    weight_out = jnp.concatenate(out_blocks, axis=0)
    near, weight_out = together(near, weight_out)
    ssm, branch, hidden, starts, out_low, g_out, d_out, squares = call(
        functools.partial(forward_kernel, tiles=tiles, groups=groups, ctx=ctx, features=features),
        "forward_states", width // block, scal,
        (*near[1:], plan_before, small, step, xs, gate, b_wide, proj, weight_out,
         scale, own_rows, teacher[0]),
        [
            *([sent_row] * (ctx - 1)), plan_spec, spec_small(block), group_spec, spec_rows(block),
            spec_rows(block), wide_spec, whole_spec(proj.shape),
            pl.BlockSpec((block, features), lambda i, scal: (i, 0)),
            pl.BlockSpec(memory_space=pltpu.SMEM), row_spec, row_spec,
        ],
        [
            spec_rows(block), spec_rows(block), hidden_spec, start_spec, row_spec, row_spec, row_spec,
            whole_spec((8, features)),
        ],
        [
            shape((2, piece, width)),
            shape((2, piece, width), BF16),
            shape((width // LANES, 2, piece, states, LANES), BF16),
            shape((2, states, width)),
            shape((rows_all, features), BF16),
            shape((rows_all, features)),
            shape((rows_all, features), BF16),
            shape((8, features)),
        ],
        [group_space] * 2 + [pltpu.VMEM((rows_all, features), F32), diag_space],
        10 * elements, elements,
    )
    d_ssm, d_gate, grad_skip, grads_first = call(
        functools.partial(first_grad_kernel, tiles=tiles, groups=groups),
        "first_grads", width // block, scal,
        (d_out, weight_out, small, step, xs, gate, ssm, c_wide),
        [
            row_spec, pl.BlockSpec((block, features), lambda i, scal: (i, 0)), spec_small(block),
            group_spec, spec_rows(block), spec_rows(block), spec_rows(block), wide_spec,
        ],
        [group_spec, spec_rows(block), pl.BlockSpec((1, block), lambda i, scal: (0, i)), state_row],
        [
            shape((2, groups, 8, width)),
            shape((2, piece, width), BF16),
            shape((1, width)),
            shape((2 * states, width), BF16),
        ],
        [], 6 * elements, elements,
    )
    back_far = gather_far(grads_first)

    pairs = fsdp // 2
    pair_spec = pl.BlockSpec((pairs, depth, cb), lambda i, scal: (0, 0, i))
    pair_at = pl.BlockSpec((pairs, depth, cb), lambda i, scal: (0, 0, cols_at(cb)(i, scal)[1]))
    keep_gate, send_gate, d_normed_gate = call(
        functools.partial(gate_grad_kernel, count=fsdp, piece=piece),
        "gate_grads", steps, scal, (normed, d_gate, *gate_blocks),
        [whole_spec((2 * ext, features)), spec_rows(cb), *weight_specs],
        [pair_at, pair_at, whole_spec((2 * ext, features))],
        [shape((pairs, depth, width), BF16)] * 2 + [shape((2 * ext, features))],
        [], 4 * rows_all * features * width,
    )
    subs = part // cb
    branch_rows = branch.reshape(rows_all, width)
    keep_out, send_out = pl.pallas_call(
        out_grad_kernel,
        grid=(pairs, subs),
        in_specs=[
            pl.BlockSpec((rows_all, cb), lambda k, s: (0, 2 * k * subs + s)),
            pl.BlockSpec((rows_all, cb), lambda k, s: (0, (2 * k + 1) * subs + s)),
            pl.BlockSpec((rows_all, features), lambda k, s: (0, 0)),
        ],
        out_specs=[pl.BlockSpec((1, cb, features), lambda k, s: (k, s, 0))] * 2,
        out_shape=[shape((pairs, part, features), BF16)] * 2,
        name="out_grads",
        compiler_params=pltpu.CompilerParams(vmem_limit_bytes=VMEM_LIMIT),
        cost_estimate=pl.CostEstimate(
            flops=2 * rows_all * width * features, bytes_accessed=9 * 2**20, transcendentals=0
        ),
    )(branch_rows, branch_rows, d_out)
    back_far, keep_gate, send_gate, keep_out, send_out = together(
        back_far, keep_gate, send_gate, keep_out, send_out
    )
    back_near, _ = gather_near(back_far)
    core_gate = (keep_gate, swap(send_gate, "fsdp", 1))
    core_out = (keep_out, swap(send_out, "fsdp", 1))
    out_steps, gate_steps = reduce_steps(False), reduce_steps(True, 1)
    out_ready, gate_ready = out_steps[0][0](core_out), gate_steps[0][0](core_gate)
    back_near, out_ready, gate_ready = together(back_near, out_ready, gate_ready)
    out_steps[0] = (lambda values: values, *out_steps[0][1:])
    gate_steps[0] = (lambda values: values, *gate_steps[0][1:])
    chains = [(out_steps, out_ready), (gate_steps, gate_ready)]

    def backward():
        def at(i):
            return i

        return call(
            functools.partial(backward_kernel, tiles=tiles, groups=groups, ctx=ctx, rank=rank),
            "backward_states", width // block, scal,
            (*back_near[1:], *near[1:], plan_behind, proj, small, step, xs, c_wide, starts, d_ssm, hidden),
            [
                *([pl.BlockSpec((2 * states, block), lambda i, scal: (0, at(i)))] * (ctx - 1)),
                *([pl.BlockSpec((2 * states + 8, block), lambda i, scal: (0, at(i)))] * (ctx - 1)),
                plan_spec,
                whole_spec(proj.shape), spec_small(block),
                pl.BlockSpec((2, groups, 8, block), lambda i, scal: (0, 0, 0, at(i))),
                spec_rows(block), wide_spec,
                pl.BlockSpec((2, states, block), lambda i, scal: (0, 0, at(i))),
                pl.BlockSpec((2, groups, 8, block), lambda i, scal: (0, 0, 0, at(i))),
                pl.BlockSpec((tiles, 2, piece, states, LANES), lambda i, scal: (at(i), 0, 0, 0, 0)),
            ],
            [
                spec_rows(block), pl.BlockSpec((rank + states + 8, block), lambda i, scal: (0, i)),
                whole_spec((rows_all, rank)),
                whole_spec((2, piece // 16, 16 * states)), whole_spec((2, piece // 16, 16 * states)),
            ],
            [
                shape((2, piece, width)),
                shape((rank + states + 8, width)),
                shape((rows_all, rank)),
                shape((2, piece // 16, 16 * states)),
                shape((2, piece // 16, 16 * states)),
            ],
            [group_space] * 2 + [pltpu.VMEM((2, piece // 16, 16, 16 * states), F32)] * 2 + [diag_space],
            16 * elements, elements,
        )

    chains, back = advance(chains, backward())

    small_rows = jnp.concatenate(
        [back[1], grad_skip, jnp.zeros((7, width), F32)], axis=0
    ).astype(BF16)
    d_proj = jnp.concatenate(
        [back[2], back[3].reshape(rows_all, states), back[4].reshape(rows_all, states)], axis=1
    ).astype(BF16)
    half_steps = steps // 2

    def tail(c, d_proj, d_before):
        base = c * half_steps

        def place(i, scal):
            return cols_at(cb)(i + base, scal)[1]

        def at_rows(dims):
            return pl.BlockSpec((2, dims, cb), lambda i, scal: (0, 0, place(i, scal)))

        return call(
            functools.partial(tail_kernel, count=fsdp, piece=piece),
            "tail_grads", half_steps, scal,
            (d_proj, small, back[0], conv, x_ext, xs, normed, d_before,
             *(x_second if c else x_first)),
            [
                whole_spec(d_proj.shape),
                pl.BlockSpec((small.shape[0], cb), lambda i, scal: (0, place(i, scal))),
                at_rows(piece), at_rows(piece), at_rows(ext), at_rows(piece),
                whole_spec((2 * ext, features)), whole_spec((2 * ext, features)),
                *([pl.BlockSpec((depth, cb), lambda i, scal: (0, i))] * fsdp),
            ],
            [
                pl.BlockSpec((104, cb), lambda i, scal: (0, i)),
                pair_spec, pair_spec, whole_spec((2 * ext, features)),
            ],
            [
                shape((104, half)),
                shape((pairs, depth, half), BF16),
                shape((pairs, depth, half), BF16),
                shape((2 * ext, features)),
            ],
            [pltpu.VMEM((2, ext + 8, cb), F32)],
            4 * rows_all * features * half,
        )

    d_before = d_normed_gate
    d_proj, d_before, _ = together(d_proj, d_before, [values for _, values in chains])
    chains, tail_first = advance(chains, tail(0, d_proj, d_before))
    got_ahead = swap(tail_first[2], "fsdp", 1)
    small_now = [small_rows[:, k * part : (k + 1) * part] for k in range(fsdp)]
    for small_now in fsdp_blocks(small_now):
        pass
    d_proj, _ = together(d_proj, [values for _, values in chains])
    chains, (tail_second, got_ahead, small_now) = advance(
        chains, (tail(1, d_proj, tail_first[3]), got_ahead, small_now)
    )
    ahead = (tail_first[1], got_ahead)
    def halo_start(d_ext, squares):
        d_normed = d_ext.reshape(2, ext, features)
        unit = rows_ext * inv_rms
        grad_gain = jnp.sum(d_normed[:, HALO - 3 :] * unit[:, HALO - 3 :], axis=(0, 1))
        square = jnp.pad(jnp.stack(three_parts(jnp.sum(squares))), (0, features - 3))
        halo_rows = d_normed[:, HALO - 3 : HALO].reshape(6, features)
        return jnp.concatenate(
            [halo_rows.astype(BF16), square[None], grad_gain.astype(BF16)[None]]
        )[None]

    def halo_vector(halo_got):
        return jnp.concatenate(
            [
                to_blocks(jnp.sum(halo_got[:, 7], axis=0)[None], depth)[0],
                jnp.pad(jnp.sum(halo_got[:, 6, 0:3])[None], (0, LANES - 1)),
            ]
        )

    tail_rows = [
        values[:, k * part : (k + 1) * part].astype(BF16)
        for values in (tail_first[0], tail_second[0])
        for k in range(fsdp // 2)
    ]
    lines = small_now[0].shape[0] // 2
    lines_tail = tail_rows[0].shape[0] // 2
    got_last = swap(tail_second[2], "fsdp", 1)
    lead = [(reduce_steps(True), ahead)]
    lead, (got_last, d_ext, squares) = advance(lead, (got_last, tail_second[3], squares))
    chains = chains + lead
    last = (tail_second[1], got_last)
    last_steps = reduce_steps(False)
    n_fsdp = len(bits_of(fsdp)) - 1
    for bit in bits_of(fsdp):
        tail_rows = fsdp_selected(tail_rows, bit)
    for_halo = None
    halo_steps = [gather_step(bit) for bit in bits_of(ctx)]
    sum_steps = [sum_step(bit) for bit in bits_of(fsdp)]
    while last_steps:
        for_last = [([last_steps.pop(0)], last)]
        more = [(halo_steps or sum_steps, for_halo)] if for_halo is not None else []
        chains, tail_rows = advance([*for_last, *chains, *more], tail_rows)
        last = chains.pop(0)[1]
        if more:
            for_halo = chains.pop()[1]
            if not halo_steps and halo_got is None:
                halo_got = for_halo.astype(F32)
                for_halo = halo_vector(halo_got)
        n_fsdp -= 1
        if n_fsdp == 0:
            extra = jnp.concatenate(
                [
                    side_by_side(small_now[0], lines),
                    side_by_side(tail_rows[0], lines_tail),
                    jnp.zeros((128 - lines - lines_tail, 2 * part), BF16),
                ],
                axis=0,
            ).reshape(1, -1, half)
            last = jnp.concatenate([part_of(last, lambda v: v), extra], axis=1)
        if n_fsdp == -1:
            last, d_ext, squares = together(last, d_ext, squares)
            for_halo, halo_got = halo_start(d_ext, squares), None
    while any(steps_left for steps_left, _ in chains):
        chains, _ = advance(chains)
    while halo_steps or sum_steps:
        [(_, for_halo)], _ = advance([(halo_steps or sum_steps, for_halo)])
        if not halo_steps and halo_got is None:
            halo_got = for_halo.astype(F32)
            for_halo = halo_vector(halo_got)
    vector = for_halo
    out_now, gate_now, ahead = [values for _, values in chains]
    sum_x = [ahead[0], last[0, :depth]]
    extra = last[0, depth:].reshape(128, 2 * part)
    sum_back = one_above(extra[:lines], part).astype(F32)
    sum_tail = one_above(extra[lines : lines + lines_tail], part).astype(F32)

    d_normed = d_ext.reshape(2, ext, features)
    sum_gain = lax.dynamic_slice_in_dim(vector, me_fsdp * depth, depth)
    loss = vector[features] / (count * features)
    halo_all = halo_got[:, 0:6].reshape(ctx, 2, 3, features)
    from_next = jnp.stack([halo_all[upper, 0], halo_all[lower, 1]])
    from_next = jnp.where(has_after[:, None, None], from_next, 0.0)
    own_normed = d_normed[:, HALO:] + jnp.pad(from_next, ((0, 0), (piece - 3, 0), (0, 0)))
    own_inv = inv_rms[:, HALO:]
    own_u = rows_ext[:, HALO:]
    scaled = own_normed * gain
    d_rows = own_inv * scaled - own_u * (own_inv * own_inv * own_inv) * jnp.mean(
        scaled * own_u, axis=2, keepdims=True
    )
    grad_tokens = (to_blocks(d_rows.reshape(rows_all, features), depth) + g_out)[None]
    grad_in = jnp.concatenate([*sum_x, gate_now[0]], axis=1).astype(F32)
    return (
        out_low[None],
        loss,
        grad_tokens,
        sum_gain,
        grad_in,
        sum_tail[0:4],
        sum_tail[4],
        sum_tail[8:104].T,
        sum_back[0:rank],
        sum_back[rank + states],
        sum_back[rank : rank + states],
        sum_back[rank + states + 8],
        out_now[0].astype(F32),
    )


def solution(mesh):
    in_specs = (
        P("fsdp", "ctx", None),
        P("fsdp", "ctx", None),
        P("fsdp", None),
        P(),
        P("fsdp"),
        P("fsdp", None),
        P(None, "fsdp"),
        P("fsdp"),
        P("fsdp", None),
        P(None, "fsdp"),
        P("fsdp"),
        P(None, "fsdp"),
        P("fsdp"),
        P("fsdp", None),
    )
    out_specs = (
        P("fsdp", "ctx", None),
        P(),
        P("fsdp", "ctx", None),
        P("fsdp"),
        P("fsdp", None),
        P(None, "fsdp"),
        P("fsdp"),
        P("fsdp", None),
        P(None, "fsdp"),
        P("fsdp"),
        P(None, "fsdp"),
        P("fsdp"),
        P("fsdp", None),
    )
    return jax.shard_map(local, mesh=mesh, in_specs=in_specs, out_specs=out_specs, check_vma=False)
```

```python
import functools

import jax
import jax.numpy as jnp
from jax import lax
from jax.experimental import pallas as pl
from jax.experimental.pallas import tpu as pltpu
from jax.sharding import PartitionSpec as P

EPSILON = 1e-05
LOG2E = 1.4426950408889634
F32 = jnp.float32
BF16 = jnp.bfloat16
LANES = 128
HALO = 16
HEAD = 16
VMEM_LIMIT = 60 * 1024 * 1024
LIMITS = {
    "inputs": 20,
    "gates": 20,
    "end_states": 28,
    "forward_states": 60,
    "first_grads": 60,
    "gate_grads": 60,
    "backward_states": 60,
    "tail_grads": 60,
}


def swap(values, axis, bit):
    size = lax.axis_size(axis)
    return lax.ppermute(values, axis, [(i, i ^ bit) for i in range(size)])


def after(values, earlier):
    return lax.optimization_barrier((values, earlier))[0]


def bits_of(size):
    return [1 << k for k in range(size.bit_length() - 1)]


def gather_fsdp(values):
    blocks = {0: values}
    for bit in reversed(bits_of(lax.axis_size("fsdp"))):
        for r in sorted(blocks):
            blocks[r | bit] = swap(blocks[r], "fsdp", bit)
    return [blocks[r] for r in range(len(blocks))]


def gather_far(values):
    size = lax.axis_size("ctx")
    return [values] + [swap(values, "ctx", j) for j in range(2, size, 2)]


def gather_near(far, beside=()):
    blocks = [block for own in far[:2] for block in (own, swap(own, "ctx", 1))]
    rest, beside = together(far[2:], beside)
    return blocks + [block for own in rest for block in (own, swap(own, "ctx", 1))], beside


def together(*trees):
    return lax.optimization_barrier(trees)


def gather_small_ctx(values):
    stacked = values[None]
    for bit in bits_of(lax.axis_size("ctx")):
        stacked = jnp.concatenate([stacked, swap(stacked, "ctx", bit)], axis=0)
    return stacked


def three_parts(values):
    high = values.astype(BF16)
    rest = values - high.astype(F32)
    middle = rest.astype(BF16)
    return high, middle, (rest - middle.astype(F32)).astype(BF16)


def total(values, axes):
    for axis in axes:
        for bit in bits_of(lax.axis_size(axis)):
            values = values + swap(values, axis, bit)
    return values


def joined(kept, received):
    return (kept.astype(F32) + received.astype(F32)).astype(BF16)


def part_of(values, take):
    if isinstance(values, tuple):
        return joined(take(values[0]), take(values[1]))
    return take(values)


def pending(own, other):
    return own, other


def fsdp_step(bit):
    def ready(values):
        return part_of(values, lambda v: v[0::2]), part_of(values, lambda v: v[1::2])

    return ready, "fsdp", bit, pending


def scatter_step(bit):
    def ready(values):
        up = (lax.axis_index("ctx") & bit) != 0

        def low(v):
            return v[:, : v.shape[1] // 2]

        def high(v):
            return v[:, v.shape[1] // 2 :]

        keep = jnp.where(up, part_of(values, high), part_of(values, low))
        return keep, jnp.where(up, part_of(values, low), part_of(values, high))

    return ready, "ctx", bit, pending


def spread_step(bit):
    def finish(own, other):
        up = (lax.axis_index("ctx") & bit) != 0
        return jnp.concatenate([jnp.where(up, other, own), jnp.where(up, own, other)], axis=1)

    def ready(values):
        values = part_of(values, lambda v: v)
        return values, values

    return ready, "ctx", bit, finish


def same_twice(values):
    return values, values


def gather_step(bit):
    return same_twice, "ctx", bit, lambda own, other: jnp.concatenate([own, other], axis=0)


def sum_step(bit):
    return same_twice, "fsdp", bit, lambda own, other: own + other


def reduce_steps(ctx_first, turn=0):
    fsdp_steps = [fsdp_step(bit) for bit in bits_of(lax.axis_size("fsdp"))[1:]]
    bits = bits_of(lax.axis_size("ctx"))
    bits = bits[turn:] + bits[:turn]
    scatter = [scatter_step(bit) for bit in bits]
    spread = [spread_step(bit) for bit in reversed(bits)]
    return (scatter + fsdp_steps if ctx_first else fsdp_steps + scatter) + spread


def advance(chains, beside=()):
    begun = []
    for steps, values in chains:
        if steps:
            ready, axis, bit, finish = steps.pop(0)
            keep, send = ready(values)
            values = (keep, swap(send, axis, bit), finish)
            begun.append((steps, values))
        else:
            begun.append((None, values))
    received, beside = together([values[1] for steps, values in begun if steps is not None], beside)
    after = []
    for steps, values in begun:
        if steps is None:
            after.append(([], values))
        else:
            after.append((steps, values[2](values[0], received.pop(0))))
    return after, beside


def fsdp_blocks(blocks):
    for bit in bits_of(lax.axis_size("fsdp")):
        blocks = [joined(k, swap(v, "fsdp", bit)) for k, v in zip(blocks[0::2], blocks[1::2])]
        yield blocks


def fsdp_selected(blocks, bit):
    up = (lax.axis_index("fsdp") & bit) != 0
    return [
        joined(jnp.where(up, high, low), swap(jnp.where(up, low, high), "fsdp", bit))
        for low, high in zip(blocks[0::2], blocks[1::2])
    ]


def side_by_side(values, rows):
    return jnp.concatenate([values[:rows], values[rows:]], axis=1)


def one_above(values, columns):
    return jnp.concatenate([values[:, :columns], values[:, columns:]], axis=0)


def dot(left, right):
    return jnp.dot(left, right, preferred_element_type=F32)


def rows_dot(left, right):
    return lax.dot_general(left, right, (((0,), (0,)), ((), ())), preferred_element_type=F32)


def back_dot(left, right):
    return lax.dot_general(left, right, (((1,), (1,)), ((), ())), preferred_element_type=F32)


def sigmoid(values):
    return 1.0 / (1.0 + jnp.exp(-values))


def softplus(values):
    small = jnp.exp(-jnp.abs(values))
    grown = 1.0 + small
    part = jnp.where(grown == 1.0, small, jnp.log(grown) * (small / jnp.maximum(grown - 1.0, 1e-30)))
    return jnp.maximum(values, 0.0) + part


def tile_cols(j):
    return slice(j * LANES, (j + 1) * LANES)


def input_kernel(scal, normed_ref, *refs, count, piece, is_upper):
    lows, highs = refs[:count], refs[count : 2 * count]
    s_ref, x_ref, conv_ref, xs_ref, proj_ref, mixed_ref = refs[2 * count :]
    depth = lows[0].shape[0]
    width = lows[0].shape[1]
    upper = is_upper(pl.program_id(0), scal)

    def mix(weights):
        mixed = dot(normed_ref[:, 0:depth], weights[0][...])
        for r in range(1, count):
            mixed = mixed + dot(normed_ref[:, r * depth : (r + 1) * depth], weights[r][...])
        mixed_ref[...] = mixed

    @pl.when(upper)
    def from_high():
        mix(highs)

    @pl.when(jnp.logical_not(upper))
    def from_low():
        mix(lows)

    x_low = mixed_ref[...].astype(BF16).reshape(2, HALO + piece, width)
    x_ref[...] = x_low
    x = x_low.astype(F32)
    head = s_ref[0:HEAD, :].astype(F32)
    conv = head[4:5] + x[:, HALO - 3 : HALO - 3 + piece] * head[0:1]
    for k in range(1, 4):
        conv = conv + x[:, HALO - 3 + k : HALO - 3 + k + piece] * head[k : k + 1]
    conv_ref[...] = conv
    xs = (conv * sigmoid(conv)).astype(BF16)
    xs_ref[...] = xs
    part = back_dot(xs.reshape(2 * piece, width), s_ref[96:192, :])

    @pl.when(pl.program_id(0) == 0)
    def first():
        proj_ref[...] = part

    @pl.when(pl.program_id(0) > 0)
    def later():
        proj_ref[...] += part


def gate_kernel(scal, normed_ref, *refs, count, piece):
    weights, (gate_ref,) = refs[:count], refs[count:]
    depth = weights[0].shape[0]
    width = weights[0].shape[1]
    own = jnp.concatenate(
        [normed_ref[HALO : HALO + piece], normed_ref[2 * HALO + piece : 2 * HALO + 2 * piece]], axis=0
    )
    gate = dot(own[:, 0:depth], weights[0][...])
    for r in range(1, count):
        gate = gate + dot(own[:, r * depth : (r + 1) * depth], weights[r][...])
    gate_ref[...] = gate.reshape(2, piece, width)


def end_kernel(
    scal, proj_ref, s_ref, xs_ref, b_ref, step_ref, end_ref, drive_ref, *, tiles, groups, rank
):
    piece = groups * 8
    width = tiles * LANES
    states = b_ref.shape[2]
    head = s_ref[0:HEAD, :].astype(F32)
    delta = proj_ref[:, 0:rank].astype(BF16)
    pre = dot(delta, s_ref[HEAD : HEAD + rank, :]) + head[5:6]
    row = lax.broadcasted_iota(jnp.int32, (piece, width), 0)
    logs = []
    for h in range(2):
        step = softplus(pre[h * piece : (h + 1) * piece])
        step = jnp.where(row < scal[1 + h], step, 0.0)
        logs.append(jnp.sum(step, axis=0, keepdims=True))
        step_ref[h] = step.reshape(groups, 8, width)
        drive_ref[h] = (step * xs_ref[h].astype(F32)).reshape(groups, 8, width)
    logs = jnp.concatenate(logs, axis=0)
    parts = [part.astype(F32) for part in three_parts(logs)]
    end_ref[2 * states : 2 * states + 8, :] = jnp.concatenate(
        parts + [jnp.zeros_like(logs)], axis=0
    ).astype(BF16)
    rate2 = -jnp.exp(s_ref[80 : 80 + states, :].astype(F32)) * LOG2E
    rates = [rate2[:, tile_cols(j)] for j in range(tiles)]

    def body(t, held):
        held = list(held)
        for s in range(8):
            for h in range(2):
                b = b_ref[h, t * 8 + s]
                for j in range(tiles):
                    step = step_ref[h, t, s : s + 1, tile_cols(j)]
                    drive = drive_ref[h, t, s : s + 1, tile_cols(j)]
                    k = h * tiles + j
                    held[k] = jnp.exp2(step * rates[j]) * held[k] + drive * b
        return tuple(held)

    zero = jnp.zeros((states, LANES), F32)
    held = lax.fori_loop(0, groups, body, (zero,) * (2 * tiles))
    for h in range(2):
        for j in range(tiles):
            end_ref[h * states : (h + 1) * states, tile_cols(j)] = held[h * tiles + j].astype(BF16)


def span_logs(ends, plan_ref, h, ctx, states):
    rows = []
    for j in range(1, ctx):
        parts = ends[j - 1][2 * states : 2 * states + 8, :].astype(F32)
        rows.append(parts[h : h + 1] + parts[2 + h : 3 + h] + parts[4 + h : 5 + h])
    logs = jnp.concatenate([jnp.zeros_like(rows[0])] + rows, axis=0)
    inside = plan_ref[h * ctx : (h + 1) * ctx, 0:ctx]
    outside = plan_ref[(2 + h) * ctx : (3 + h) * ctx, 0:1]
    return outside + lax.dot_general(
        inside, logs, (((1,), (0,)), ((), ())), precision=lax.Precision.HIGHEST, preferred_element_type=F32
    )


def diagonal_maps(proj_ref, first, states):
    rows = proj_ref.shape[0]
    k = lax.broadcasted_iota(jnp.int32, (proj_ref.shape[1], 16 * states), 0)
    n = lax.broadcasted_iota(jnp.int32, (proj_ref.shape[1], 16 * states), 1) % states
    spread = dot(proj_ref[...].astype(BF16), (k == n + first).astype(F32).astype(BF16))
    row = lax.broadcasted_iota(jnp.int32, (rows, 16 * states), 0) % 16
    col = lax.broadcasted_iota(jnp.int32, (rows, 16 * states), 1) // states
    return jnp.where(row == col, spread, 0.0).astype(BF16)


def carried(ends, logs, rate2, h, ctx, states, cols):
    value = jnp.zeros((states, LANES), F32)
    for j in range(1, ctx):
        decay = jnp.exp2(rate2 * logs[j : j + 1, cols])
        value = value + decay * ends[j - 1][h * states : (h + 1) * states, cols].astype(F32)
    return value


def forward_kernel(scal, *refs, tiles, groups, ctx, features):
    ends = refs[: ctx - 1]
    plan_ref, s_ref, step_ref, xs_ref, gate_ref, b_ref, proj_ref, weight_ref = refs[ctx - 1 : ctx + 7]
    rest = refs[ctx + 7 :]
    scale_ref, tokens_ref, teacher_ref = rest[:3]
    ssm_ref, branch_ref, hidden_ref, start_ref, out_ref, gout_ref, dout_ref, square_ref = rest[3:11]
    drive_ref, read_ref, acc_ref, cdiag_ref = rest[11:]
    piece = groups * 8
    width = tiles * LANES
    states = b_ref.shape[2]
    i = pl.program_id(0)
    head = s_ref[0:HEAD, :].astype(F32)

    @pl.when(i == 0)
    def maps():
        values = diagonal_maps(proj_ref, proj_ref.shape[1] - states, states)
        cdiag_ref[...] = values.reshape(cdiag_ref.shape)

    for h in range(2):
        drive_ref[h] = step_ref[h] * xs_ref[h].astype(F32).reshape(groups, 8, width)
    rate2 = -jnp.exp(s_ref[80 : 80 + states, :].astype(F32)) * LOG2E
    rates = [rate2[:, tile_cols(j)] for j in range(tiles)]
    held = []
    for h in range(2):
        logs = span_logs(ends, plan_ref, h, ctx, states)
        for j in range(tiles):
            held.append(carried(ends, logs, rates[j], h, ctx, states, tile_cols(j)))
            start_ref[h, :, tile_cols(j)] = held[-1]

    def scan(t, held):
        held = list(held)
        for s in range(16):
            p = t * 16 + s
            for h in range(2):
                b = b_ref[h, p]
                for j in range(tiles):
                    cols = tile_cols(j)
                    step = step_ref[h, t * 2 + s // 8, s % 8 : s % 8 + 1, cols]
                    drive = drive_ref[h, t * 2 + s // 8, s % 8 : s % 8 + 1, cols]
                    k = h * tiles + j
                    held[k] = jnp.exp2(step * rates[j]) * held[k] + drive * b
                    hidden_ref[j, h, p] = held[k].astype(BF16)
        return tuple(held)

    def read(t):
        for h in range(2):
            for j in range(tiles):
                low = hidden_ref[j, h, pl.ds(t * 16, 16)].reshape(16 * states, LANES)
                out = dot(cdiag_ref[h, t], low)
                read_ref[h, t * 2, :, tile_cols(j)] = out[0:8]
                read_ref[h, t * 2 + 1, :, tile_cols(j)] = out[8:16]

    def body(t, held):
        read(t - 1)
        return scan(t, held)

    blocks = groups // 2
    lax.fori_loop(1, blocks, body, scan(0, tuple(held)))
    read(blocks - 1)
    branches = []
    for h in range(2):
        ssm = read_ref[h].reshape(piece, width) + head[6:7] * xs_ref[h].astype(F32)
        ssm_ref[h] = ssm
        gate = gate_ref[h]
        branches.append((ssm * (gate * sigmoid(gate))).astype(BF16))
        branch_ref[h] = branches[-1]
    part = dot(jnp.concatenate(branches, axis=0), weight_ref[...])

    @pl.when(i == 0)
    def first():
        acc_ref[...] = part

    @pl.when(i > 0)
    def later():
        acc_ref[...] += part

    @pl.when(i == pl.num_programs(0) - 1)
    def last():
        row = lax.broadcasted_iota(jnp.int32, (piece, features), 0)
        square = jnp.zeros((8, features), F32)
        for h in range(2):
            rows = slice(h * piece, (h + 1) * piece)
            block_out = tokens_ref[rows, :].astype(F32) + acc_ref[rows, :]
            out_ref[rows, :] = block_out.astype(BF16)
            error = jnp.where(row < scal[1 + h], block_out - teacher_ref[rows, :].astype(F32), 0.0)
            square = square + jnp.sum((error * error).reshape(groups, 8, features), axis=0)
            g_out = error * (2.0 * scale_ref[0, 0])
            gout_ref[rows, :] = g_out
            dout_ref[rows, :] = g_out.astype(BF16)
        square_ref[...] = square


def first_grad_kernel(
    scal, dout_ref, weight_ref, s_ref, step_ref, xs_ref, gate_ref, ssm_ref, c_ref,
    dssm_ref, dgate_ref, skip_ref, grad_ref, *, tiles, groups
):
    piece = groups * 8
    width = tiles * LANES
    states = c_ref.shape[2]
    d_branch = back_dot(dout_ref[...], weight_ref[...])
    skip = jnp.zeros((1, width), F32)
    for h in range(2):
        grad = d_branch[h * piece : (h + 1) * piece]
        gate = gate_ref[h]
        sig = sigmoid(gate)
        d_ssm = grad * (gate * sig)
        dgate_ref[h] = (grad * ssm_ref[h] * (sig * (1.0 + gate * (1.0 - sig)))).astype(BF16)
        skip = skip + jnp.sum(d_ssm * xs_ref[h].astype(F32), axis=0, keepdims=True)
        dssm_ref[h] = d_ssm.reshape(groups, 8, width)
    skip_ref[...] = skip
    rate2 = -jnp.exp(s_ref[80 : 80 + states, :].astype(F32)) * LOG2E
    rates = [rate2[:, tile_cols(j)] for j in range(tiles)]

    def body(i, held):
        held = list(held)
        t = groups - 1 - i
        for s in range(7, -1, -1):
            for h in range(2):
                c = c_ref[h, t * 8 + s]
                for j in range(tiles):
                    step = step_ref[h, t, s : s + 1, tile_cols(j)]
                    dssm = dssm_ref[h, t, s : s + 1, tile_cols(j)]
                    k = h * tiles + j
                    held[k] = jnp.exp2(step * rates[j]) * (held[k] + dssm * c)
        return tuple(held)

    zero = jnp.zeros((states, LANES), F32)
    held = lax.fori_loop(0, groups, body, (zero,) * (2 * tiles))
    for h in range(2):
        for j in range(tiles):
            grad_ref[h * states : (h + 1) * states, tile_cols(j)] = held[h * tiles + j].astype(BF16)


def out_grad_kernel(even_ref, odd_ref, dout_ref, keep_ref, send_ref):
    keep_ref[0] = rows_dot(even_ref[...], dout_ref[...]).astype(BF16)
    send_ref[0] = rows_dot(odd_ref[...], dout_ref[...]).astype(BF16)


def gate_grad_kernel(scal, normed_ref, dgate_ref, *refs, count, piece):
    weights, (keep_ref, send_ref, dnormed_ref) = refs[:count], refs[count:]
    depth = weights[0].shape[0]
    width = weights[0].shape[1]
    own = jnp.concatenate(
        [normed_ref[HALO : HALO + piece], normed_ref[2 * HALO + piece : 2 * HALO + 2 * piece]], axis=0
    )
    d_gate = dgate_ref[...].reshape(2 * piece, width)

    @pl.when(pl.program_id(0) == 0)
    def clear():
        dnormed_ref[...] = jnp.zeros_like(dnormed_ref)

    for r in range(count):
        cols = slice(r * depth, (r + 1) * depth)
        target = send_ref if r % 2 else keep_ref
        target[r // 2] = rows_dot(own[:, cols], d_gate).astype(BF16)
        back = back_dot(d_gate, weights[r][...])
        for h in range(2):
            rows = slice(h * (HALO + piece) + HALO, (h + 1) * (HALO + piece))
            dnormed_ref[rows, cols] += back[h * piece : (h + 1) * piece]


def backward_kernel(scal, *refs, tiles, groups, ctx, rank):
    grads = refs[: ctx - 1]
    ends = refs[ctx - 1 : 2 * ctx - 2]
    (
        plan_ref, proj_ref, s_ref, step_ref, xs_ref, c_ref, start_ref, dssm_ref, hidden_ref,
        dxs_ref, small_ref, ddelta_ref, db_ref, dc_ref,
        adj_ref, dstep_ref, dbs_ref, dcs_ref, bdiag_ref,
    ) = refs[2 * ctx - 2 :]
    piece = groups * 8
    width = tiles * LANES
    states = c_ref.shape[2]
    blocks = groups // 2
    i = pl.program_id(0)
    head = s_ref[0:HEAD, :].astype(F32)

    @pl.when(i == 0)
    def clear():
        dbs_ref[...] = jnp.zeros_like(dbs_ref)
        dcs_ref[...] = jnp.zeros_like(dcs_ref)
        bdiag_ref[...] = diagonal_maps(proj_ref, rank, states).reshape(bdiag_ref.shape)
        ddelta_ref[...] = jnp.zeros_like(ddelta_ref)

    rate = -jnp.exp(s_ref[80 : 80 + states, :].astype(F32))
    rates = [rate[:, tile_cols(j)] for j in range(tiles)]
    rates2 = [values * LOG2E for values in rates]
    row16 = lax.broadcasted_iota(jnp.int32, (16, 16 * states), 0)
    col16 = lax.broadcasted_iota(jnp.int32, (16, 16 * states), 1)
    same = (col16 // states == row16).astype(F32)
    same_low = same.astype(BF16)

    def work(t, first, later, sums):
        for h in range(2):
            adjoints = [[None] * 16 for _ in range(tiles)]
            terms = [[None] * 16 for _ in range(tiles)]
            for s in range(15, -1, -1):
                p = t * 16 + s
                c = c_ref[h, p]
                for j in range(tiles):
                    cols = tile_cols(j)
                    step = step_ref[h, t * 2 + s // 8, s % 8 : s % 8 + 1, cols]
                    dssm = dssm_ref[h, t * 2 + s // 8, s % 8 : s % 8 + 1, cols]
                    k = h * tiles + j
                    if first and s == 0:
                        before = start_ref[h, :, cols]
                    else:
                        before = hidden_ref[j, h, p - 1].astype(F32)
                    adjoint = dssm * c + later[k]
                    later[k] = jnp.exp2(step * rates2[j]) * adjoint
                    term = later[k] * before
                    sums[j] = sums[j] + term * step
                    adjoints[j][s] = adjoint.astype(BF16)
                    terms[j][s] = (term * rates[j]).astype(BF16)
            db = dc = None
            for j in range(tiles):
                cols = tile_cols(j)
                adjoint = jnp.concatenate(adjoints[j], axis=0)
                out = dot(bdiag_ref[h, t], adjoint)
                adj_ref[h, t * 2, :, cols] = out[0:8]
                adj_ref[h, t * 2 + 1, :, cols] = out[8:16]
                out = dot(same_low, jnp.concatenate(terms[j], axis=0))
                dstep_ref[h, t * 2, :, cols] = out[0:8]
                dstep_ref[h, t * 2 + 1, :, cols] = out[8:16]
                step = step_ref[h, pl.ds(t * 2, 2), :, cols].reshape(16, LANES)
                dssm = dssm_ref[h, pl.ds(t * 2, 2), :, cols].reshape(16, LANES)
                drive = (step * xs_ref[h, pl.ds(t * 16, 16), cols].astype(F32)).astype(BF16)
                hidden = hidden_ref[j, h, pl.ds(t * 16, 16)].reshape(16 * states, LANES)
                db_now = back_dot(drive, adjoint)
                dc_now = back_dot(dssm.astype(BF16), hidden)
                db = db_now if db is None else db + db_now
                dc = dc_now if dc is None else dc + dc_now
            dbs_ref[h, t] += db
            dcs_ref[h, t] += dc

    def body(k, both):
        later, sums = list(both[: 2 * tiles]), list(both[2 * tiles :])
        work(blocks - 1 - k, False, later, sums)
        return tuple(later + sums)

    later = []
    for h in range(2):
        logs = span_logs(ends, plan_ref, h, ctx, states)
        for j in range(tiles):
            later.append(carried(grads, logs, rates2[j], h, ctx, states, tile_cols(j)))
    sums = [jnp.zeros((states, LANES), F32)] * tiles
    both = lax.fori_loop(0, blocks - 1, body, tuple(later + sums))
    later, sums = list(both[: 2 * tiles]), list(both[2 * tiles :])
    work(0, True, later, sums)
    for j in range(tiles):
        small_ref[rank : rank + states, tile_cols(j)] = sums[j] * rates[j]
    delta = proj_ref[:, 0:rank].astype(BF16)
    pre = dot(delta, s_ref[HEAD : HEAD + rank, :]) + head[5:6]
    row = lax.broadcasted_iota(jnp.int32, (piece, width), 0)
    lows = []
    bias = jnp.zeros((1, width), F32)
    for h in range(2):
        xs = xs_ref[h].astype(F32)
        adj = adj_ref[h].reshape(piece, width)
        d_step = xs * adj + dstep_ref[h].reshape(piece, width)
        d_pre = jnp.where(row < scal[1 + h], d_step * sigmoid(pre[h * piece : (h + 1) * piece]), 0.0)
        bias = bias + jnp.sum(d_pre, axis=0, keepdims=True)
        lows.append(d_pre.astype(BF16))
        dxs_ref[h] = head[6:7] * dssm_ref[h].reshape(piece, width) + step_ref[h].reshape(piece, width) * adj
    small_ref[rank + states : rank + states + 8, :] = jnp.broadcast_to(bias, (8, width))
    low = jnp.concatenate(lows, axis=0)
    small_ref[0:rank, :] = rows_dot(delta, low)
    ddelta_ref[...] += back_dot(low, s_ref[HEAD : HEAD + rank, :])

    @pl.when(i == pl.num_programs(0) - 1)
    def last():
        for h in range(2):
            for t in range(blocks):
                db_ref[h, t : t + 1, :] = jnp.sum(dbs_ref[h, t] * same, axis=0, keepdims=True)
                dc_ref[h, t : t + 1, :] = jnp.sum(dcs_ref[h, t] * same, axis=0, keepdims=True)


def tail_kernel(
    scal, dproj_ref, s_ref, dxs_ref, conv_ref, x_ref, xs_ref, normed_ref, before_ref, *refs,
    count, piece
):
    weights, (small_ref, keep_ref, send_ref, dnormed_ref, pad_ref) = refs[:count], refs[count:]
    depth = weights[0].shape[0]
    width = weights[0].shape[1]
    ext = HALO + piece

    @pl.when(pl.program_id(0) == 0)
    def clear():
        dnormed_ref[...] = before_ref[...]
        for h in range(2):
            pad_ref[h, 0:HALO, :] = jnp.zeros((HALO, width), F32)
            pad_ref[h, ext : ext + 8, :] = jnp.zeros((8, width), F32)

    head = s_ref[0:HEAD, :].astype(F32)
    small_ref[8:104, :] = rows_dot(dproj_ref[...], xs_ref[...].reshape(2 * piece, width))
    d_xs = dot(dproj_ref[...], s_ref[96:192, :])
    taps = [jnp.zeros((1, width), F32) for _ in range(5)]
    lows = []
    for h in range(2):
        conv = conv_ref[h]
        sig = sigmoid(conv)
        d_conv = (dxs_ref[h] + d_xs[h * piece : (h + 1) * piece]) * (sig * (1.0 + conv * (1.0 - sig)))
        pad_ref[h, HALO:ext, :] = d_conv
        x = x_ref[h].astype(F32)
        for k in range(4):
            rows = slice(HALO - 3 + k, HALO - 3 + k + piece)
            taps[k] = taps[k] + jnp.sum(d_conv * x[rows], axis=0, keepdims=True)
        taps[4] = taps[4] + jnp.sum(d_conv, axis=0, keepdims=True)
        d_x = head[3:4] * pad_ref[h, 0:ext, :]
        for k in range(3):
            d_x = d_x + head[k : k + 1] * pad_ref[h, 3 - k : 3 - k + ext, :]
        lows.append(d_x.astype(BF16))
    small_ref[0:8, :] = jnp.concatenate(taps + [jnp.zeros((3, width), F32)], axis=0)
    low = jnp.concatenate(lows, axis=0)
    for r in range(count):
        cols = slice(r * depth, (r + 1) * depth)
        target = send_ref if r % 2 else keep_ref
        target[r // 2] = rows_dot(normed_ref[:, cols], low).astype(BF16)
        dnormed_ref[:, cols] += back_dot(low, weights[r][...])


def shape(dims, dtype=F32):
    return jax.ShapeDtypeStruct(dims, dtype)


def call(kernel, name, grid, scal, args, in_specs, out_specs, out_shape, scratch, flops, exps=0):
    size = sum(a.size * a.dtype.itemsize for a in args) + sum(
        s.size * s.dtype.itemsize for s in out_shape
    )
    return pl.pallas_call(
        kernel,
        grid_spec=pltpu.PrefetchScalarGridSpec(
            num_scalar_prefetch=1,
            grid=(grid,),
            in_specs=in_specs,
            out_specs=out_specs,
            scratch_shapes=scratch,
        ),
        out_shape=out_shape,
        name=name,
        compiler_params=pltpu.CompilerParams(vmem_limit_bytes=LIMITS[name] * 2**20),
        cost_estimate=pl.CostEstimate(flops=flops, bytes_accessed=size, transcendentals=exps),
    )(scal, *args)


def whole_spec(dims):
    return pl.BlockSpec(dims, lambda i, scal: (0,) * len(dims))


def local(
    tokens,
    teacher,
    lengths,
    pair_owner,
    norm_gain,
    in_proj,
    conv_weight,
    conv_bias,
    x_proj,
    dt_proj,
    dt_bias,
    a_log,
    skip_scale,
    out_proj,
):
    ctx = lax.axis_size("ctx")
    fsdp = lax.axis_size("fsdp")
    me_ctx = lax.axis_index("ctx")
    me_fsdp = lax.axis_index("fsdp")
    piece = tokens.shape[1] // 2
    features = tokens.shape[2]
    width = in_proj.shape[1] // 2
    rank = dt_proj.shape[0]
    states = a_log.shape[0]
    groups = piece // 8
    ext = HALO + piece
    depth = features // fsdp
    part = width // fsdp
    rows_all = 2 * piece
    elements = rows_all * states * width

    relative = jnp.arange(ctx, dtype=jnp.int32) ^ me_ctx
    pair_of = jnp.sum(
        jnp.arange(ctx, dtype=jnp.int32)[None, :]
        * (pair_owner[None, :] == relative[:, None]).astype(jnp.int32),
        axis=1,
    )
    places = jnp.stack([pair_of, ctx - 1 - pair_of])
    pair_id = pair_of[0]
    own = places[:, 0]
    limits = jnp.clip(lengths[0] - own * piece, 0, piece)
    scal = jnp.concatenate([me_fsdp[None], limits]).astype(jnp.int32)
    between = (places[:, :, None] < places[:, None, :]) & (
        places[:, None, :] < own[:, None, None]
    )
    between_back = (places[:, :, None] > places[:, None, :]) & (
        places[:, None, :] > own[:, None, None]
    )
    before = places < own[:, None]
    behind = places > own[:, None]
    has_before = jnp.stack([pair_id > 0, pair_id < ctx - 1])
    has_after = jnp.stack([pair_id < ctx - 1, pair_id > 0])
    lower_owner = pair_owner[jnp.maximum(pair_id - 1, 0)]
    upper_owner = pair_owner[jnp.minimum(pair_id + 1, ctx - 1)]
    lower, upper = lower_owner ^ me_ctx, upper_owner ^ me_ctx

    def plan_of(inside, wanted):
        inside = jnp.pad(inside.astype(F32), ((0, 0), (0, 0), (0, LANES - ctx)))
        outside = jnp.broadcast_to(jnp.where(wanted, 0.0, 1e30)[..., None], (2, ctx, LANES))
        return jnp.concatenate([inside, outside], axis=0).reshape(4 * ctx, LANES).astype(F32)

    plan_before = plan_of(between, before)
    plan_behind = plan_of(between_back, behind)

    def to_blocks(values, size):
        axis = values.ndim - 1
        return jnp.concatenate(
            [
                lax.dynamic_slice_in_dim(values, (me_fsdp ^ r) * size, size, axis=axis)
                for r in range(fsdp)
            ],
            axis=axis,
        )

    own_rows = tokens[0]
    valid_slots = jnp.minimum(lengths[0], 2 * ctx * piece)
    coded = jnp.concatenate([valid_slots // 128, valid_slots % 128]).astype(BF16)[None]
    rows_head = jnp.concatenate(
        [
            conv_weight,
            conv_bias[None],
            dt_bias[None],
            skip_scale[None],
            jnp.pad(norm_gain, (0, part - depth))[None],
            jnp.pad(coded, ((0, 0), (0, part - 4))),
            jnp.zeros((HEAD - 9, part), BF16),
            dt_proj,
            a_log,
            x_proj.T,
        ],
        axis=0,
    )
    half = width // 2
    to_send = in_proj[:, :half]
    x_far = [to_send] + [swap(to_send, "fsdp", bit) for bit in range(2, fsdp, 2)]
    last_rows = to_blocks(own_rows.reshape(2, piece, features)[:, piece - 3 :], depth)
    last_rows = jnp.broadcast_to(last_rows[None], (ctx, 2, 3, features))
    token_rel = to_blocks(own_rows, depth).reshape(2, piece, features)
    tails = lax.all_to_all(last_rows, "ctx", 0, 0)
    x_far, second, rows_head, tails, scal, plan_before, plan_behind = together(
        x_far, in_proj[:, half:width], rows_head, tails, scal, plan_before, plan_behind
    )
    x_first = [block for own in x_far for block in (own, swap(own, "fsdp", 1))]
    small_blocks = gather_fsdp(rows_head)
    small = jnp.concatenate(small_blocks, axis=1)
    gain = jnp.concatenate([block[7, :depth] for block in small_blocks]).astype(F32)
    x_second = gather_fsdp(second)

    before_rows = jnp.stack([tails[lower_owner, 0], tails[upper_owner, 1]])
    before_rows = jnp.where(has_before[:, None, None], before_rows, jnp.zeros_like(before_rows))
    rows_ext = jnp.concatenate(
        [jnp.zeros((2, HALO - 3, features), BF16), before_rows, token_rel], axis=1
    ).astype(F32)
    inv_rms = lax.rsqrt(jnp.mean(rows_ext * rows_ext, axis=2, keepdims=True) + EPSILON)
    normed = (rows_ext * inv_rms * gain).astype(BF16).reshape(2 * ext, features)

    codes = jnp.stack([block[8, :4] for block in small_blocks]).astype(F32)
    count = jnp.sum(codes[:, 0:2] * 128.0 + codes[:, 2:4])
    scale = ((fsdp * rows_all * ctx) / count).reshape(1, 1)
    normed, scale = together(normed, scale)

    def cols_at(block):
        per = part // block
        return lambda i, scal: (0, (scal[0] ^ (i // per)) * per + i % per)

    def spec_small(block, offset=0):
        return pl.BlockSpec((small.shape[0], block), lambda i, scal: (0, i + offset))

    def spec_rows(block, offset=0):
        return pl.BlockSpec((2, piece, block), lambda i, scal: (0, 0, i + offset))

    def spec_groups(block):
        return pl.BlockSpec((2, groups, 8, block), lambda i, scal: (0, 0, 0, i))

    cb = min(256, part)
    steps = width // cb
    weight_specs = [pl.BlockSpec((depth, cb), cols_at(cb)) for _ in range(fsdp)]
    half_blocks = half // cb

    def upper_place(i, scal):
        return cols_at(cb)(i, scal)[1] >= half_blocks

    low_spec = pl.BlockSpec(
        (depth, cb), lambda i, scal: (0, jnp.minimum(cols_at(cb)(i, scal)[1], half_blocks - 1))
    )
    high_spec = pl.BlockSpec(
        (depth, cb), lambda i, scal: (0, jnp.maximum(cols_at(cb)(i, scal)[1] - half_blocks, 0))
    )
    x_ext, conv, xs, proj = call(
        functools.partial(input_kernel, count=fsdp, piece=piece, is_upper=upper_place),
        "inputs", steps, scal, (normed, *x_first, *x_second, small),
        [whole_spec((2 * ext, features)), *([low_spec] * fsdp), *([high_spec] * fsdp), spec_small(cb)],
        [
            pl.BlockSpec((2, ext, cb), lambda i, scal: (0, 0, i)),
            spec_rows(cb),
            spec_rows(cb),
            whole_spec((rows_all, rank + 2 * states)),
        ],
        [
            shape((2, ext, width), BF16),
            shape((2, piece, width)),
            shape((2, piece, width), BF16),
            shape((rows_all, rank + 2 * states)),
        ],
        [pltpu.VMEM((2 * ext, cb), F32)], 2 * rows_all * features * width,
    )
    gate_first = after(in_proj[:, width:], x_second[fsdp // 2])
    gate_far = [gate_first] + [swap(gate_first, "fsdp", bit) for bit in range(2, fsdp, 2)]
    gate_far, proj = together(gate_far, proj)
    gate_blocks = [block for own in gate_far for block in (own, swap(own, "fsdp", 1))]
    out_first = after(out_proj, gate_far[-1])
    out_far = [out_first] + [swap(out_first, "fsdp", bit) for bit in range(2, fsdp, 2)]
    wide_dims = (2, piece, states, LANES)
    maps = proj[:, rank:].reshape(2, piece, 2 * states, 1)
    b_wide = jnp.broadcast_to(maps[:, :, :states], wide_dims)

    tiles = 4
    block = tiles * LANES
    per_half = half // block
    group_spec = spec_groups(block)
    state_row = pl.BlockSpec((2 * states, block), lambda i, scal: (0, i))
    sent_row = pl.BlockSpec((2 * states + 8, block), lambda i, scal: (0, i))
    plan_spec = whole_spec((4 * ctx, LANES))
    row_spec = whole_spec((rows_all, features))
    wide_spec = whole_spec(wide_dims)
    diag_space = pltpu.VMEM((2, piece // 16, 16, 16 * states), BF16)
    hidden_spec = pl.BlockSpec((tiles, 2, piece, states, LANES), lambda i, scal: (i, 0, 0, 0, 0))
    start_spec = pl.BlockSpec((2, states, block), lambda i, scal: (0, 0, i))
    group_space = pltpu.VMEM((2, groups, 8, block), F32)

    step, sent = call(
        functools.partial(end_kernel, tiles=tiles, groups=groups, rank=rank),
        "end_states", width // block, scal, (proj, small, xs, b_wide),
        [whole_spec(proj.shape), spec_small(block), spec_rows(block), wide_spec],
        [group_spec, pl.BlockSpec((2 * states + 8, block), lambda i, scal: (0, i))],
        [shape((2, groups, 8, width)), shape((2 * states + 8, width), BF16)],
        [group_space], 5 * elements, elements,
    )

    far = gather_far(sent)
    (gate,) = call(
        functools.partial(gate_kernel, count=fsdp, piece=piece),
        "gates", steps, scal, (normed, *gate_blocks),
        [whole_spec((2 * ext, features)), *weight_specs], [spec_rows(cb)],
        [shape((2, piece, width))], [], 2 * rows_all * features * width,
    )
    c_wide = jnp.broadcast_to(maps[:, :, states:], wide_dims)
    far, gate, out_far = together(far, gate, out_far)
    near, c_wide = gather_near(far, c_wide)
    out_blocks = [block for own in out_far for block in (own, swap(own, "fsdp", 1))]
    weight_out = jnp.concatenate(out_blocks, axis=0)
    near, weight_out = together(near, weight_out)
    ssm, branch, hidden, starts, out_low, g_out, d_out, squares = call(
        functools.partial(forward_kernel, tiles=tiles, groups=groups, ctx=ctx, features=features),
        "forward_states", width // block, scal,
        (*near[1:], plan_before, small, step, xs, gate, b_wide, proj, weight_out,
         scale, own_rows, teacher[0]),
        [
            *([sent_row] * (ctx - 1)), plan_spec, spec_small(block), group_spec, spec_rows(block),
            spec_rows(block), wide_spec, whole_spec(proj.shape),
            pl.BlockSpec((block, features), lambda i, scal: (i, 0)),
            pl.BlockSpec(memory_space=pltpu.SMEM), row_spec, row_spec,
        ],
        [
            spec_rows(block), spec_rows(block), hidden_spec, start_spec, row_spec, row_spec, row_spec,
            whole_spec((8, features)),
        ],
        [
            shape((2, piece, width)),
            shape((2, piece, width), BF16),
            shape((width // LANES, 2, piece, states, LANES), BF16),
            shape((2, states, width)),
            shape((rows_all, features), BF16),
            shape((rows_all, features)),
            shape((rows_all, features), BF16),
            shape((8, features)),
        ],
        [group_space] * 2 + [pltpu.VMEM((rows_all, features), F32), diag_space],
        10 * elements, elements,
    )
    d_ssm, d_gate, grad_skip, grads_first = call(
        functools.partial(first_grad_kernel, tiles=tiles, groups=groups),
        "first_grads", width // block, scal,
        (d_out, weight_out, small, step, xs, gate, ssm, c_wide),
        [
            row_spec, pl.BlockSpec((block, features), lambda i, scal: (i, 0)), spec_small(block),
            group_spec, spec_rows(block), spec_rows(block), spec_rows(block), wide_spec,
        ],
        [group_spec, spec_rows(block), pl.BlockSpec((1, block), lambda i, scal: (0, i)), state_row],
        [
            shape((2, groups, 8, width)),
            shape((2, piece, width), BF16),
            shape((1, width)),
            shape((2 * states, width), BF16),
        ],
        [], 6 * elements, elements,
    )
    back_far = gather_far(grads_first)

    pairs = fsdp // 2
    pair_spec = pl.BlockSpec((pairs, depth, cb), lambda i, scal: (0, 0, i))
    pair_at = pl.BlockSpec((pairs, depth, cb), lambda i, scal: (0, 0, cols_at(cb)(i, scal)[1]))
    keep_gate, send_gate, d_normed_gate = call(
        functools.partial(gate_grad_kernel, count=fsdp, piece=piece),
        "gate_grads", steps, scal, (normed, d_gate, *gate_blocks),
        [whole_spec((2 * ext, features)), spec_rows(cb), *weight_specs],
        [pair_at, pair_at, whole_spec((2 * ext, features))],
        [shape((pairs, depth, width), BF16)] * 2 + [shape((2 * ext, features))],
        [], 4 * rows_all * features * width,
    )
    subs = part // cb
    branch_rows = branch.reshape(rows_all, width)
    keep_out, send_out = pl.pallas_call(
        out_grad_kernel,
        grid=(pairs, subs),
        in_specs=[
            pl.BlockSpec((rows_all, cb), lambda k, s: (0, 2 * k * subs + s)),
            pl.BlockSpec((rows_all, cb), lambda k, s: (0, (2 * k + 1) * subs + s)),
            pl.BlockSpec((rows_all, features), lambda k, s: (0, 0)),
        ],
        out_specs=[pl.BlockSpec((1, cb, features), lambda k, s: (k, s, 0))] * 2,
        out_shape=[shape((pairs, part, features), BF16)] * 2,
        name="out_grads",
        compiler_params=pltpu.CompilerParams(vmem_limit_bytes=VMEM_LIMIT),
        cost_estimate=pl.CostEstimate(
            flops=2 * rows_all * width * features, bytes_accessed=9 * 2**20, transcendentals=0
        ),
    )(branch_rows, branch_rows, d_out)
    back_far, keep_gate, send_gate, keep_out, send_out = together(
        back_far, keep_gate, send_gate, keep_out, send_out
    )
    back_near, _ = gather_near(back_far)
    core_gate = (keep_gate, swap(send_gate, "fsdp", 1))
    core_out = (keep_out, swap(send_out, "fsdp", 1))
    out_steps, gate_steps = reduce_steps(False), reduce_steps(True, 1)
    out_ready, gate_ready = out_steps[0][0](core_out), gate_steps[0][0](core_gate)
    back_near, out_ready, gate_ready = together(back_near, out_ready, gate_ready)
    out_steps[0] = (lambda values: values, *out_steps[0][1:])
    gate_steps[0] = (lambda values: values, *gate_steps[0][1:])
    chains = [(out_steps, out_ready), (gate_steps, gate_ready)]

    def backward():
        def at(i):
            return i

        return call(
            functools.partial(backward_kernel, tiles=tiles, groups=groups, ctx=ctx, rank=rank),
            "backward_states", width // block, scal,
            (*back_near[1:], *near[1:], plan_behind, proj, small, step, xs, c_wide, starts, d_ssm, hidden),
            [
                *([pl.BlockSpec((2 * states, block), lambda i, scal: (0, at(i)))] * (ctx - 1)),
                *([pl.BlockSpec((2 * states + 8, block), lambda i, scal: (0, at(i)))] * (ctx - 1)),
                plan_spec,
                whole_spec(proj.shape), spec_small(block),
                pl.BlockSpec((2, groups, 8, block), lambda i, scal: (0, 0, 0, at(i))),
                spec_rows(block), wide_spec,
                pl.BlockSpec((2, states, block), lambda i, scal: (0, 0, at(i))),
                pl.BlockSpec((2, groups, 8, block), lambda i, scal: (0, 0, 0, at(i))),
                pl.BlockSpec((tiles, 2, piece, states, LANES), lambda i, scal: (at(i), 0, 0, 0, 0)),
            ],
            [
                spec_rows(block), pl.BlockSpec((rank + states + 8, block), lambda i, scal: (0, i)),
                whole_spec((rows_all, rank)),
                whole_spec((2, piece // 16, 16 * states)), whole_spec((2, piece // 16, 16 * states)),
            ],
            [
                shape((2, piece, width)),
                shape((rank + states + 8, width)),
                shape((rows_all, rank)),
                shape((2, piece // 16, 16 * states)),
                shape((2, piece // 16, 16 * states)),
            ],
            [group_space] * 2 + [pltpu.VMEM((2, piece // 16, 16, 16 * states), F32)] * 2 + [diag_space],
            16 * elements, elements,
        )

    chains, back = advance(chains, backward())

    small_rows = jnp.concatenate(
        [back[1], grad_skip, jnp.zeros((7, width), F32)], axis=0
    ).astype(BF16)
    d_proj = jnp.concatenate(
        [back[2], back[3].reshape(rows_all, states), back[4].reshape(rows_all, states)], axis=1
    ).astype(BF16)
    half_steps = steps // 2

    def tail(c, d_proj, d_before):
        base = c * half_steps

        def place(i, scal):
            return cols_at(cb)(i + base, scal)[1]

        def at_rows(dims):
            return pl.BlockSpec((2, dims, cb), lambda i, scal: (0, 0, place(i, scal)))

        return call(
            functools.partial(tail_kernel, count=fsdp, piece=piece),
            "tail_grads", half_steps, scal,
            (d_proj, small, back[0], conv, x_ext, xs, normed, d_before,
             *(x_second if c else x_first)),
            [
                whole_spec(d_proj.shape),
                pl.BlockSpec((small.shape[0], cb), lambda i, scal: (0, place(i, scal))),
                at_rows(piece), at_rows(piece), at_rows(ext), at_rows(piece),
                whole_spec((2 * ext, features)), whole_spec((2 * ext, features)),
                *([pl.BlockSpec((depth, cb), lambda i, scal: (0, i))] * fsdp),
            ],
            [
                pl.BlockSpec((104, cb), lambda i, scal: (0, i)),
                pair_spec, pair_spec, whole_spec((2 * ext, features)),
            ],
            [
                shape((104, half)),
                shape((pairs, depth, half), BF16),
                shape((pairs, depth, half), BF16),
                shape((2 * ext, features)),
            ],
            [pltpu.VMEM((2, ext + 8, cb), F32)],
            4 * rows_all * features * half,
        )

    d_before = d_normed_gate
    d_proj, d_before, _ = together(d_proj, d_before, [values for _, values in chains])
    chains, tail_first = advance(chains, tail(0, d_proj, d_before))
    got_ahead = swap(tail_first[2], "fsdp", 1)
    small_now = [small_rows[:, k * part : (k + 1) * part] for k in range(fsdp)]
    for small_now in fsdp_blocks(small_now):
        pass
    d_proj, _ = together(d_proj, [values for _, values in chains])
    chains, (tail_second, got_ahead, small_now) = advance(
        chains, (tail(1, d_proj, tail_first[3]), got_ahead, small_now)
    )
    ahead = (tail_first[1], got_ahead)
    def halo_start(d_ext, squares):
        d_normed = d_ext.reshape(2, ext, features)
        unit = rows_ext * inv_rms
        grad_gain = jnp.sum(d_normed[:, HALO - 3 :] * unit[:, HALO - 3 :], axis=(0, 1))
        square = jnp.pad(jnp.stack(three_parts(jnp.sum(squares))), (0, features - 3))
        halo_rows = d_normed[:, HALO - 3 : HALO].reshape(6, features)
        return jnp.concatenate(
            [halo_rows.astype(BF16), square[None], grad_gain.astype(BF16)[None]]
        )[None]

    def halo_vector(halo_got):
        return jnp.concatenate(
            [
                to_blocks(jnp.sum(halo_got[:, 7], axis=0)[None], depth)[0],
                jnp.pad(jnp.sum(halo_got[:, 6, 0:3])[None], (0, LANES - 1)),
            ]
        )

    tail_rows = [
        values[:, k * part : (k + 1) * part].astype(BF16)
        for values in (tail_first[0], tail_second[0])
        for k in range(fsdp // 2)
    ]
    lines = small_now[0].shape[0] // 2
    lines_tail = tail_rows[0].shape[0] // 2
    got_last = swap(tail_second[2], "fsdp", 1)
    lead = [(reduce_steps(True), ahead)]
    lead, (got_last, d_ext, squares) = advance(lead, (got_last, tail_second[3], squares))
    chains = chains + lead
    last = (tail_second[1], got_last)
    last_steps = reduce_steps(False)
    n_fsdp = len(bits_of(fsdp)) - 1
    for bit in bits_of(fsdp):
        tail_rows = fsdp_selected(tail_rows, bit)
    for_halo = None
    halo_steps = [gather_step(bit) for bit in bits_of(ctx)]
    sum_steps = [sum_step(bit) for bit in bits_of(fsdp)]
    while last_steps:
        for_last = [([last_steps.pop(0)], last)]
        more = [(halo_steps or sum_steps, for_halo)] if for_halo is not None else []
        chains, tail_rows = advance([*for_last, *chains, *more], tail_rows)
        last = chains.pop(0)[1]
        if more:
            for_halo = chains.pop()[1]
            if not halo_steps and halo_got is None:
                halo_got = for_halo.astype(F32)
                for_halo = halo_vector(halo_got)
        n_fsdp -= 1
        if n_fsdp == 0:
            extra = jnp.concatenate(
                [
                    side_by_side(small_now[0], lines),
                    side_by_side(tail_rows[0], lines_tail),
                    jnp.zeros((128 - lines - lines_tail, 2 * part), BF16),
                ],
                axis=0,
            ).reshape(1, -1, half)
            last = jnp.concatenate([part_of(last, lambda v: v), extra], axis=1)
        if n_fsdp == -1:
            last, d_ext, squares = together(last, d_ext, squares)
            for_halo, halo_got = halo_start(d_ext, squares), None
    while any(steps_left for steps_left, _ in chains):
        chains, _ = advance(chains)
    while halo_steps or sum_steps:
        [(_, for_halo)], _ = advance([(halo_steps or sum_steps, for_halo)])
        if not halo_steps and halo_got is None:
            halo_got = for_halo.astype(F32)
            for_halo = halo_vector(halo_got)
    vector = for_halo
    out_now, gate_now, ahead = [values for _, values in chains]
    sum_x = [ahead[0], last[0, :depth]]
    extra = last[0, depth:].reshape(128, 2 * part)
    sum_back = one_above(extra[:lines], part).astype(F32)
    sum_tail = one_above(extra[lines : lines + lines_tail], part).astype(F32)

    d_normed = d_ext.reshape(2, ext, features)
    sum_gain = lax.dynamic_slice_in_dim(vector, me_fsdp * depth, depth)
    loss = vector[features] / (count * features)
    halo_all = halo_got[:, 0:6].reshape(ctx, 2, 3, features)
    from_next = jnp.stack([halo_all[upper, 0], halo_all[lower, 1]])
    from_next = jnp.where(has_after[:, None, None], from_next, 0.0)
    own_normed = d_normed[:, HALO:] + jnp.pad(from_next, ((0, 0), (piece - 3, 0), (0, 0)))
    own_inv = inv_rms[:, HALO:]
    own_u = rows_ext[:, HALO:]
    scaled = own_normed * gain
    d_rows = own_inv * scaled - own_u * (own_inv * own_inv * own_inv) * jnp.mean(
        scaled * own_u, axis=2, keepdims=True
    )
    grad_tokens = (to_blocks(d_rows.reshape(rows_all, features), depth) + g_out)[None]
    grad_in = jnp.concatenate([*sum_x, gate_now[0]], axis=1).astype(F32)
    return (
        out_low[None],
        loss,
        grad_tokens,
        sum_gain,
        grad_in,
        sum_tail[0:4],
        sum_tail[4],
        sum_tail[8:104].T,
        sum_back[0:rank],
        sum_back[rank + states],
        sum_back[rank : rank + states],
        sum_back[rank + states + 8],
        out_now[0].astype(F32),
    )


def solution(mesh):
    in_specs = (
        P("fsdp", "ctx", None),
        P("fsdp", "ctx", None),
        P("fsdp", None),
        P(),
        P("fsdp"),
        P("fsdp", None),
        P(None, "fsdp"),
        P("fsdp"),
        P("fsdp", None),
        P(None, "fsdp"),
        P("fsdp"),
        P(None, "fsdp"),
        P("fsdp"),
        P("fsdp", None),
    )
    out_specs = (
        P("fsdp", "ctx", None),
        P(),
        P("fsdp", "ctx", None),
        P("fsdp"),
        P("fsdp", None),
        P(None, "fsdp"),
        P("fsdp"),
        P("fsdp", None),
        P(None, "fsdp"),
        P("fsdp"),
        P(None, "fsdp"),
        P("fsdp"),
        P("fsdp", None),
    )
    return jax.shard_map(local, mesh=mesh, in_specs=in_specs, out_specs=out_specs, check_vma=False)
```
